768 devices in a mesh: lon: 192 (over y, x_hi, z), lat: 4 (over x_lo, core).
Axes of the slice: x: 4 (x_hi: 2, x_lo: 2; x = x_hi * 2 + x_lo), y: 8, z: 12, core: 2. Of those that a mesh axis runs over, the one named last changes fastest.
Arguments:
- thermal_anomaly: float32 [8, 3072, 1536], P(None, 'lon', 'lat'), may hold values from -6 to 6
- saltiness_anomaly: float32 [8, 3072, 1536], P(None, 'lon', 'lat'), may hold values from -6 to 6
- eastward_transit_ratio: float32 [8, 3072, 1536], P(None, 'lon', 'lat'), may hold values from -0.45 to 0.45
- poleward_transit_ratio: float32 [8, 3072, 1536], P(None, 'lon', 'lat'), may hold values from -0.45 to 0.45
- elevation_prior: float32 [3072, 1536], P('lon', 'lat'), may hold values from -12 to 12
- ocean_point_flag: int32 [3072, 1536], P('lon', 'lat'), may hold values 0 or 1
- depth_layers: int32 [3072, 1536], P('lon', 'lat'), may hold values from 1 to 8
- fold_counterpart: int32 [3072], P('lon'), may hold values from 0 to 3071, as said below
Outputs:
- temperature_next: float32 [8, 3072, 1536], P(None, 'lon', 'lat')
- salinity_next: float32 [8, 3072, 1536], P(None, 'lon', 'lat')
- surface_next: float32 [3072, 1536], P('lon', 'lat')
- surface_residual: float32 [3072, 1536], P('lon', 'lat')
The draws below stay inside these ranges and needn't reach their ends.
Inputs may be any that keep to these rules, and one draw needn't show every extreme that they name: Partner is a mirror across the fold: fold_counterpart[i] = (s - i) mod 3072 for one s with s + 1 a multiple of 16, so fold_counterpart[fold_counterpart[i]] = i and fold_counterpart[i] != i.
All inputs are finite; a program needn't handle non-finite values. No bound on the sum of `ocean_point_flag` on one device may be relied on, other than what follows from the above.
Results may differ from the reference program's by a relative error of at most 0.00035.
Values sent between devices are 32-bit elements; how exact they have to be, the bound alone decides.
No kernel may reach another device: no remote copies, remote signals or barrier semaphores. Data moves between devices by JAX's collectives and lax.ppermute only.
A program may use at most 64 MiB of HBM per device.

```python
import jax
import jax.numpy as jnp
from jax import lax

DEPTH_LAYERS = 8
CLON = 16
ITERS = 3
MERIDIAN_TOTAL = 3072
PARALLEL_TOTAL = 1536


def draw_elevation_prior(key, part):
    key = jax.random.fold_in(key, 7)
    ramp = 1.0 + 2.0 * jnp.arange(MERIDIAN_TOTAL, dtype=jnp.float32)[:, None] / MERIDIAN_TOTAL
    base = jnp.clip(jax.random.normal(key, (MERIDIAN_TOTAL, PARALLEL_TOTAL), jnp.float32), -4.0, 4.0)
    return (base * ramp).astype(jnp.float32)


def draw_fold_counterpart(key, part):
    key = jax.random.fold_in(key, 11)
    first_key, second_key = jax.random.split(key)
    blocks = MERIDIAN_TOTAL // CLON
    ordering = jax.random.permutation(first_key, jnp.arange(blocks, dtype=jnp.int32))
    pick = jax.random.randint(second_key, (16,), 0, blocks).astype(jnp.int32)
    chosen = jnp.mod(jnp.sum(pick), blocks).astype(jnp.int32)
    offset_block = (jnp.sum(jnp.where(jnp.arange(blocks, dtype=jnp.int32) == chosen, ordering, 0)) + 1).astype(jnp.int32)
    mirror_sum = offset_block * CLON - 1
    longitudes = jnp.arange(MERIDIAN_TOTAL, dtype=jnp.int32)
    return jnp.mod(mirror_sum - longitudes, MERIDIAN_TOTAL).astype(jnp.int32)


def set_ends(result, key, smallest, largest):
    longest = result.shape.index(max(result.shape))
    spots = []
    for shift in (0, 1):
        where = [jax.random.randint(jax.random.fold_in(key, axis), (), 0, length) for axis, length in enumerate(result.shape)]
        where[longest] = (where[longest] + shift) % result.shape[longest]
        spots.append(tuple(where))
    return result.at[spots[0]].set(smallest).at[spots[1]].set(largest)


def steps_of(stream_key, extent, cuts, smallest, largest):
    level, own = 1.0, jax.random.fold_in(stream_key, 6)
    for position, parts in cuts:
        heights = jnp.exp(jax.random.uniform(jax.random.fold_in(own, position), (parts,), jnp.float32, smallest / len(cuts), largest / len(cuts)))
        level = level * jnp.repeat(heights, extent[position] // parts).reshape([-1 if axis == position else 1 for axis in range(len(extent))])
    return level


def bell_draw(rng, dims, spread, limit, cuts=(), kind=jnp.bfloat16):
    values = spread * jax.random.normal(rng, dims, jnp.float32)
    if cuts:
        values = values * steps_of(rng, dims, cuts, -0.22, 0.18)
    return jnp.clip(values, -limit, limit).astype(kind)


def setup_inputs(seed: int = 0) -> dict:
    key_of = jax.random.split(jax.random.key(seed), 9)
    return {
        "thermal_anomaly": bell_draw(key_of[0], (DEPTH_LAYERS, MERIDIAN_TOTAL, PARALLEL_TOTAL), 1.0, 6.0, ((1, 192), (2, 4)), jnp.float32),
        "saltiness_anomaly": bell_draw(key_of[1], (DEPTH_LAYERS, MERIDIAN_TOTAL, PARALLEL_TOTAL), 1.0, 6.0, ((1, 192), (2, 4)), jnp.float32),
        "eastward_transit_ratio": jnp.clip(jax.random.uniform(key_of[2], (DEPTH_LAYERS, MERIDIAN_TOTAL, PARALLEL_TOTAL), jnp.float32, -0.45, 0.45) * steps_of(key_of[2], (DEPTH_LAYERS, MERIDIAN_TOTAL, PARALLEL_TOTAL), ((1, 192), (2, 4)), -0.4, 0.0), -0.45, 0.45),
        "poleward_transit_ratio": jnp.clip(jax.random.uniform(key_of[3], (DEPTH_LAYERS, MERIDIAN_TOTAL, PARALLEL_TOTAL), jnp.float32, -0.45, 0.45) * steps_of(key_of[3], (DEPTH_LAYERS, MERIDIAN_TOTAL, PARALLEL_TOTAL), ((1, 192), (2, 4)), -0.4, 0.0), -0.45, 0.45),
        "elevation_prior": draw_elevation_prior(jax.random.fold_in(key_of[8], 71), 0),
        "ocean_point_flag": set_ends((jax.random.randint(key_of[5], (MERIDIAN_TOTAL, PARALLEL_TOTAL), 0, 5) < 4).astype(jnp.int32), jax.random.fold_in(key_of[5], 1), 0, 1),
        "depth_layers": set_ends(jax.random.randint(key_of[6], (MERIDIAN_TOTAL, PARALLEL_TOTAL), 1, DEPTH_LAYERS + 1), jax.random.fold_in(key_of[6], 1), 1, DEPTH_LAYERS).astype(jnp.int32),
        "fold_counterpart": draw_fold_counterpart(jax.random.fold_in(key_of[8], 71), 0),
    }


def weno_face(far_up, near_up, center, near_down, far_down):
    stencil_low = (2.0 * far_up - 7.0 * near_up + 11.0 * center) / 6.0
    stencil_mid = (-near_up + 5.0 * center + 2.0 * near_down) / 6.0
    stencil_top = (2.0 * center + 5.0 * near_down - far_down) / 6.0
    beta_low = 13.0 / 12.0 * (far_up - 2.0 * near_up + center) ** 2 + 0.25 * (far_up - 4.0 * near_up + 3.0 * center) ** 2
    beta_mid = 13.0 / 12.0 * (near_up - 2.0 * center + near_down) ** 2 + 0.25 * (near_up - near_down) ** 2
    beta_top = 13.0 / 12.0 * (center - 2.0 * near_down + far_down) ** 2 + 0.25 * (3.0 * center - 4.0 * near_down + far_down) ** 2
    weight_low = 0.1 / (1e-06 + beta_low) ** 2
    weight_mid = 0.6 / (1e-06 + beta_mid) ** 2
    weight_top = 0.3 / (1e-06 + beta_top) ** 2
    summed = weight_low * stencil_low + weight_mid * stencil_mid + weight_top * stencil_top
    return summed / (weight_low + weight_mid + weight_top)

def face_flux(padded, speed, count, axis):
    shifted = [lax.slice_in_dim(padded, offset, offset + count + 1, axis=axis) for offset in range(6)]
    upwind_left = weno_face(shifted[0], shifted[1], shifted[2], shifted[3], shifted[4])
    upwind_right = weno_face(shifted[5], shifted[4], shifted[3], shifted[2], shifted[1])
    return jnp.maximum(speed, 0.0) * upwind_left + jnp.minimum(speed, 0.0) * upwind_right

def operate(scalar_quantity, coupler):
    scaled = coupler * scalar_quantity
    east_cells = jnp.roll(scaled, -1, axis=0)
    west_cells = jnp.roll(scaled, 1, axis=0)
    padded = jnp.pad(scaled, ((0, 0), (1, 1)))
    laplace = 4.0 * scaled - east_cells - west_cells - padded[:, 2:] - padded[:, :-2]
    return scalar_quantity + coupler * laplace

def reference(thermal_anomaly, saltiness_anomaly, eastward_transit_ratio, poleward_transit_ratio, elevation_prior, ocean_point_flag, depth_layers, fold_counterpart):
    layer_positions = lax.broadcasted_iota(jnp.int32, thermal_anomaly.shape, 0)
    ocean_indicator = jnp.where((ocean_point_flag[None] == 1) & (layer_positions < depth_layers[None]), 1.0, 0.0).astype(jnp.float32)
    east_speed = eastward_transit_ratio * ocean_indicator
    north_speed = poleward_transit_ratio * ocean_indicator
    east_faces = jnp.concatenate([east_speed[:, -1:], east_speed], axis=1)
    north_faces = jnp.concatenate([jnp.zeros_like(north_speed[:, :, :1]), north_speed], axis=2)
    results = []
    for scalar_quantity in (thermal_anomaly, saltiness_anomaly):
        masked = scalar_quantity * ocean_indicator
        zonal_pad = jnp.concatenate([masked[:, -3:], masked, masked[:, :3]], axis=1)
        fold_rows = jnp.flip(masked[:, :, PARALLEL_TOTAL - 3:], axis=2)[:, fold_counterpart, :]
        merid_pad = jnp.concatenate([jnp.zeros_like(masked[:, :, :3]), masked, fold_rows], axis=2)
        flux_x = face_flux(zonal_pad, east_faces, MERIDIAN_TOTAL, 1)
        flux_y = face_flux(merid_pad, north_faces, PARALLEL_TOTAL, 2)
        updated = masked - (flux_x[:, 1:] - flux_x[:, :-1]) - (flux_y[:, :, 1:] - flux_y[:, :, :-1])
        results.append(updated * ocean_indicator)
    east_mean = lax.optimization_barrier(jnp.sum(east_faces, axis=0)) / DEPTH_LAYERS
    north_mean = lax.optimization_barrier(jnp.sum(north_faces, axis=0)) / DEPTH_LAYERS
    divergence = east_mean[1:] - east_mean[:-1] + north_mean[:, 1:] - north_mean[:, :-1]
    right_side = elevation_prior - divergence
    coupler = 2.0 * jnp.sqrt((depth_layers * ocean_point_flag).astype(jnp.float32) / DEPTH_LAYERS)
    solution = jnp.zeros_like(right_side)
    residual = right_side
    direction = right_side
    norm_now = jnp.sum(residual * residual)
    for iteration in range(ITERS):
        product_field = operate(direction, coupler)
        step_size = norm_now / jnp.sum(direction * product_field)
        solution = solution + step_size * direction
        residual = residual - step_size * product_field
        norm_next = jnp.sum(residual * residual)
        direction = residual + norm_next / norm_now * direction
        norm_now = norm_next
    return (results[0], results[1], solution, residual)
```

```python
import jax
import jax.numpy as jnp
from jax import lax
from jax.sharding import Mesh, PartitionSpec as P

ITERS = 3
LON = ("y", "xh", "z")
LAT = ("xl", "core")
ALL = LON + LAT
SIZES = (8, 2, 12, 2, 2)
NLON = 192
NLAT = 4
SHIFT = 17.0
SCALE = 16.0


def weno_upwind(a, b, c, d, e):
    d0, d1, d2, d3 = b - a, c - b, d - c, e - d
    s0, s1, s2 = d1 - d0, d2 - d1, d3 - d2
    t0 = s0 + 2.0 * d1
    t1 = d1 + d2
    t2 = s2 - 2.0 * d2
    k = 13.0 / 12.0
    e0 = 1e-06 + k * s0 * s0 + 0.25 * t0 * t0
    e1 = 1e-06 + k * s1 * s1 + 0.25 * t1 * t1
    e2 = 1e-06 + k * s2 * s2 + 0.25 * t2 * t2
    w0, w1, w2 = e1 * e2, e0 * e2, e0 * e1
    w0, w1, w2 = 0.1 * w0 * w0, 0.6 * w1 * w1, 0.3 * w2 * w2
    top = w0 * (5.0 * d1 - 2.0 * d0) + w1 * (d1 + 2.0 * d2) + w2 * (4.0 * d2 - d3)
    return c + top / (6.0 * (w0 + w1 + w2))


def face_flux(padded, speed, count, axis):
    q = [lax.slice_in_dim(padded, o, o + count + 1, axis=axis) for o in range(6)]
    pos = speed > 0.0
    a, b, c, d, e = (
        jnp.where(pos, q[i], q[5 - i]) for i in range(5)
    )
    return speed * weno_upwind(a, b, c, d, e)


def sum_over(value, axes, count):
    spread = jnp.broadcast_to(value[None], (count,) + value.shape)
    return jnp.sum(lax.all_to_all(spread, axes, 0, 0), axis=0)


def coefficients(gram):
    def form(p, q):
        total = 0.0
        for i in range(4):
            for j in range(4):
                if p[i] is not None and q[j] is not None:
                    total = total + p[i] * q[j] * gram[min(i, j)][max(i, j)]
        return total

    def add(p, s, q):
        return [
            (p[i] if q[i] is None else (s * q[i] if p[i] is None else p[i] + s * q[i]))
            for i in range(4)
        ]

    def image(p):
        out = [None] * 4

        def put(i, x):
            out[i] = x if out[i] is None else out[i] + x

        for i in range(3):
            if p[i] is None:
                continue
            put(i, SHIFT * p[i])
            if i == 0:
                put(1, SCALE * p[0])
            else:
                put(i + 1, 0.5 * SCALE * p[i])
                put(i - 1, 0.5 * SCALE * p[i])
        return out

    one = jnp.float32(1.0)
    x = [None] * 4
    r = [one, None, None, None]
    p = list(r)
    norm = form(r, r)
    for it in range(ITERS):
        ap = image(p)
        step = norm / form(p, ap)
        x = add(x, step, p)
        r = add(r, -step, ap)
        if it + 1 < ITERS:
            new = form(r, r)
            p = add(r, new / norm, p)
            norm = new
    return x, r


def on_device(t, s, u, v, elev, flag, depth, fc):
    nl, ni, nj = t.shape
    lat = lax.axis_index(LAT)
    lon = lax.axis_index(LON)
    odd = (lat % 2) == 1
    last = lat == NLAT - 1
    level = lax.broadcasted_iota(jnp.int32, t.shape, 0)
    mask = jnp.where((flag[None] == 1) & (level < depth[None]), 1.0, 0.0).astype(jnp.float32)
    q = jnp.stack([t * mask, s * mask])
    ue = u * mask
    vn = v * mask
    em = jnp.sum(ue, axis=0) / nl
    nm = jnp.sum(vn, axis=0) / nl
    coupler = 2.0 * jnp.sqrt((depth * flag).astype(jnp.float32) / nl)
    part = elev - em - nm

    up = jnp.concatenate(
        [q[:, :, ni - 3 :].reshape(6 * nl, nj), ue[:, ni - 1], part[ni - 3 :], em[ni - 4 :], nm[ni - 3 :], coupler[ni - 3 :]]
    )
    down = jnp.concatenate([q[:, :, :3].reshape(6 * nl, nj), part[:3], em[:3], nm[:3], coupler[:3]])
    west = lax.ppermute(up, LON, [(i, (i + 1) % NLON) for i in range(NLON)])
    east = lax.ppermute(down, LON, [((i + 1) % NLON, i) for i in range(NLON)])
    n6 = 6 * nl
    q_west, q_east = west[:n6].reshape(2, nl, 3, nj), east[:n6].reshape(2, nl, 3, nj)
    u_west = west[n6 : n6 + nl]
    cw, ce = west[n6 + nl :], east[n6:]
    zero = jnp.zeros((1, nj), jnp.float32)
    fields = jnp.stack(
        [
            jnp.concatenate([zero, cw[0:3], part, ce[0:3]]),
            jnp.concatenate([cw[3:7], em, ce[3:6]]),
            jnp.concatenate([zero, cw[7:10], nm, ce[6:9]]),
            jnp.concatenate([zero, cw[10:13], coupler, ce[9:12]]),
        ]
    )
    rows = fields.shape[1]

    def edge(qpart, vcol, fpart):
        a = jnp.transpose(qpart, (0, 3, 1, 2)).reshape(6, nl * ni)
        b = vcol.reshape(1, nl * ni)
        c = jnp.pad(jnp.transpose(fpart, (0, 2, 1)).reshape(16, rows), ((0, 0), (0, nl * ni - rows)))
        return jnp.concatenate([a, b, c])

    to_north = edge(q[..., nj - 3 :], vn[..., nj - 1], fields[..., nj - 4 :])
    to_south = edge(q[..., :3], vn[..., 0], fields[..., :4])
    fold_edge = jnp.transpose(jnp.flip(q[..., nj - 3 :], axis=(2, 3)), (0, 3, 1, 2)).reshape(6, nl * ni)
    fold = jnp.concatenate([fold_edge, to_north[6:]])
    send_a = jnp.where(odd, to_south, to_north)
    send_b = jnp.where(lat == 1, to_north, jnp.where(lat == 2, to_south, fold))
    got_a = lax.ppermute(send_a, LAT, [(0, 1), (1, 0), (2, 3), (3, 2)])
    turn = jnp.mod(fc[0] // ni + lon, NLON)

    def branch(k):
        pairs = []
        for i in range(NLON):
            pairs += [(4 * i + 1, 4 * i + 2), (4 * i + 2, 4 * i + 1), (4 * i + 3, 4 * ((k - i) % NLON) + 3)]
        return lambda value: lax.ppermute(value, ALL, pairs)

    got_b = lax.switch(turn, [branch(k) for k in range(NLON)], send_b)
    north = jnp.where(odd, got_b, got_a)
    south = jnp.where(odd, got_a, got_b)

    def columns(msg):
        return jnp.transpose(msg[:6].reshape(2, 3, nl, ni), (0, 2, 3, 1))

    q_north, q_south = columns(north), columns(south)
    v_south = south[6].reshape(nl, ni, 1)
    keep = jnp.where(last, 0.0, 1.0)

    def fcols(msg):
        return jnp.transpose(msg[7:23, :rows].reshape(4, 4, rows), (0, 2, 1))

    full = jnp.concatenate([fcols(south), fields, fcols(north) * keep], axis=2)
    rhs = full[0, 1:, 1:] + full[1, :-1, 1:] + full[2, 1:, :-1]
    cpl = full[3, 1:, 1:]

    def operate(e):
        f = jnp.pad(cpl * e, ((1, 1), (1, 1)))
        lap = 4.0 * f[1:-1, 1:-1] - f[2:, 1:-1] - f[:-2, 1:-1] - f[1:-1, 2:] - f[1:-1, :-2]
        return e + cpl * lap

    def scaled(e):
        return (operate(e) - SHIFT * e) * (1.0 / SCALE)

    b0 = rhs
    b1 = scaled(b0)
    b2 = 2.0 * scaled(b1) - b0
    b3 = 2.0 * scaled(b2) - b1
    basis = [x[3 : 3 + ni, 3 : 3 + nj] for x in (b0, b1, b2, b3)]
    sums = jnp.stack([jnp.sum(basis[i] * basis[j]) for i in range(4) for j in range(i, 4)])
    sums = jnp.pad(sums, (0, 118)).reshape(1, 128)
    sums = sum_over(sums, "z", 12)
    sums = sum_over(sums, ("y", "xh") + LAT, 64)
    gram = [[None] * 4 for _ in range(4)]
    at = 0
    for i in range(4):
        for j in range(i, 4):
            gram[i][j] = sums[0, at]
            at += 1
    xc, rc = coefficients(gram)
    surface = sum(c * f for c, f in zip(xc, basis) if c is not None)
    residual = sum(c * f for c, f in zip(rc, basis) if c is not None)

    zonal = jnp.concatenate([q_west, q, q_east], axis=2)
    merid = jnp.concatenate([q_south, q, q_north], axis=3)
    speed_x = jnp.concatenate([u_west[:, None], ue], axis=1)
    speed_y = jnp.concatenate([v_south, vn], axis=2)
    flux_x = face_flux(zonal, speed_x[None], ni, 2)
    flux_y = face_flux(merid, speed_y[None], nj, 3)
    updated = q - (flux_x[:, :, 1:] - flux_x[:, :, :-1]) - (flux_y[..., 1:] - flux_y[..., :-1])
    updated = updated * mask
    return updated[0], updated[1], surface, residual


def solution(mesh):
    fine = Mesh(mesh.devices.reshape(SIZES), ALL)
    block, plane = P(None, LON, LAT), P(LON, LAT)
    return jax.shard_map(
        on_device,
        mesh=fine,
        in_specs=(block,) * 4 + (plane,) * 3 + (P(LON),),
        out_specs=(block, block, plane, plane),
        check_vma=False,
    )
```

```python
import jax
import jax.numpy as jnp
from jax import lax
from jax.experimental import pallas as pl
from jax.experimental.pallas import tpu as pltpu
from jax.sharding import Mesh, PartitionSpec as P

ITERS = 3
LON = ("y", "xh", "z")
LAT = ("xl", "core")
ALL = LON + LAT
SIZES = (8, 2, 12, 2, 2)
SHIFT = 17.0
SCALE = 16.0
PAIRS = [(i, j) for i in range(4) for j in range(i, 4)]


def weno_upwind(a, b, c, d, e):
    d0, d1, d2, d3 = b - a, c - b, d - c, e - d
    s0, s1, s2 = d1 - d0, d2 - d1, d3 - d2
    t0 = s0 + 2.0 * d1
    t1 = d1 + d2
    t2 = s2 - 2.0 * d2
    k = 13.0 / 12.0
    e0 = 1e-06 + k * s0 * s0 + 0.25 * t0 * t0
    e1 = 1e-06 + k * s1 * s1 + 0.25 * t1 * t1
    e2 = 1e-06 + k * s2 * s2 + 0.25 * t2 * t2
    w0, w1, w2 = e1 * e2, e0 * e2, e0 * e1
    w0, w1, w2 = 0.1 * w0 * w0, 0.6 * w1 * w1, 0.3 * w2 * w2
    top = w0 * (5.0 * d1 - 2.0 * d0) + w1 * (d1 + 2.0 * d2) + w2 * (4.0 * d2 - d3)
    return c + top / (6.0 * (w0 + w1 + w2))


def face_flux(padded, speed, count, axis):
    q = [lax.slice_in_dim(padded, o, o + count, axis=axis) for o in range(6)]
    pos = speed > 0.0
    a, b, c, d, e = (jnp.where(pos, q[i], q[5 - i]) for i in range(5))
    return speed * weno_upwind(a, b, c, d, e)


def spread_to(value, axes, count):
    return lax.all_to_all(jnp.broadcast_to(value[None], (count,) + value.shape), axes, 0, 0)


def coefficients(gram):
    def form(p, q):
        total = 0.0
        for i in range(4):
            for j in range(4):
                if p[i] is not None and q[j] is not None:
                    total = total + p[i] * q[j] * gram[min(i, j), max(i, j)]
        return total

    def add(p, s, q):
        return [
            (p[i] if q[i] is None else (s * q[i] if p[i] is None else p[i] + s * q[i]))
            for i in range(4)
        ]

    def image(p):
        out = [None] * 4

        def put(i, x):
            out[i] = x if out[i] is None else out[i] + x

        for i in range(3):
            if p[i] is None:
                continue
            put(i, SHIFT * p[i])
            if i == 0:
                put(1, SCALE * p[0])
            else:
                put(i + 1, 0.5 * SCALE * p[i])
                put(i - 1, 0.5 * SCALE * p[i])
        return out

    x = [None] * 4
    r = [jnp.ones_like(gram[0, 0]), None, None, None]
    p = list(r)
    norm = form(r, r)
    for it in range(ITERS):
        ap = image(p)
        step = norm / form(p, ap)
        x = add(x, step, p)
        r = add(r, -step, ap)
        if it + 1 < ITERS:
            new = form(r, r)
            p = add(r, new / norm, p)
            norm = new
    return x, r


def krylov_kernel(full_ref, basis_ref, sums_ref):
    ni, nj = basis_ref.shape[1:]
    part, em, nm, cpl = (full_ref[k] for k in range(4))
    rows, lanes = part.shape
    b0 = part + pltpu.roll(em, 1, 0) + pltpu.roll(nm, 1, 1)

    def scaled(e):
        f = cpl * e
        lap = (
            4.0 * f
            - pltpu.roll(f, 1, 0)
            - pltpu.roll(f, rows - 1, 0)
            - pltpu.roll(f, 1, 1)
            - pltpu.roll(f, lanes - 1, 1)
        )
        return ((1.0 - SHIFT) * e + cpl * lap) * (1.0 / SCALE)

    b1 = scaled(b0)
    b2 = 2.0 * scaled(b1) - b0
    b3 = 2.0 * scaled(b2) - b1
    basis = [b[8 : 8 + ni, :nj] for b in (b0, b1, b2, b3)]
    for k in range(4):
        basis_ref[k] = basis[k]
    row = lax.broadcasted_iota(jnp.int32, (8, 128), 0)
    col = lax.broadcasted_iota(jnp.int32, (8, 128), 1)
    total = jnp.zeros((8, 128), jnp.float32)
    for n, (i, j) in enumerate(PAIRS):
        prod = basis[i] * basis[j]
        prod = prod[:8] + prod[8:]
        acc = prod[:, :128]
        for k in range(1, nj // 128):
            acc = acc + prod[:, 128 * k : 128 * (k + 1)]
        one = jnp.sum(jnp.sum(acc, axis=0, keepdims=True), axis=1, keepdims=True)
        total = total + jnp.where((row == 6) & (col == n), one, 0.0)
    sums_ref[...] = total


def finish_kernel(basis_ref, sums_ref, surface_ref, residual_ref):
    total = sums_ref[0]
    for k in range(1, sums_ref.shape[0]):
        total = total + sums_ref[k]
    row = lax.broadcasted_iota(jnp.int32, (8, 128), 0)
    col = lax.broadcasted_iota(jnp.int32, (8, 128), 1)
    gram = {}
    for n, pair in enumerate(PAIRS):
        cell = jnp.where((row == 6) & (col == n), total, 0.0)
        gram[pair] = jnp.sum(jnp.sum(cell, axis=0, keepdims=True), axis=1, keepdims=True)
    xc, rc = coefficients(gram)
    basis = [basis_ref[k] for k in range(4)]
    surface_ref[...] = sum(c * f for c, f in zip(xc, basis) if c is not None)
    residual_ref[...] = sum(c * f for c, f in zip(rc, basis) if c is not None)


def make_on_device(sizes):
    ny, nxh, nz, nxl, ncore = sizes
    n_lon, n_lat = ny * nxh * nz, nxl * ncore

    def on_device(t, s, u, v, elev, flag, depth, fc):
        nl, ni, nj = t.shape
        lat = lax.axis_index(LAT)
        lon = lax.axis_index(LON)
        last = lat == n_lat - 1
        level = lax.broadcasted_iota(jnp.int32, t.shape, 0)
        mask = jnp.where((flag[None] == 1) & (level < depth[None]), 1.0, 0.0).astype(jnp.float32)
        q = jnp.stack([t * mask, s * mask])
        ue = u * mask
        vn = v * mask
        em = jnp.sum(ue, axis=0) / nl
        nm = jnp.sum(vn, axis=0) / nl
        coupler = 2.0 * jnp.sqrt((depth * flag).astype(jnp.float32) / nl)
        part = elev - em - nm

        up = jnp.concatenate(
            [
                q[:, :, ni - 3 :].reshape(6 * nl, nj),
                ue[:, ni - 1],
                part[ni - 3 :],
                em[ni - 4 :],
                nm[ni - 3 :],
                coupler[ni - 3 :],
            ]
        )
        down = jnp.concatenate(
            [q[:, :, :3].reshape(6 * nl, nj), part[:3], em[:3], nm[:3], coupler[:3]]
        )
        west = lax.ppermute(up, LON, [(i, (i + 1) % n_lon) for i in range(n_lon)])
        east = lax.ppermute(down, LON, [((i + 1) % n_lon, i) for i in range(n_lon)])
        n6 = 6 * nl
        q_west, q_east = west[:n6].reshape(2, nl, 3, nj), east[:n6].reshape(2, nl, 3, nj)
        u_west = west[n6 : n6 + nl]
        cw, ce = west[n6 + nl :], east[n6:]

        def blank(n):
            return jnp.zeros((n, nj), jnp.float32)

        fields = jnp.stack(
            [
                jnp.concatenate([blank(5), cw[0:3], part, ce[0:3], blank(5)]),
                jnp.concatenate([blank(4), cw[3:7], em, ce[3:6], blank(5)]),
                jnp.concatenate([blank(5), cw[7:10], nm, ce[6:9], blank(5)]),
                jnp.concatenate([blank(5), cw[10:13], coupler, ce[9:12], blank(5)]),
            ]
        )

        rows = fields.shape[1]

        def edge(qpart, vcol, fpart):
            a = jnp.transpose(qpart, (0, 3, 1, 2)).reshape(6, nl * ni)
            b = vcol.reshape(1, nl * ni)
            c = jnp.transpose(fpart, (2, 0, 1)).reshape(4, 4 * rows)
            return jnp.concatenate([a, b, jnp.zeros_like(b), c, jnp.zeros_like(c)])

        to_north = edge(q[..., nj - 3 :], vn[..., nj - 1], fields[..., nj - 4 :])
        to_south = edge(q[..., :3], vn[..., 0], fields[..., :4])
        slot = lax.broadcasted_iota(jnp.int32, (n_lat, 1, 1), 0)
        got = lax.all_to_all(
            jnp.where(slot > lat, to_north[None], to_south[None]), LAT, 0, 0
        )
        north = jnp.where(
            last, 0.0, lax.dynamic_index_in_dim(got, jnp.minimum(lat + 1, n_lat - 1), 0, False)
        )
        south = jnp.where(
            lat == 0, 0.0, lax.dynamic_index_in_dim(got, jnp.maximum(lat - 1, 0), 0, False)
        )

        def columns(msg):
            return jnp.transpose(msg[:6].reshape(2, 3, nl, ni), (0, 2, 3, 1))

        q_north, q_south = columns(north), columns(south)
        v_south = south[6].reshape(nl, ni, 1)

        def fcols(msg):
            return jnp.transpose(msg[8:12].reshape(4, 4, rows), (1, 2, 0))

        full = jnp.concatenate(
            [fields, fcols(north), jnp.zeros((4, rows, 120), jnp.float32), fcols(south)], axis=2
        )
        basis, sums = pl.pallas_call(
            krylov_kernel,
            out_shape=(
                jax.ShapeDtypeStruct((4, ni, nj), jnp.float32),
                jax.ShapeDtypeStruct((8, 128), jnp.float32),
            ),
            name="krylov",
        )(full)

        fold = jnp.transpose(jnp.flip(q[..., nj - 3 :], axis=(2, 3)), (0, 3, 1, 2)).reshape(6, nl * ni)
        source = jnp.mod(fc[0] // ni, n_lon)
        sums = jnp.sum(spread_to(sums[6:7], LAT, n_lat), axis=0)
        tail = jnp.zeros((1, 128), jnp.float32)
        got = spread_to(jnp.concatenate([fold, sums, tail]), "z", nz)
        fold = lax.dynamic_index_in_dim(got, source % nz, 0, False)[:6]
        sums = jnp.sum(got[:, 6:7], axis=0)
        got = spread_to(jnp.concatenate([fold, sums, tail]), ("y", "xh"), ny * nxh)
        fold = lax.dynamic_index_in_dim(got, source // nz, 0, False)[:6].reshape(2, 3, nl * ni)
        surface, residual = pl.pallas_call(
            finish_kernel,
            out_shape=(jax.ShapeDtypeStruct((ni, nj), jnp.float32),) * 2,
            name="finish",
        )(basis, got)

        zonal = jnp.concatenate([q_west, q, q_east], axis=2)
        merid = jnp.concatenate([q_south, q, q_north], axis=3)
        speed_x = jnp.concatenate([u_west[:, None], ue], axis=1)
        place = lax.broadcasted_iota(jnp.int32, (1, 1, nj + 1), 2)
        speed_y = jnp.concatenate([v_south, vn], axis=2)
        speed_y = jnp.where(last & (place > nj - 3), 0.0, speed_y)
        flux_x = face_flux(zonal, speed_x[None], ni + 1, 2)
        flux_y = face_flux(merid, speed_y[None], nj + 1, 3)
        updated = q - (flux_x[:, :, 1:] - flux_x[:, :, :-1]) - (flux_y[..., 1:] - flux_y[..., :-1])
        own = jnp.transpose(q[..., nj - 5 :], (0, 3, 1, 2)).reshape(2, 5, nl * ni)
        speed = jnp.transpose(vn[..., nj - 3 :], (2, 0, 1)).reshape(1, 3, nl * ni)
        beyond = face_flux(jnp.concatenate([own, fold], axis=1), jnp.where(last, speed, 0.0), 3, 1)
        change = jnp.concatenate([beyond[:, :1], beyond[:, 1:] - beyond[:, :-1]], axis=1)
        change = jnp.transpose(change.reshape(2, 3, nl, ni), (0, 2, 3, 1))
        updated = (updated - jnp.pad(change, ((0, 0), (0, 0), (0, 0), (nj - 3, 0)))) * mask
        return updated[0], updated[1], surface, residual

    return on_device


def solution(mesh, sizes=SIZES):
    fine = Mesh(mesh.devices.reshape(sizes), ALL)
    block, plane = P(None, LON, LAT), P(LON, LAT)
    return jax.shard_map(
        make_on_device(sizes),
        mesh=fine,
        in_specs=(block,) * 4 + (plane,) * 3 + (P(LON),),
        out_specs=(block, block, plane, plane),
        check_vma=False,
    )
```

```python
import jax
import jax.numpy as jnp
from jax import lax
from jax.experimental import pallas as pl
from jax.experimental.pallas import tpu as pltpu
from jax.sharding import Mesh, PartitionSpec as P

ITERS = 3
LON = ("y", "xh", "z")
LAT = ("xl", "core")
ALL = LON + LAT
SIZES = (8, 2, 12, 2, 2)
SHIFT = 17.0
SCALE = 16.0
PAIRS = [(i, j) for i in range(4) for j in range(i, 4)]


def weno_upwind(a, b, c, d, e):
    d0, d1, d2, d3 = b - a, c - b, d - c, e - d
    s0, s1, s2 = d1 - d0, d2 - d1, d3 - d2
    t0 = s0 + 2.0 * d1
    t1 = d1 + d2
    t2 = s2 - 2.0 * d2
    k = 13.0 / 12.0
    e0 = 1e-06 + k * s0 * s0 + 0.25 * t0 * t0
    e1 = 1e-06 + k * s1 * s1 + 0.25 * t1 * t1
    e2 = 1e-06 + k * s2 * s2 + 0.25 * t2 * t2
    w0, w1, w2 = e1 * e2, e0 * e2, e0 * e1
    w0, w1, w2 = 0.1 * w0 * w0, 0.6 * w1 * w1, 0.3 * w2 * w2
    top = w0 * (5.0 * d1 - 2.0 * d0) + w1 * (d1 + 2.0 * d2) + w2 * (4.0 * d2 - d3)
    return c + top / (6.0 * (w0 + w1 + w2))


def face_flux(padded, speed, count, axis):
    q = [lax.slice_in_dim(padded, o, o + count, axis=axis) for o in range(6)]
    pos = speed > 0.0
    a, b, c, d, e = (jnp.where(pos, q[i], q[5 - i]) for i in range(5))
    return speed * weno_upwind(a, b, c, d, e)


def coefficients(gram):
    def form(p, q):
        total = 0.0
        for i in range(4):
            for j in range(4):
                if p[i] is not None and q[j] is not None:
                    total = total + p[i] * q[j] * gram[min(i, j), max(i, j)]
        return total

    def add(p, s, q):
        return [
            (p[i] if q[i] is None else (s * q[i] if p[i] is None else p[i] + s * q[i]))
            for i in range(4)
        ]

    def image(p):
        out = [None] * 4

        def put(i, x):
            out[i] = x if out[i] is None else out[i] + x

        for i in range(3):
            if p[i] is None:
                continue
            put(i, SHIFT * p[i])
            if i == 0:
                put(1, SCALE * p[0])
            else:
                put(i + 1, 0.5 * SCALE * p[i])
                put(i - 1, 0.5 * SCALE * p[i])
        return out

    x = [None] * 4
    r = [jnp.ones_like(gram[0, 0]), None, None, None]
    p = list(r)
    norm = form(r, r)
    for it in range(ITERS):
        ap = image(p)
        step = norm / form(p, ap)
        x = add(x, step, p)
        r = add(r, -step, ap)
        if it + 1 < ITERS:
            new = form(r, r)
            p = add(r, new / norm, p)
            norm = new
    return x, r


def lat_index():
    return 2 * lax.axis_index("xl") + lax.axis_index("core")


def mirror16(x):
    lane = lax.broadcasted_iota(jnp.int32, x.shape, 1)
    for bit in (1, 2, 4, 8):
        x = jnp.where((lane & bit) != 0, pltpu.roll(x, bit, 1), pltpu.roll(x, 128 - bit, 1))
    return x


def pack_kernel(t, s, u, v, elev, flag, depth, fc, up, down, fields, edges, source, tile):
    nl, ni, nj = t.shape
    ocean = flag[...] == 1
    wet = depth[...]
    lane = lax.broadcasted_iota(jnp.int32, (ni, 128), 1)
    em = jnp.zeros((ni, nj), jnp.float32)
    nm = jnp.zeros((ni, nj), jnp.float32)
    zero = jnp.zeros((8, nj), jnp.float32)
    for l in range(nl):
        m = jnp.where(ocean & (wet > l), 1.0, 0.0)
        tt, ss, uu, vv = t[l] * m, s[l] * m, u[l] * m, v[l] * m
        em = em + uu
        nm = nm + vv
        up[8 * l : 8 * l + 3] = tt[ni - 3 :]
        up[8 * l + 3 : 8 * l + 6] = ss[ni - 3 :]
        up[8 * l + 6 : 8 * l + 7] = uu[ni - 1 :]
        up[8 * l + 7 : 8 * l + 8] = zero[:1]
        down[8 * l : 8 * l + 3] = tt[:3]
        down[8 * l + 3 : 8 * l + 6] = ss[:3]
        down[8 * l + 6 : 8 * l + 8] = zero[:2]
        x = jnp.where(lane < 8, tt[:, :128], tt[:, nj - 128 :])
        x = jnp.where((lane >= 8) & (lane < 16), pltpu.roll(ss[:, :128], 8, 1), x)
        x = jnp.where((lane >= 112) & (lane < 120), pltpu.roll(ss[:, nj - 128 :], 120, 1), x)
        x = jnp.where((lane >= 104) & (lane < 112), pltpu.roll(vv[:, nj - 128 :], 112, 1), x)
        tile[ni * l : ni * (l + 1)] = x
    em = em / nl
    nm = nm / nl
    part = elev[...] - em - nm
    coupler = 2.0 * jnp.sqrt((wet * flag[...]).astype(jnp.float32) / nl)
    for k, f in enumerate((part, em, nm, coupler)):
        fields[k] = f
    up[64:67] = part[ni - 3 :]
    up[67:71] = em[ni - 4 :]
    up[71:74] = nm[ni - 3 :]
    up[74:77] = coupler[ni - 3 :]
    up[77:80] = zero[:3]
    down[64:67] = part[:3]
    down[67:70] = em[:3]
    down[70:73] = nm[:3]
    down[73:76] = coupler[:3]
    down[76:80] = zero[:4]
    turned = tile[...].T
    edges[0:16] = turned[0:16]
    edges[16:40] = turned[104:128]
    block = lax.shift_right_logical(jnp.broadcast_to(fc[0:1, 0:1], (8, 128)), 4)
    row = jnp.zeros((8, 128), jnp.int32)
    nz = lax.axis_size("z")
    for k in range(1, lax.axis_size("y") * lax.axis_size("xh")):
        row = row + jnp.where(block >= nz * k, 1, 0)
    source[0] = block - nz * row
    source[1] = row


def widen_kernel(west, east, fields, edges, wide, slots):
    _, ni, nj = fields.shape
    lat = lat_index()
    blank = jnp.zeros((8, nj), jnp.float32)
    spans = ((64, 67, 64, 67), (67, 71, 67, 70), (71, 74, 70, 73), (74, 77, 73, 76))
    for k, (w0, w1, e0, e1) in enumerate(spans):
        wide[k, 0:8] = blank
        wide[k, 24:32] = blank
        wide[k, 8 - (w1 - w0) : 8] = west[w0:w1]
        wide[k, 8 : 8 + ni] = fields[k]
        wide[k, 24 : 24 + (e1 - e0)] = east[e0:e1]
    lane = lax.broadcasted_iota(jnp.int32, (4, 32, 128), 2)
    both = jnp.where(lane < 64, wide[:, :, 0:128], wide[:, :, nj - 128 : nj])
    turned = both.reshape(128, 128).T
    none = jnp.zeros((4, 128), jnp.float32)
    fold = jnp.concatenate(
        [edges[k : k + 1] for k in (39, 38, 37, 31, 30, 29)] + [none[:2]], axis=0
    )
    fold = mirror16(fold)
    north = jnp.concatenate(
        [edges[37:40], edges[29:32], edges[23:24], none[:1]], axis=0
    )
    south = jnp.concatenate([edges[0:3], edges[8:11], none[:2]], axis=0)
    for p in range(4):
        ahead = p > lat
        slots[p, 0:8] = jnp.where(ahead, north, south)
        slots[p, 8:12] = jnp.where(ahead, turned[124:128], turned[0:4])
        slots[p, 12:14] = fold[2 * p : 2 * p + 2]
        slots[p, 14:16] = none[:2]


def krylov_kernel(wide, got, basis_ref, message, tile):
    ni, nj = basis_ref.shape[1:]
    lat = lat_index()
    tile[...] = jnp.zeros((128, 128), jnp.float32)
    tile[0:4] = jnp.where(lat < 3, got[jnp.minimum(lat + 1, 3), 8:12], 0.0)
    tile[124:128] = jnp.where(lat > 0, got[jnp.maximum(lat - 1, 0), 8:12], 0.0)
    beyond = tile[...].T.reshape(4, 32, 128)
    part, em, nm, cpl = (jnp.concatenate([wide[k], beyond[k]], axis=1) for k in range(4))
    rows, lanes = part.shape
    b0 = part + pltpu.roll(em, 1, 0) + pltpu.roll(nm, 1, 1)

    def scaled(e):
        f = cpl * e
        lap = (
            4.0 * f
            - pltpu.roll(f, 1, 0)
            - pltpu.roll(f, rows - 1, 0)
            - pltpu.roll(f, 1, 1)
            - pltpu.roll(f, lanes - 1, 1)
        )
        return ((1.0 - SHIFT) * e + cpl * lap) * (1.0 / SCALE)

    b1 = scaled(b0)
    b2 = 2.0 * scaled(b1) - b0
    b3 = 2.0 * scaled(b2) - b1
    basis = [b[8 : 8 + ni, :nj] for b in (b0, b1, b2, b3)]
    for k in range(4):
        basis_ref[k] = basis[k]
    row = lax.broadcasted_iota(jnp.int32, (4, 128), 0)
    col = lax.broadcasted_iota(jnp.int32, (4, 128), 1)
    total = jnp.concatenate([got[3, 12:14], jnp.zeros((2, 128), jnp.float32)], axis=0)
    for n, (i, j) in enumerate(PAIRS):
        prod = basis[i] * basis[j]
        prod = prod[:8] + prod[8:]
        acc = prod[:, :128]
        for k in range(1, nj // 128):
            acc = acc + prod[:, 128 * k : 128 * (k + 1)]
        one = jnp.sum(jnp.sum(acc, axis=0, keepdims=True), axis=1, keepdims=True)
        total = jnp.where((row == 2) & (col == n), one, total)
    for k in range(message.shape[0]):
        message[k] = total


def relay_kernel(source, got, message):
    peers = got.shape[0]
    total = got[0]
    for k in range(1, peers):
        total = total + got[k]
    which = source[0, 0:2]
    pieces = []
    for p in range(3):
        piece = got[p, 0:2]
        for z in range(1, peers // 4):
            piece = jnp.where(which == z, got[4 * z + p, 0:2], piece)
        pieces.append(piece)
    text = jnp.concatenate(pieces + [total[2:4]], axis=0)
    for k in range(message.shape[0]):
        message[k] = text


def finish_kernel(basis_ref, source, got, surface_ref, residual_ref, fold_ref):
    total = got[0]
    fold = got[0]
    which = source[1]
    for k in range(1, got.shape[0]):
        total = total + got[k]
        fold = jnp.where(which == k, got[k], fold)
    fold_ref[...] = fold
    row = lax.broadcasted_iota(jnp.int32, (8, 128), 0)
    col = lax.broadcasted_iota(jnp.int32, (8, 128), 1)
    gram = {}
    for n, pair in enumerate(PAIRS):
        cell = jnp.where((row == 6) & (col == n), total, 0.0)
        gram[pair] = jnp.sum(jnp.sum(cell, axis=0, keepdims=True), axis=1, keepdims=True)
    xc, rc = coefficients(gram)
    basis = [basis_ref[k] for k in range(4)]
    surface_ref[...] = sum(c * f for c, f in zip(xc, basis) if c is not None)
    residual_ref[...] = sum(c * f for c, f in zip(rc, basis) if c is not None)


def f32(*shape):
    return jax.ShapeDtypeStruct(shape, jnp.float32)


def vmem(*shape):
    return pltpu.VMEM(shape, jnp.float32)


def make_on_device(sizes):
    ny, nxh, nz, nxl, ncore = sizes
    n_lon, n_lat = ny * nxh * nz, nxl * ncore

    def on_device(t, s, u, v, elev, flag, depth, fc):
        nl, ni, nj = t.shape
        lat = lax.axis_index(LAT)
        last = lat == n_lat - 1

        up, down, fields, edges, source = pl.pallas_call(
            pack_kernel,
            out_shape=(
                vmem(80, nj),
                vmem(80, nj),
                vmem(4, ni, nj),
                vmem(40, 128),
                pltpu.VMEM((2, 8, 128), jnp.int32),
            ),
            scratch_shapes=[vmem(128, 128)],
            name="pack",
        )(t, s, u, v, elev, flag, depth, fc.reshape(1, ni))
        west = lax.ppermute(up, LON, [(i, (i + 1) % n_lon) for i in range(n_lon)])
        east = lax.ppermute(down, LON, [((i + 1) % n_lon, i) for i in range(n_lon)])
        wide, slots = pl.pallas_call(
            widen_kernel,
            out_shape=(vmem(4, 32, nj), vmem(4, 16, 128)),
            name="widen",
        )(west, east, fields, edges)
        halo = lax.all_to_all(slots, LAT, 0, 0)
        basis, message = pl.pallas_call(
            krylov_kernel,
            out_shape=(vmem(4, ni, nj), vmem(nz * n_lat, 4, 128)),
            scratch_shapes=[vmem(128, 128)],
            name="krylov",
        )(wide, halo)
        got = lax.all_to_all(message, ("z",) + LAT, 0, 0)
        message = pl.pallas_call(
            relay_kernel, out_shape=vmem(ny * nxh, 8, 128), name="relay"
        )(source, got)
        got = lax.all_to_all(message, ("y", "xh"), 0, 0)
        surface, residual, fold = pl.pallas_call(
            finish_kernel, out_shape=(f32(ni, nj), f32(ni, nj), vmem(8, 128)), name="finish"
        )(basis, source, got)

        level = lax.broadcasted_iota(jnp.int32, t.shape, 0)
        mask = jnp.where((flag[None] == 1) & (level < depth[None]), 1.0, 0.0).astype(jnp.float32)
        q = jnp.stack([t * mask, s * mask])
        ue = u * mask
        vn = v * mask

        def sides(msg):
            tiles = msg[: 8 * nl].reshape(nl, 8, nj)
            return jnp.stack([tiles[:, 0:3], tiles[:, 3:6]]), tiles[:, 6:7]

        q_west, u_west = sides(west)
        q_east, _ = sides(east)
        north = jnp.where(
            last, 0.0, lax.dynamic_index_in_dim(halo, jnp.minimum(lat + 1, n_lat - 1), 0, False)
        )
        south = jnp.where(
            lat == 0, 0.0, lax.dynamic_index_in_dim(halo, jnp.maximum(lat - 1, 0), 0, False)
        )

        def columns(msg):
            return jnp.transpose(msg[:6].reshape(2, 3, nl, ni), (0, 2, 3, 1))

        q_north, q_south = columns(north), columns(south)
        v_south = south[6].reshape(nl, ni, 1)
        zonal = jnp.concatenate([q_west, q, q_east], axis=2)
        merid = jnp.concatenate([q_south, q, q_north], axis=3)
        speed_x = jnp.concatenate([u_west, ue], axis=1)
        place = lax.broadcasted_iota(jnp.int32, (1, 1, nj + 1), 2)
        speed_y = jnp.concatenate([v_south, vn], axis=2)
        speed_y = jnp.where(last & (place > nj - 3), 0.0, speed_y)
        flux_x = face_flux(zonal, speed_x[None], ni + 1, 2)
        flux_y = face_flux(merid, speed_y[None], nj + 1, 3)
        updated = q - (flux_x[:, :, 1:] - flux_x[:, :, :-1]) - (flux_y[..., 1:] - flux_y[..., :-1])
        own = jnp.stack([edges[35:40], edges[27:32]])
        speed = edges[None, 21:24]
        beyond = face_flux(
            jnp.concatenate([own, fold[:6].reshape(2, 3, 128)], axis=1),
            jnp.where(last, speed, 0.0),
            3,
            1,
        )
        change = jnp.concatenate([beyond[:, :1], beyond[:, 1:] - beyond[:, :-1]], axis=1)
        change = jnp.transpose(change.reshape(2, 3, nl, ni), (0, 2, 3, 1))
        updated = (updated - jnp.pad(change, ((0, 0), (0, 0), (0, 0), (nj - 3, 0)))) * mask
        return updated[0], updated[1], surface, residual

    return on_device


def solution(mesh, sizes=SIZES):
    fine = Mesh(mesh.devices.reshape(sizes), ALL)
    block, plane = P(None, LON, LAT), P(LON, LAT)
    return jax.shard_map(
        make_on_device(sizes),
        mesh=fine,
        in_specs=(block,) * 4 + (plane,) * 3 + (P(LON),),
        out_specs=(block, block, plane, plane),
        check_vma=False,
    )
```

```python
import jax
import jax.numpy as jnp
from jax import lax
from jax.experimental import pallas as pl
from jax.experimental.pallas import tpu as pltpu
from jax.sharding import Mesh, PartitionSpec as P

ITERS = 3
LON = ("y", "xh", "z")
LAT = ("xl", "core")
ALL = LON + LAT
SIZES = (8, 2, 12, 2, 2)
SHIFT = 17.0
SCALE = 16.0
PAIRS = [(i, j) for i in range(4) for j in range(i, 4)]


def weno_upwind(a, b, c, d, e):
    d0, d1, d2, d3 = b - a, c - b, d - c, e - d
    s0, s1, s2 = d1 - d0, d2 - d1, d3 - d2
    t0 = s0 + 2.0 * d1
    t1 = d1 + d2
    t2 = s2 - 2.0 * d2
    k = 13.0 / 12.0
    e0 = 1e-06 + k * s0 * s0 + 0.25 * t0 * t0
    e1 = 1e-06 + k * s1 * s1 + 0.25 * t1 * t1
    e2 = 1e-06 + k * s2 * s2 + 0.25 * t2 * t2
    w0, w1, w2 = e1 * e2, e0 * e2, e0 * e1
    w0, w1, w2 = 0.1 * w0 * w0, 0.6 * w1 * w1, 0.3 * w2 * w2
    top = w0 * (5.0 * d1 - 2.0 * d0) + w1 * (d1 + 2.0 * d2) + w2 * (4.0 * d2 - d3)
    return c + top / (6.0 * (w0 + w1 + w2))


def face_flux(padded, speed, count, axis):
    q = [lax.slice_in_dim(padded, o, o + count, axis=axis) for o in range(6)]
    pos = speed > 0.0
    a, b, c, d, e = (jnp.where(pos, q[i], q[5 - i]) for i in range(5))
    return speed * weno_upwind(a, b, c, d, e)


def coefficients(gram):
    def form(p, q):
        total = 0.0
        for i in range(4):
            for j in range(4):
                if p[i] is not None and q[j] is not None:
                    total = total + p[i] * q[j] * gram[min(i, j), max(i, j)]
        return total

    def add(p, s, q):
        return [
            (p[i] if q[i] is None else (s * q[i] if p[i] is None else p[i] + s * q[i]))
            for i in range(4)
        ]

    def image(p):
        out = [None] * 4

        def put(i, x):
            out[i] = x if out[i] is None else out[i] + x

        for i in range(3):
            if p[i] is None:
                continue
            put(i, SHIFT * p[i])
            if i == 0:
                put(1, SCALE * p[0])
            else:
                put(i + 1, 0.5 * SCALE * p[i])
                put(i - 1, 0.5 * SCALE * p[i])
        return out

    x = [None] * 4
    r = [jnp.ones_like(gram[0, 0]), None, None, None]
    p = list(r)
    norm = form(r, r)
    for it in range(ITERS):
        ap = image(p)
        step = norm / form(p, ap)
        x = add(x, step, p)
        r = add(r, -step, ap)
        if it + 1 < ITERS:
            new = form(r, r)
            p = add(r, new / norm, p)
            norm = new
    return x, r


def lat_index():
    return 2 * lax.axis_index("xl") + lax.axis_index("core")


def mirror16(x):
    lane = lax.broadcasted_iota(jnp.int32, x.shape, 1)
    for bit in (1, 2, 4, 8):
        x = jnp.where((lane & bit) != 0, pltpu.roll(x, bit, 1), pltpu.roll(x, 128 - bit, 1))
    return x


def pack_kernel(t, s, u, v, elev, flag, depth, fc, up, down, fields, edges, source, tile):
    nl, ni, nj = t.shape
    ocean = flag[...] == 1
    wet = depth[...]
    lane = lax.broadcasted_iota(jnp.int32, (ni, 128), 1)
    em = jnp.zeros((ni, nj), jnp.float32)
    nm = jnp.zeros((ni, nj), jnp.float32)
    zero = jnp.zeros((8, nj), jnp.float32)
    for l in range(nl):
        m = jnp.where(ocean & (wet > l), 1.0, 0.0)
        tt, ss, uu, vv = t[l] * m, s[l] * m, u[l] * m, v[l] * m
        em = em + uu
        nm = nm + vv
        up[8 * l : 8 * l + 3] = tt[ni - 3 :]
        up[8 * l + 3 : 8 * l + 6] = ss[ni - 3 :]
        up[8 * l + 6 : 8 * l + 7] = uu[ni - 1 :]
        up[8 * l + 7 : 8 * l + 8] = zero[:1]
        down[8 * l : 8 * l + 3] = tt[:3]
        down[8 * l + 3 : 8 * l + 6] = ss[:3]
        down[8 * l + 6 : 8 * l + 8] = zero[:2]
        x = jnp.where(lane < 8, tt[:, :128], tt[:, nj - 128 :])
        x = jnp.where((lane >= 8) & (lane < 16), pltpu.roll(ss[:, :128], 8, 1), x)
        x = jnp.where((lane >= 112) & (lane < 120), pltpu.roll(ss[:, nj - 128 :], 120, 1), x)
        x = jnp.where((lane >= 104) & (lane < 112), pltpu.roll(vv[:, nj - 128 :], 112, 1), x)
        tile[ni * l : ni * (l + 1)] = x
    em = em / nl
    nm = nm / nl
    part = elev[...] - em - nm
    coupler = 2.0 * jnp.sqrt((wet * flag[...]).astype(jnp.float32) / nl)
    for k, f in enumerate((part, em, nm, coupler)):
        fields[k] = f
    up[64:67] = part[ni - 3 :]
    up[67:71] = em[ni - 4 :]
    up[71:74] = nm[ni - 3 :]
    up[74:77] = coupler[ni - 3 :]
    up[77:80] = zero[:3]
    down[64:67] = part[:3]
    down[67:70] = em[:3]
    down[70:73] = nm[:3]
    down[73:76] = coupler[:3]
    down[76:80] = zero[:4]
    turned = tile[...].T
    edges[0:16] = turned[0:16]
    edges[16:40] = turned[104:128]
    block = lax.shift_right_logical(jnp.broadcast_to(fc[0:1, 0:1], (8, 128)), 4)
    row = jnp.zeros((8, 128), jnp.int32)
    nz = lax.axis_size("z")
    for k in range(1, lax.axis_size("y") * lax.axis_size("xh")):
        row = row + jnp.where(block >= nz * k, 1, 0)
    source[0] = block - nz * row
    source[1] = row


def widen_kernel(west, east, fields, edges, wide, slots):
    _, ni, nj = fields.shape
    lat = lat_index()
    blank = jnp.zeros((8, nj), jnp.float32)
    spans = ((64, 67, 64, 67), (67, 71, 67, 70), (71, 74, 70, 73), (74, 77, 73, 76))
    for k, (w0, w1, e0, e1) in enumerate(spans):
        wide[k, 0:8] = blank
        wide[k, 24:32] = blank
        wide[k, 8 - (w1 - w0) : 8] = west[w0:w1]
        wide[k, 8 : 8 + ni] = fields[k]
        wide[k, 24 : 24 + (e1 - e0)] = east[e0:e1]
    lane = lax.broadcasted_iota(jnp.int32, (4, 32, 128), 2)
    both = jnp.where(lane < 64, wide[:, :, 0:128], wide[:, :, nj - 128 : nj])
    turned = both.reshape(128, 128).T
    none = jnp.zeros((4, 128), jnp.float32)
    fold = jnp.concatenate(
        [edges[k : k + 1] for k in (39, 38, 37, 31, 30, 29)] + [none[:2]], axis=0
    )
    fold = mirror16(fold)
    north = jnp.concatenate(
        [edges[37:40], edges[29:32], edges[23:24], none[:1]], axis=0
    )
    south = jnp.concatenate([edges[0:3], edges[8:11], none[:2]], axis=0)
    for p in range(4):
        ahead = p > lat
        slots[p, 0:8] = jnp.where(ahead, north, south)
        slots[p, 8:12] = jnp.where(ahead, turned[124:128], turned[0:4])
        slots[p, 12:14] = fold[2 * p : 2 * p + 2]
        slots[p, 14:16] = none[:2]


def krylov_kernel(wide, got, basis_ref, message, tile):
    ni, nj = basis_ref.shape[1:]
    lat = lat_index()
    tile[...] = jnp.zeros((128, 128), jnp.float32)
    tile[0:4] = jnp.where(lat < 3, got[jnp.minimum(lat + 1, 3), 8:12], 0.0)
    tile[124:128] = jnp.where(lat > 0, got[jnp.maximum(lat - 1, 0), 8:12], 0.0)
    beyond = tile[...].T.reshape(4, 32, 128)
    part, em, nm, cpl = (jnp.concatenate([wide[k], beyond[k]], axis=1) for k in range(4))
    rows, lanes = part.shape
    b0 = part + pltpu.roll(em, 1, 0) + pltpu.roll(nm, 1, 1)

    def scaled(e):
        f = cpl * e
        lap = (
            4.0 * f
            - pltpu.roll(f, 1, 0)
            - pltpu.roll(f, rows - 1, 0)
            - pltpu.roll(f, 1, 1)
            - pltpu.roll(f, lanes - 1, 1)
        )
        return ((1.0 - SHIFT) * e + cpl * lap) * (1.0 / SCALE)

    b1 = scaled(b0)
    b2 = 2.0 * scaled(b1) - b0
    b3 = 2.0 * scaled(b2) - b1
    basis = [b[8 : 8 + ni, :nj] for b in (b0, b1, b2, b3)]
    for k in range(4):
        basis_ref[k] = basis[k]
    row = lax.broadcasted_iota(jnp.int32, (4, 128), 0)
    col = lax.broadcasted_iota(jnp.int32, (4, 128), 1)
    total = jnp.concatenate([got[3, 12:14], jnp.zeros((2, 128), jnp.float32)], axis=0)
    for n, (i, j) in enumerate(PAIRS):
        prod = basis[i] * basis[j]
        prod = prod[:8] + prod[8:]
        acc = prod[:, :128]
        for k in range(1, nj // 128):
            acc = acc + prod[:, 128 * k : 128 * (k + 1)]
        one = jnp.sum(jnp.sum(acc, axis=0, keepdims=True), axis=1, keepdims=True)
        total = jnp.where((row == 2) & (col == n), one, total)
    for k in range(message.shape[0]):
        message[k] = total


def relay_kernel(source, got, message):
    peers = got.shape[0]
    total = got[0]
    for k in range(1, peers):
        total = total + got[k]
    which = source[0, 0:2]
    pieces = []
    for p in range(3):
        piece = got[p, 0:2]
        for z in range(1, peers // 4):
            piece = jnp.where(which == z, got[4 * z + p, 0:2], piece)
        pieces.append(piece)
    text = jnp.concatenate(pieces + [total[2:4]], axis=0)
    for k in range(message.shape[0]):
        message[k] = text


def finish_kernel(
    basis_ref, source, got, edges, tail, wet, base_t, base_s,
    surface_ref, residual_ref, out_t, out_s, tile, final, sems,
):
    del base_t, base_s
    total = got[0]
    fold = got[0]
    which = source[1]
    for k in range(1, got.shape[0]):
        total = total + got[k]
        fold = jnp.where(which == k, got[k], fold)
    last = jnp.where(lat_index() == 3, 1.0, 0.0)
    rows = [
        jnp.concatenate([edges[35:40], fold[0:3]], axis=0),
        jnp.concatenate([edges[27:32], fold[3:6]], axis=0),
    ]
    row = lax.broadcasted_iota(jnp.int32, (8, 128), 0)
    speed = jnp.where(row < 3, pltpu.roll(edges[16:24], 3, 0) * last, 0.0)
    pos = speed > 0.0
    nj = surface_ref.shape[1]
    copies = []
    for k, out in enumerate((out_t, out_s)):
        q = [rows[k]] + [pltpu.roll(rows[k], 8 - o, 0) for o in range(1, 6)]
        face = speed * weno_upwind(*[jnp.where(pos, q[i], q[5 - i]) for i in range(5)])
        change = face - jnp.where(row == 0, 0.0, pltpu.roll(face, 1, 0))
        tile[...] = jnp.zeros((128, 128), jnp.float32)
        tile[125:128] = change[0:3]
        final[k] = (tail[k] - tile[...].T.reshape(tail.shape[1:])) * wet[...]
        copy = pltpu.make_async_copy(final.at[k], out.at[:, :, nj - 128 : nj], sems.at[k])
        copy.start()
        copies.append(copy)
    line = total[6:7]
    col = lax.broadcasted_iota(jnp.int32, (1, 128), 1)
    gram = {}
    for n, pair in enumerate(PAIRS):
        gram[pair] = jnp.sum(jnp.where(col == n, line, 0.0), axis=1, keepdims=True)
    xc, rc = coefficients(gram)
    basis = [basis_ref[k] for k in range(4)]
    surface_ref[...] = sum(c * f for c, f in zip(xc, basis) if c is not None)
    residual_ref[...] = sum(c * f for c, f in zip(rc, basis) if c is not None)
    for copy in copies:
        copy.wait()


def near(value):
    return pltpu.with_memory_space_constraint(value, pltpu.VMEM)


def f32(*shape):
    return jax.ShapeDtypeStruct(shape, jnp.float32)


def vmem(*shape):
    return pltpu.VMEM(shape, jnp.float32)


def make_on_device(sizes):
    ny, nxh, nz, nxl, ncore = sizes
    n_lon, n_lat = ny * nxh * nz, nxl * ncore

    def on_device(t, s, u, v, elev, flag, depth, fc):
        nl, ni, nj = t.shape
        lat = lax.axis_index(LAT)
        last = lat == n_lat - 1

        up, down, fields, edges, source = pl.pallas_call(
            pack_kernel,
            out_shape=(
                vmem(80, nj),
                vmem(80, nj),
                vmem(4, ni, nj),
                vmem(40, 128),
                pltpu.VMEM((2, 8, 128), jnp.int32),
            ),
            scratch_shapes=[vmem(128, 128)],
            name="pack",
        )(t, s, u, v, elev, flag, depth, fc.reshape(1, ni))
        west = lax.ppermute(up, LON, [(i, (i + 1) % n_lon) for i in range(n_lon)])
        east = lax.ppermute(down, LON, [((i + 1) % n_lon, i) for i in range(n_lon)])
        wide, slots = pl.pallas_call(
            widen_kernel,
            out_shape=(vmem(4, 32, nj), vmem(4, 16, 128)),
            name="widen",
        )(near(west), near(east), near(fields), near(edges))
        halo = lax.all_to_all(slots, LAT, 0, 0)
        basis, message = pl.pallas_call(
            krylov_kernel,
            out_shape=(vmem(4, ni, nj), vmem(nz * n_lat, 4, 128)),
            scratch_shapes=[vmem(128, 128)],
            name="krylov",
        )(near(wide), near(halo))
        got = lax.all_to_all(message, ("z",) + LAT, 0, 0)
        message = pl.pallas_call(
            relay_kernel, out_shape=vmem(ny * nxh, 8, 128), name="relay"
        )(near(source), near(got))
        got = lax.all_to_all(message, ("y", "xh"), 0, 0)
        level = lax.broadcasted_iota(jnp.int32, t.shape, 0)
        mask = jnp.where((flag[None] == 1) & (level < depth[None]), 1.0, 0.0).astype(jnp.float32)
        q = jnp.stack([t * mask, s * mask])
        ue = u * mask
        vn = v * mask

        def sides(msg):
            tiles = msg[: 8 * nl].reshape(nl, 8, nj)
            return jnp.stack([tiles[:, 0:3], tiles[:, 3:6]]), tiles[:, 6:7]

        q_west, u_west = sides(west)
        q_east, _ = sides(east)
        north = jnp.where(
            last, 0.0, lax.dynamic_index_in_dim(halo, jnp.minimum(lat + 1, n_lat - 1), 0, False)
        )
        south = jnp.where(
            lat == 0, 0.0, lax.dynamic_index_in_dim(halo, jnp.maximum(lat - 1, 0), 0, False)
        )

        def columns(msg):
            return jnp.transpose(msg[:6].reshape(2, 3, nl, ni), (0, 2, 3, 1))

        q_north, q_south = columns(north), columns(south)
        v_south = south[6].reshape(nl, ni, 1)
        zonal = jnp.concatenate([q_west, q, q_east], axis=2)
        merid = jnp.concatenate([q_south, q, q_north], axis=3)
        speed_x = jnp.concatenate([u_west, ue], axis=1)
        place = lax.broadcasted_iota(jnp.int32, (1, 1, nj + 1), 2)
        speed_y = jnp.concatenate([v_south, vn], axis=2)
        speed_y = jnp.where(last & (place > nj - 3), 0.0, speed_y)
        flux_x = face_flux(zonal, speed_x[None], ni + 1, 2)
        flux_y = face_flux(merid, speed_y[None], nj + 1, 3)
        updated = q - (flux_x[:, :, 1:] - flux_x[:, :, :-1]) - (flux_y[..., 1:] - flux_y[..., :-1])
        updated = updated * mask
        hbm, local = pl.BlockSpec(memory_space=pl.ANY), pl.BlockSpec(memory_space=pltpu.VMEM)
        surface, residual, t_next, s_next = pl.pallas_call(
            finish_kernel,
            in_specs=[local] * 6 + [hbm] * 2,
            out_specs=(local, local, hbm, hbm),
            out_shape=(f32(ni, nj), f32(ni, nj), f32(nl, ni, nj), f32(nl, ni, nj)),
            input_output_aliases={6: 2, 7: 3},
            scratch_shapes=[vmem(128, 128), vmem(2, nl, ni, 128), pltpu.SemaphoreType.DMA((2,))],
            name="finish",
        )(
            near(basis),
            near(source),
            near(got),
            near(edges),
            near(updated[..., nj - 128 :]),
            near(mask[..., nj - 128 :]),
            updated[0],
            updated[1],
        )
        return t_next, s_next, surface, residual

    return on_device


def solution(mesh, sizes=SIZES):
    fine = Mesh(mesh.devices.reshape(sizes), ALL)
    block, plane = P(None, LON, LAT), P(LON, LAT)
    return jax.shard_map(
        make_on_device(sizes),
        mesh=fine,
        in_specs=(block,) * 4 + (plane,) * 3 + (P(LON),),
        out_specs=(block, block, plane, plane),
        check_vma=False,
    )
```

```python
import jax
import jax.numpy as jnp
from jax import lax
from jax.experimental import pallas as pl
from jax.experimental.pallas import tpu as pltpu
from jax.sharding import Mesh, PartitionSpec as P

ITERS = 3
LON = ("y", "xh", "z")
LAT = ("xl", "core")
ALL = LON + LAT
SIZES = (8, 2, 12, 2, 2)
SHIFT = 17.0
SCALE = 16.0
PAIRS = [(i, j) for i in range(4) for j in range(i, 4)]


def weno_upwind(a, b, c, d, e):
    d0, d1, d2, d3 = b - a, c - b, d - c, e - d
    s0, s1, s2 = d1 - d0, d2 - d1, d3 - d2
    t0 = s0 + 2.0 * d1
    t1 = d1 + d2
    t2 = s2 - 2.0 * d2
    k = 13.0 / 12.0
    e0 = 1e-06 + k * s0 * s0 + 0.25 * t0 * t0
    e1 = 1e-06 + k * s1 * s1 + 0.25 * t1 * t1
    e2 = 1e-06 + k * s2 * s2 + 0.25 * t2 * t2
    w0, w1, w2 = e1 * e2, e0 * e2, e0 * e1
    w0, w1, w2 = 0.1 * w0 * w0, 0.6 * w1 * w1, 0.3 * w2 * w2
    top = w0 * (5.0 * d1 - 2.0 * d0) + w1 * (d1 + 2.0 * d2) + w2 * (4.0 * d2 - d3)
    return c + top / (6.0 * (w0 + w1 + w2))


def face_flux(padded, speed, count, axis):
    q = [lax.slice_in_dim(padded, o, o + count, axis=axis) for o in range(6)]
    pos = speed > 0.0
    a, b, c, d, e = (jnp.where(pos, q[i], q[5 - i]) for i in range(5))
    return speed * weno_upwind(a, b, c, d, e)


def coefficients(gram):
    def form(p, q):
        total = 0.0
        for i in range(4):
            for j in range(4):
                if p[i] is not None and q[j] is not None:
                    total = total + p[i] * q[j] * gram[min(i, j), max(i, j)]
        return total

    def add(p, s, q):
        return [
            (p[i] if q[i] is None else (s * q[i] if p[i] is None else p[i] + s * q[i]))
            for i in range(4)
        ]

    def image(p):
        out = [None] * 4

        def put(i, x):
            out[i] = x if out[i] is None else out[i] + x

        for i in range(3):
            if p[i] is None:
                continue
            put(i, SHIFT * p[i])
            if i == 0:
                put(1, SCALE * p[0])
            else:
                put(i + 1, 0.5 * SCALE * p[i])
                put(i - 1, 0.5 * SCALE * p[i])
        return out

    x = [None] * 4
    r = [jnp.ones_like(gram[0, 0]), None, None, None]
    p = list(r)
    norm = form(r, r)
    for it in range(ITERS):
        ap = image(p)
        step = norm / form(p, ap)
        x = add(x, step, p)
        r = add(r, -step, ap)
        if it + 1 < ITERS:
            new = form(r, r)
            p = add(r, new / norm, p)
            norm = new
    return x, r


def lat_index():
    return 2 * lax.axis_index("xl") + lax.axis_index("core")


def mirror16(x):
    lane = lax.broadcasted_iota(jnp.int32, x.shape, 1)
    for bit in (1, 2, 4, 8):
        x = jnp.where((lane & bit) != 0, pltpu.roll(x, bit, 1), pltpu.roll(x, 128 - bit, 1))
    return x


def lon_even():
    return lax.rem(lax.axis_index("z"), 2) == 0


def pack_kernel(
    t, s, u, v, elev, flag, depth, fc, far, close, fields, edges, source, up, down, tile
):
    nl, ni, nj = t.shape
    ocean = flag[...] == 1
    wet = depth[...]
    lane = lax.broadcasted_iota(jnp.int32, (ni, 128), 1)
    em = jnp.zeros((ni, nj), jnp.float32)
    nm = jnp.zeros((ni, nj), jnp.float32)
    zero = jnp.zeros((8, nj), jnp.float32)
    for l in range(nl):
        m = jnp.where(ocean & (wet > l), 1.0, 0.0)
        tt, ss, uu, vv = t[l] * m, s[l] * m, u[l] * m, v[l] * m
        em = em + uu
        nm = nm + vv
        up[8 * l : 8 * l + 3] = tt[ni - 3 :]
        up[8 * l + 3 : 8 * l + 6] = ss[ni - 3 :]
        up[8 * l + 6 : 8 * l + 7] = uu[ni - 1 :]
        up[8 * l + 7 : 8 * l + 8] = zero[:1]
        down[8 * l : 8 * l + 3] = tt[:3]
        down[8 * l + 3 : 8 * l + 6] = ss[:3]
        down[8 * l + 6 : 8 * l + 8] = zero[:2]
        x = jnp.where(lane < 8, tt[:, :128], tt[:, nj - 128 :])
        x = jnp.where((lane >= 8) & (lane < 16), pltpu.roll(ss[:, :128], 8, 1), x)
        x = jnp.where((lane >= 112) & (lane < 120), pltpu.roll(ss[:, nj - 128 :], 120, 1), x)
        x = jnp.where((lane >= 104) & (lane < 112), pltpu.roll(vv[:, nj - 128 :], 112, 1), x)
        tile[ni * l : ni * (l + 1)] = x
    em = em / nl
    nm = nm / nl
    part = elev[...] - em - nm
    coupler = 2.0 * jnp.sqrt((wet * flag[...]).astype(jnp.float32) / nl)
    for k, f in enumerate((part, em, nm, coupler)):
        fields[k] = f
    up[64:67] = part[ni - 3 :]
    up[67:71] = em[ni - 4 :]
    up[71:74] = nm[ni - 3 :]
    up[74:77] = coupler[ni - 3 :]
    up[77:80] = zero[:3]
    down[64:67] = part[:3]
    down[67:70] = em[:3]
    down[70:73] = nm[:3]
    down[73:76] = coupler[:3]
    down[76:80] = zero[:4]
    even = lon_even()
    far[...] = jnp.where(even, down[...], up[...])
    close[...] = jnp.where(even, up[...], down[...])
    turned = tile[...].T
    edges[0:16] = turned[0:16]
    edges[16:40] = turned[104:128]
    block = lax.shift_right_logical(jnp.broadcast_to(fc[0:1, 0:1], (8, 128)), 4)
    row = jnp.zeros((8, 128), jnp.int32)
    nz = lax.axis_size("z")
    for k in range(1, lax.axis_size("y") * lax.axis_size("xh")):
        row = row + jnp.where(block >= nz * k, 1, 0)
    source[0] = block - nz * row
    source[1] = row


def widen_kernel(far, close, fields, edges, wide, slots):
    _, ni, nj = fields.shape
    lat = lat_index()
    even = lon_even()
    blank = jnp.zeros((8, nj), jnp.float32)
    spans = ((64, 67, 64, 67), (67, 71, 67, 70), (71, 74, 70, 73), (74, 77, 73, 76))
    for k, (w0, w1, e0, e1) in enumerate(spans):
        wide[k, 0:8] = blank
        wide[k, 24:32] = blank
        wide[k, 8 - (w1 - w0) : 8] = jnp.where(even, far[w0:w1], close[w0:w1])
        wide[k, 8 : 8 + ni] = fields[k]
        wide[k, 24 : 24 + (e1 - e0)] = jnp.where(even, close[e0:e1], far[e0:e1])
    lane = lax.broadcasted_iota(jnp.int32, (4, 32, 128), 2)
    both = jnp.where(lane < 64, wide[:, :, 0:128], wide[:, :, nj - 128 : nj])
    turned = both.reshape(128, 128).T
    none = jnp.zeros((4, 128), jnp.float32)
    fold = jnp.concatenate(
        [edges[k : k + 1] for k in (39, 38, 37, 31, 30, 29)] + [none[:2]], axis=0
    )
    fold = mirror16(fold)
    north = jnp.concatenate(
        [edges[37:40], edges[29:32], edges[23:24], none[:1]], axis=0
    )
    south = jnp.concatenate([edges[0:3], edges[8:11], none[:2]], axis=0)
    for p in range(4):
        ahead = p > lat
        slots[p, 0:8] = jnp.where(ahead, north, south)
        slots[p, 8:12] = jnp.where(ahead, turned[124:128], turned[0:4])
        slots[p, 12:15] = fold[0:3] if p < 2 else fold[3:6]
        slots[p, 15:16] = none[:1]


def krylov_kernel(wide, got, basis_ref, message, rims, tile):
    ni, nj = basis_ref.shape[1:]
    lat = lat_index()
    tile[...] = jnp.zeros((128, 128), jnp.float32)
    north = jnp.where(lat < 3, got[jnp.minimum(lat + 1, 3)], 0.0)
    south = jnp.where(lat > 0, got[jnp.maximum(lat - 1, 0)], 0.0)
    rims[0] = north[0:8]
    rims[1] = south[0:8]
    tile[0:4] = north[8:12]
    tile[124:128] = south[8:12]
    beyond = tile[...].T.reshape(4, 32, 128)
    part, em, nm, cpl = (jnp.concatenate([wide[k], beyond[k]], axis=1) for k in range(4))
    rows, lanes = part.shape
    b0 = part + pltpu.roll(em, 1, 0) + pltpu.roll(nm, 1, 1)

    def scaled(e):
        f = cpl * e
        lap = (
            4.0 * f
            - pltpu.roll(f, 1, 0)
            - pltpu.roll(f, rows - 1, 0)
            - pltpu.roll(f, 1, 1)
            - pltpu.roll(f, lanes - 1, 1)
        )
        return ((1.0 - SHIFT) * e + cpl * lap) * (1.0 / SCALE)

    b1 = scaled(b0)
    b2 = 2.0 * scaled(b1) - b0
    b3 = 2.0 * scaled(b2) - b1
    basis = [b[8 : 8 + ni, :nj] for b in (b0, b1, b2, b3)]
    for k in range(4):
        basis_ref[k] = basis[k]
    row = lax.broadcasted_iota(jnp.int32, (4, 128), 0)
    col = lax.broadcasted_iota(jnp.int32, (4, 128), 1)
    total = jnp.concatenate([got[3, 12:15], jnp.zeros((1, 128), jnp.float32)], axis=0)
    for n, (i, j) in enumerate(PAIRS):
        prod = basis[i] * basis[j]
        prod = prod[:8] + prod[8:]
        acc = prod[:, :128]
        for k in range(1, nj // 128):
            acc = acc + prod[:, 128 * k : 128 * (k + 1)]
        one = jnp.sum(jnp.sum(acc, axis=0, keepdims=True), axis=1, keepdims=True)
        total = jnp.where((row == 3) & (col == n), one, total)
    for k in range(message.shape[0]):
        message[k] = total


def relay_kernel(source, got, message):
    peers = got.shape[0]
    total = got[0]
    for k in range(1, peers):
        total = total + got[k]
    which = source[0, 0:4]
    piece = got[0]
    for z in range(1, peers // 2):
        piece = jnp.where(which == z, got[2 * z], piece)
    row = lax.broadcasted_iota(jnp.int32, (4, 128), 0)
    text = jnp.where(row < 3, piece, total)
    for k in range(message.shape[0]):
        message[k] = text


def finish_kernel(
    basis_ref, source, got, edges, tail, wet, base_t, base_s,
    surface_ref, residual_ref, out_t, out_s, tile, final, sems,
):
    del base_t, base_s
    total = got[0]
    for k in range(1, got.shape[0]):
        total = total + got[k]
    fold = [got[0], got[1]]
    which = source[1, 0:4]
    for k in range(1, got.shape[0] // 2):
        fold = [jnp.where(which == k, got[2 * k + i], fold[i]) for i in range(2)]
    last = jnp.where(lat_index() == 3, 1.0, 0.0)
    rows = [
        jnp.concatenate([edges[35:40], fold[0][0:3]], axis=0),
        jnp.concatenate([edges[27:32], fold[1][0:3]], axis=0),
    ]
    row = lax.broadcasted_iota(jnp.int32, (8, 128), 0)
    speed = jnp.where(row < 3, pltpu.roll(edges[16:24], 3, 0) * last, 0.0)
    pos = speed > 0.0
    nj = surface_ref.shape[1]
    copies = []
    for k, out in enumerate((out_t, out_s)):
        q = [rows[k]] + [pltpu.roll(rows[k], 8 - o, 0) for o in range(1, 6)]
        face = speed * weno_upwind(*[jnp.where(pos, q[i], q[5 - i]) for i in range(5)])
        change = face - jnp.where(row == 0, 0.0, pltpu.roll(face, 1, 0))
        tile[...] = jnp.zeros((128, 128), jnp.float32)
        tile[125:128] = change[0:3]
        final[k] = (tail[k] - tile[...].T.reshape(tail.shape[1:])) * wet[...]
        copy = pltpu.make_async_copy(final.at[k], out.at[:, :, nj - 128 : nj], sems.at[k])
        copy.start()
        copies.append(copy)
    line = total[3:4]
    col = lax.broadcasted_iota(jnp.int32, (1, 128), 1)
    gram = {}
    for n, pair in enumerate(PAIRS):
        gram[pair] = jnp.sum(jnp.where(col == n, line, 0.0), axis=1, keepdims=True)
    xc, rc = coefficients(gram)
    basis = [basis_ref[k] for k in range(4)]
    surface_ref[...] = sum(c * f for c, f in zip(xc, basis) if c is not None)
    residual_ref[...] = sum(c * f for c, f in zip(rc, basis) if c is not None)
    for copy in copies:
        copy.wait()


def near(value):
    return pltpu.with_memory_space_constraint(value, pltpu.VMEM)


def f32(*shape):
    return jax.ShapeDtypeStruct(shape, jnp.float32)


def vmem(*shape):
    return pltpu.VMEM(shape, jnp.float32)


def make_on_device(sizes):
    ny, nxh, nz, nxl, ncore = sizes
    n_lon, n_lat = ny * nxh * nz, nxl * ncore

    def on_device(t, s, u, v, elev, flag, depth, fc):
        nl, ni, nj = t.shape
        lat = lax.axis_index(LAT)
        last = lat == n_lat - 1

        far, close, fields, edges, source = pl.pallas_call(
            pack_kernel,
            out_shape=(
                vmem(80, nj),
                vmem(80, nj),
                vmem(4, ni, nj),
                vmem(40, 128),
                pltpu.VMEM((2, 8, 128), jnp.int32),
            ),
            scratch_shapes=[vmem(80, nj), vmem(80, nj), vmem(128, 128)],
            name="pack",
        )(t, s, u, v, elev, flag, depth, fc.reshape(1, ni))
        def swaps(first):
            pairs = []
            for i in range(first, n_lon, 2):
                pairs += [(i, (i + 1) % n_lon), ((i + 1) % n_lon, i)]
            return pairs

        far = lax.ppermute(far, LON, swaps(1))
        close = lax.ppermute(close, LON, swaps(0))
        wide, slots = pl.pallas_call(
            widen_kernel,
            out_shape=(vmem(4, 32, nj), vmem(4, 16, 128)),
            name="widen",
        )(near(far), near(close), near(fields), near(edges))
        halo = lax.all_to_all(slots, LAT, 0, 0)
        basis, message, rims = pl.pallas_call(
            krylov_kernel,
            out_shape=(vmem(4, ni, nj), vmem(nz * ncore, 4, 128), vmem(2, 8, 128)),
            scratch_shapes=[vmem(128, 128)],
            name="krylov",
        )(near(wide), near(halo))
        got = lax.all_to_all(message, ("z", "core"), 0, 0)
        message = pl.pallas_call(
            relay_kernel, out_shape=vmem(ny * nxh * nxl, 4, 128), name="relay"
        )(near(source), near(got))
        got = lax.all_to_all(message, ("y", "xh", "xl"), 0, 0)
        level = lax.broadcasted_iota(jnp.int32, t.shape, 0)
        mask = jnp.where((flag[None] == 1) & (level < depth[None]), 1.0, 0.0).astype(jnp.float32)
        q = jnp.stack([t * mask, s * mask])
        ue = u * mask
        vn = v * mask

        def sides(msg):
            tiles = msg[: 8 * nl].reshape(nl, 8, nj)
            return jnp.stack([tiles[:, 0:3], tiles[:, 3:6]]), tiles[:, 6:7]

        even = lon_even()
        west = jnp.where(even, far, close)
        east = jnp.where(even, close, far)
        q_west, u_west = sides(west)
        q_east, _ = sides(east)
        north, south = rims[0], rims[1]

        def columns(msg):
            return jnp.transpose(msg[:6].reshape(2, 3, nl, ni), (0, 2, 3, 1))

        q_north, q_south = columns(north), columns(south)
        v_south = south[6].reshape(nl, ni, 1)
        zonal = jnp.concatenate([q_west, q, q_east], axis=2)
        merid = jnp.concatenate([q_south, q, q_north], axis=3)
        speed_x = jnp.concatenate([u_west, ue], axis=1)
        place = lax.broadcasted_iota(jnp.int32, (1, 1, nj + 1), 2)
        speed_y = jnp.concatenate([v_south, vn], axis=2)
        speed_y = jnp.where(last & (place > nj - 3), 0.0, speed_y)
        flux_x = face_flux(zonal, speed_x[None], ni + 1, 2)
        flux_y = face_flux(merid, speed_y[None], nj + 1, 3)
        updated = q - (flux_x[:, :, 1:] - flux_x[:, :, :-1]) - (flux_y[..., 1:] - flux_y[..., :-1])
        updated = updated * mask
        hbm, local = pl.BlockSpec(memory_space=pl.ANY), pl.BlockSpec(memory_space=pltpu.VMEM)
        surface, residual, t_next, s_next = pl.pallas_call(
            finish_kernel,
            in_specs=[local] * 6 + [hbm] * 2,
            out_specs=(local, local, hbm, hbm),
            out_shape=(f32(ni, nj), f32(ni, nj), f32(nl, ni, nj), f32(nl, ni, nj)),
            input_output_aliases={6: 2, 7: 3},
            scratch_shapes=[vmem(128, 128), vmem(2, nl, ni, 128), pltpu.SemaphoreType.DMA((2,))],
            name="finish",
        )(
            near(basis),
            near(source),
            near(got),
            near(edges),
            near(updated[..., nj - 128 :]),
            near(mask[..., nj - 128 :]),
            updated[0],
            updated[1],
        )
        return t_next, s_next, surface, residual

    return on_device


def solution(mesh, sizes=SIZES):
    fine = Mesh(mesh.devices.reshape(sizes), ALL)
    block, plane = P(None, LON, LAT), P(LON, LAT)
    return jax.shard_map(
        make_on_device(sizes),
        mesh=fine,
        in_specs=(block,) * 4 + (plane,) * 3 + (P(LON),),
        out_specs=(block, block, plane, plane),
        check_vma=False,
    )
```

```python
import jax
import jax.numpy as jnp
from jax import lax
from jax.experimental import pallas as pl
from jax.experimental.pallas import tpu as pltpu
from jax.sharding import Mesh, PartitionSpec as P

ITERS = 3
LON = ("y", "xh", "z")
LAT = ("xl", "core")
ALL = LON + LAT
SIZES = (8, 2, 12, 2, 2)
SHIFT = 17.0
SCALE = 16.0
PAIRS = [(i, j) for i in range(4) for j in range(i, 4)]


def weno_upwind(a, b, c, d, e):
    d0, d1, d2, d3 = b - a, c - b, d - c, e - d
    s0, s1, s2 = d1 - d0, d2 - d1, d3 - d2
    t0 = s0 + 2.0 * d1
    t1 = d1 + d2
    t2 = s2 - 2.0 * d2
    k = 13.0 / 12.0
    e0 = 1e-06 + k * s0 * s0 + 0.25 * t0 * t0
    e1 = 1e-06 + k * s1 * s1 + 0.25 * t1 * t1
    e2 = 1e-06 + k * s2 * s2 + 0.25 * t2 * t2
    w0, w1, w2 = e1 * e2, e0 * e2, e0 * e1
    w0, w1, w2 = 0.1 * w0 * w0, 0.6 * w1 * w1, 0.3 * w2 * w2
    top = w0 * (5.0 * d1 - 2.0 * d0) + w1 * (d1 + 2.0 * d2) + w2 * (4.0 * d2 - d3)
    return c + top / (6.0 * (w0 + w1 + w2))


def face_flux(padded, speed, count, axis):
    q = [lax.slice_in_dim(padded, o, o + count, axis=axis) for o in range(6)]
    pos = speed > 0.0
    a, b, c, d, e = (jnp.where(pos, q[i], q[5 - i]) for i in range(5))
    return speed * weno_upwind(a, b, c, d, e)


def coefficients(gram):
    def form(p, q):
        total = 0.0
        for i in range(4):
            for j in range(4):
                if p[i] is not None and q[j] is not None:
                    total = total + p[i] * q[j] * gram[min(i, j), max(i, j)]
        return total

    def add(p, s, q):
        return [
            (p[i] if q[i] is None else (s * q[i] if p[i] is None else p[i] + s * q[i]))
            for i in range(4)
        ]

    def image(p):
        out = [None] * 4

        def put(i, x):
            out[i] = x if out[i] is None else out[i] + x

        for i in range(3):
            if p[i] is None:
                continue
            put(i, SHIFT * p[i])
            if i == 0:
                put(1, SCALE * p[0])
            else:
                put(i + 1, 0.5 * SCALE * p[i])
                put(i - 1, 0.5 * SCALE * p[i])
        return out

    x = [None] * 4
    r = [jnp.ones_like(gram[0, 0]), None, None, None]
    p = list(r)
    norm = form(r, r)
    for it in range(ITERS):
        ap = image(p)
        step = norm / form(p, ap)
        x = add(x, step, p)
        r = add(r, -step, ap)
        if it + 1 < ITERS:
            new = form(r, r)
            p = add(r, new / norm, p)
            norm = new
    return x, r


def lat_index():
    return 2 * lax.axis_index("xl") + lax.axis_index("core")


def mirror16(x):
    lane = lax.broadcasted_iota(jnp.int32, x.shape, 1)
    for bit in (1, 2, 4, 8):
        x = jnp.where((lane & bit) != 0, pltpu.roll(x, bit, 1), pltpu.roll(x, 128 - bit, 1))
    return x


def lon_even():
    return lax.rem(lax.axis_index("z"), 2) == 0


def pack_kernel(
    t, s, u, v, elev, flag, depth, fc,
    far, close, far_q, close_q, fields, edges, source, up, down, tile
):
    nl, ni, nj = t.shape
    ocean = flag[...] == 1
    wet = depth[...]
    lane = lax.broadcasted_iota(jnp.int32, (ni, 128), 1)
    em = jnp.zeros((ni, nj), jnp.float32)
    nm = jnp.zeros((ni, nj), jnp.float32)
    zero = jnp.zeros((8, nj), jnp.float32)
    for l in range(nl):
        m = jnp.where(ocean & (wet > l), 1.0, 0.0)
        tt, ss, uu, vv = t[l] * m, s[l] * m, u[l] * m, v[l] * m
        em = em + uu
        nm = nm + vv
        up[8 * l : 8 * l + 3] = tt[ni - 3 :]
        up[8 * l + 3 : 8 * l + 6] = ss[ni - 3 :]
        up[8 * l + 6 : 8 * l + 7] = uu[ni - 1 :]
        up[8 * l + 7 : 8 * l + 8] = zero[:1]
        down[8 * l : 8 * l + 3] = tt[:3]
        down[8 * l + 3 : 8 * l + 6] = ss[:3]
        down[8 * l + 6 : 8 * l + 8] = zero[:2]
        x = jnp.where(lane < 8, tt[:, :128], tt[:, nj - 128 :])
        x = jnp.where((lane >= 8) & (lane < 16), pltpu.roll(ss[:, :128], 8, 1), x)
        x = jnp.where((lane >= 112) & (lane < 120), pltpu.roll(ss[:, nj - 128 :], 120, 1), x)
        x = jnp.where((lane >= 104) & (lane < 112), pltpu.roll(vv[:, nj - 128 :], 112, 1), x)
        tile[ni * l : ni * (l + 1)] = x
    em = em / nl
    nm = nm / nl
    part = elev[...] - em - nm
    coupler = 2.0 * jnp.sqrt((wet * flag[...]).astype(jnp.float32) / nl)
    for k, f in enumerate((part, em, nm, coupler)):
        fields[k] = f
    up[64:67] = part[ni - 3 :]
    up[67:71] = em[ni - 4 :]
    up[71:74] = nm[ni - 3 :]
    up[74:77] = coupler[ni - 3 :]
    up[77:80] = zero[:3]
    down[64:67] = part[:3]
    down[67:70] = em[:3]
    down[70:73] = nm[:3]
    down[73:76] = coupler[:3]
    down[76:80] = zero[:4]
    even = lon_even()
    far[...] = jnp.where(even, down[64:80], up[64:80])
    close[...] = jnp.where(even, up[64:80], down[64:80])
    far_q[...] = jnp.where(even, down[0:64], up[0:64])
    close_q[...] = jnp.where(even, up[0:64], down[0:64])
    turned = tile[...].T
    edges[0:16] = turned[0:16]
    edges[16:40] = turned[104:128]
    block = lax.shift_right_logical(jnp.broadcast_to(fc[0:1, 0:1], (8, 128)), 4)
    row = jnp.zeros((8, 128), jnp.int32)
    nz = lax.axis_size("z")
    for k in range(1, lax.axis_size("y") * lax.axis_size("xh")):
        row = row + jnp.where(block >= nz * k, 1, 0)
    source[0] = block - nz * row
    source[1] = row


def widen_kernel(far, close, fields, edges, wide, slots):
    _, ni, nj = fields.shape
    lat = lat_index()
    even = lon_even()
    blank = jnp.zeros((8, nj), jnp.float32)
    spans = ((0, 3, 0, 3), (3, 7, 3, 6), (7, 10, 6, 9), (10, 13, 9, 12))
    for k, (w0, w1, e0, e1) in enumerate(spans):
        wide[k, 0:8] = blank
        wide[k, 24:32] = blank
        wide[k, 8 - (w1 - w0) : 8] = jnp.where(even, far[w0:w1], close[w0:w1])
        wide[k, 8 : 8 + ni] = fields[k]
        wide[k, 24 : 24 + (e1 - e0)] = jnp.where(even, close[e0:e1], far[e0:e1])
    lane = lax.broadcasted_iota(jnp.int32, (4, 32, 128), 2)
    both = jnp.where(lane < 64, wide[:, :, 0:128], wide[:, :, nj - 128 : nj])
    turned = both.reshape(128, 128).T
    none = jnp.zeros((4, 128), jnp.float32)
    fold = jnp.concatenate(
        [edges[k : k + 1] for k in (39, 38, 37, 31, 30, 29)] + [none[:2]], axis=0
    )
    fold = mirror16(fold)
    north = jnp.concatenate(
        [edges[37:40], edges[29:32], edges[23:24], none[:1]], axis=0
    )
    south = jnp.concatenate([edges[0:3], edges[8:11], none[:2]], axis=0)
    for p in range(4):
        ahead = p > lat
        slots[p, 0:8] = jnp.where(ahead, north, south)
        slots[p, 8:12] = jnp.where(ahead, turned[124:128], turned[0:4])
        slots[p, 12:15] = fold[0:3] if p < 2 else fold[3:6]
        slots[p, 15:16] = none[:1]


def krylov_kernel(wide, got, basis_ref, message, rims, tile):
    ni, nj = basis_ref.shape[1:]
    lat = lat_index()
    tile[...] = jnp.zeros((128, 128), jnp.float32)
    north = jnp.where(lat < 3, got[jnp.minimum(lat + 1, 3)], 0.0)
    south = jnp.where(lat > 0, got[jnp.maximum(lat - 1, 0)], 0.0)
    rims[0] = north[0:8]
    rims[1] = south[0:8]
    tile[0:4] = north[8:12]
    tile[124:128] = south[8:12]
    beyond = tile[...].T.reshape(4, 32, 128)
    part, em, nm, cpl = (jnp.concatenate([wide[k], beyond[k]], axis=1) for k in range(4))
    rows, lanes = part.shape
    b0 = part + pltpu.roll(em, 1, 0) + pltpu.roll(nm, 1, 1)

    def scaled(e):
        f = cpl * e
        lap = (
            4.0 * f
            - pltpu.roll(f, 1, 0)
            - pltpu.roll(f, rows - 1, 0)
            - pltpu.roll(f, 1, 1)
            - pltpu.roll(f, lanes - 1, 1)
        )
        return ((1.0 - SHIFT) * e + cpl * lap) * (1.0 / SCALE)

    b1 = scaled(b0)
    b2 = 2.0 * scaled(b1) - b0
    b3 = 2.0 * scaled(b2) - b1
    basis = [b[8 : 8 + ni, :nj] for b in (b0, b1, b2, b3)]
    for k in range(4):
        basis_ref[k] = basis[k]
    row = lax.broadcasted_iota(jnp.int32, (4, 128), 0)
    col = lax.broadcasted_iota(jnp.int32, (4, 128), 1)
    total = jnp.concatenate([got[3, 12:15], jnp.zeros((1, 128), jnp.float32)], axis=0)
    for n, (i, j) in enumerate(PAIRS):
        prod = basis[i] * basis[j]
        prod = prod[:8] + prod[8:]
        acc = prod[:, :128]
        for k in range(1, nj // 128):
            acc = acc + prod[:, 128 * k : 128 * (k + 1)]
        one = jnp.sum(jnp.sum(acc, axis=0, keepdims=True), axis=1, keepdims=True)
        total = jnp.where((row == 3) & (col == n), one, total)
    for k in range(message.shape[0]):
        message[k] = total


def relay_kernel(source, got, message):
    peers = got.shape[0]
    total = got[0]
    for k in range(1, peers):
        total = total + got[k]
    which = source[0, 0:4]
    piece = got[0]
    for z in range(1, peers // 2):
        piece = jnp.where(which == z, got[2 * z], piece)
    row = lax.broadcasted_iota(jnp.int32, (4, 128), 0)
    text = jnp.where(row < 3, piece, total)
    for k in range(message.shape[0]):
        message[k] = text


def finish_kernel(
    basis_ref, source, got, edges, tail, wet, base_t, base_s,
    surface_ref, residual_ref, out_t, out_s, tile, final, sems,
):
    del base_t, base_s
    total = got[0]
    for k in range(1, got.shape[0]):
        total = total + got[k]
    fold = [got[0], got[1]]
    which = source[1, 0:4]
    for k in range(1, got.shape[0] // 2):
        fold = [jnp.where(which == k, got[2 * k + i], fold[i]) for i in range(2)]
    last = jnp.where(lat_index() == 3, 1.0, 0.0)
    rows = [
        jnp.concatenate([edges[35:40], fold[0][0:3]], axis=0),
        jnp.concatenate([edges[27:32], fold[1][0:3]], axis=0),
    ]
    row = lax.broadcasted_iota(jnp.int32, (8, 128), 0)
    speed = jnp.where(row < 3, pltpu.roll(edges[16:24], 3, 0) * last, 0.0)
    pos = speed > 0.0
    nj = surface_ref.shape[1]
    copies = []
    for k, out in enumerate((out_t, out_s)):
        q = [rows[k]] + [pltpu.roll(rows[k], 8 - o, 0) for o in range(1, 6)]
        face = speed * weno_upwind(*[jnp.where(pos, q[i], q[5 - i]) for i in range(5)])
        change = face - jnp.where(row == 0, 0.0, pltpu.roll(face, 1, 0))
        tile[...] = jnp.zeros((128, 128), jnp.float32)
        tile[125:128] = change[0:3]
        final[k] = (tail[k] - tile[...].T.reshape(tail.shape[1:])) * wet[...]
        copy = pltpu.make_async_copy(final.at[k], out.at[:, :, nj - 128 : nj], sems.at[k])
        copy.start()
        copies.append(copy)
    line = total[3:4]
    col = lax.broadcasted_iota(jnp.int32, (1, 128), 1)
    gram = {}
    for n, pair in enumerate(PAIRS):
        gram[pair] = jnp.sum(jnp.where(col == n, line, 0.0), axis=1, keepdims=True)
    xc, rc = coefficients(gram)
    basis = [basis_ref[k] for k in range(4)]
    surface_ref[...] = sum(c * f for c, f in zip(xc, basis) if c is not None)
    residual_ref[...] = sum(c * f for c, f in zip(rc, basis) if c is not None)
    for copy in copies:
        copy.wait()


def near(value):
    return pltpu.with_memory_space_constraint(value, pltpu.VMEM)


def f32(*shape):
    return jax.ShapeDtypeStruct(shape, jnp.float32)


def vmem(*shape):
    return pltpu.VMEM(shape, jnp.float32)


def make_on_device(sizes):
    ny, nxh, nz, nxl, ncore = sizes
    n_lon, n_lat = ny * nxh * nz, nxl * ncore

    def on_device(t, s, u, v, elev, flag, depth, fc):
        nl, ni, nj = t.shape
        lat = lax.axis_index(LAT)
        last = lat == n_lat - 1

        far, close, far_q, close_q, fields, edges, source = pl.pallas_call(
            pack_kernel,
            out_shape=(
                vmem(16, nj),
                vmem(16, nj),
                vmem(64, nj),
                vmem(64, nj),
                vmem(4, ni, nj),
                vmem(40, 128),
                pltpu.VMEM((2, 8, 128), jnp.int32),
            ),
            scratch_shapes=[vmem(80, nj), vmem(80, nj), vmem(128, 128)],
            name="pack",
        )(t, s, u, v, elev, flag, depth, fc.reshape(1, ni))
        def swaps(first):
            pairs = []
            for i in range(first, n_lon, 2):
                pairs += [(i, (i + 1) % n_lon), ((i + 1) % n_lon, i)]
            return pairs

        far = lax.ppermute(far, LON, swaps(1))
        close = lax.ppermute(close, LON, swaps(0))
        wide, slots = pl.pallas_call(
            widen_kernel,
            out_shape=(vmem(4, 32, nj), vmem(4, 16, 128)),
            name="widen",
        )(near(far), near(close), near(fields), near(edges))
        slots, far_q, close_q = lax.optimization_barrier((slots, far_q, close_q))
        halo = lax.all_to_all(slots, LAT, 0, 0)
        far_q = lax.ppermute(far_q, LON, swaps(1))
        close_q = lax.ppermute(close_q, LON, swaps(0))
        basis, message, rims = pl.pallas_call(
            krylov_kernel,
            out_shape=(vmem(4, ni, nj), vmem(nz * ncore, 4, 128), vmem(2, 8, 128)),
            scratch_shapes=[vmem(128, 128)],
            name="krylov",
        )(near(wide), near(halo))
        got = lax.all_to_all(message, ("z", "core"), 0, 0)
        message = pl.pallas_call(
            relay_kernel, out_shape=vmem(ny * nxh * nxl, 4, 128), name="relay"
        )(near(source), near(got))
        got = lax.all_to_all(message, ("y", "xh", "xl"), 0, 0)
        level = lax.broadcasted_iota(jnp.int32, t.shape, 0)
        mask = jnp.where((flag[None] == 1) & (level < depth[None]), 1.0, 0.0).astype(jnp.float32)
        q = jnp.stack([t * mask, s * mask])
        ue = u * mask
        vn = v * mask

        def sides(msg):
            tiles = msg[: 8 * nl].reshape(nl, 8, nj)
            return jnp.stack([tiles[:, 0:3], tiles[:, 3:6]]), tiles[:, 6:7]

        even = lon_even()
        west = jnp.where(even, far_q, close_q)
        east = jnp.where(even, close_q, far_q)
        q_west, u_west = sides(west)
        q_east, _ = sides(east)
        north, south = rims[0], rims[1]

        def columns(msg):
            return jnp.transpose(msg[:6].reshape(2, 3, nl, ni), (0, 2, 3, 1))

        q_north, q_south = columns(north), columns(south)
        v_south = south[6].reshape(nl, ni, 1)
        zonal = jnp.concatenate([q_west, q, q_east], axis=2)
        merid = jnp.concatenate([q_south, q, q_north], axis=3)
        speed_x = jnp.concatenate([u_west, ue], axis=1)
        place = lax.broadcasted_iota(jnp.int32, (1, 1, nj + 1), 2)
        speed_y = jnp.concatenate([v_south, vn], axis=2)
        speed_y = jnp.where(last & (place > nj - 3), 0.0, speed_y)
        flux_x = face_flux(zonal, speed_x[None], ni + 1, 2)
        flux_y = face_flux(merid, speed_y[None], nj + 1, 3)
        updated = q - (flux_x[:, :, 1:] - flux_x[:, :, :-1]) - (flux_y[..., 1:] - flux_y[..., :-1])
        updated = updated * mask
        hbm, local = pl.BlockSpec(memory_space=pl.ANY), pl.BlockSpec(memory_space=pltpu.VMEM)
        surface, residual, t_next, s_next = pl.pallas_call(
            finish_kernel,
            in_specs=[local] * 6 + [hbm] * 2,
            out_specs=(local, local, hbm, hbm),
            out_shape=(f32(ni, nj), f32(ni, nj), f32(nl, ni, nj), f32(nl, ni, nj)),
            input_output_aliases={6: 2, 7: 3},
            scratch_shapes=[vmem(128, 128), vmem(2, nl, ni, 128), pltpu.SemaphoreType.DMA((2,))],
            name="finish",
        )(
            near(basis),
            near(source),
            near(got),
            near(edges),
            near(updated[..., nj - 128 :]),
            near(mask[..., nj - 128 :]),
            updated[0],
            updated[1],
        )
        return t_next, s_next, surface, residual

    return on_device


def solution(mesh, sizes=SIZES):
    fine = Mesh(mesh.devices.reshape(sizes), ALL)
    block, plane = P(None, LON, LAT), P(LON, LAT)
    return jax.shard_map(
        make_on_device(sizes),
        mesh=fine,
        in_specs=(block,) * 4 + (plane,) * 3 + (P(LON),),
        out_specs=(block, block, plane, plane),
        check_vma=False,
    )
```

```python
import jax
import jax.numpy as jnp
from jax import lax
from jax.experimental import pallas as pl
from jax.experimental.pallas import tpu as pltpu
from jax.sharding import Mesh, PartitionSpec as P

ITERS = 3
LON = ("y", "xh", "z")
LAT = ("xl", "core")
ALL = LON + LAT
SIZES = (8, 2, 12, 2, 2)
SHIFT = 17.0
SCALE = 16.0
PAIRS = [(i, j) for i in range(4) for j in range(i, 4)]


def weno_upwind(a, b, c, d, e):
    d0, d1, d2, d3 = b - a, c - b, d - c, e - d
    s0, s1, s2 = d1 - d0, d2 - d1, d3 - d2
    t0 = s0 + 2.0 * d1
    t1 = d1 + d2
    t2 = s2 - 2.0 * d2
    k = 13.0 / 12.0
    e0 = 1e-06 + k * s0 * s0 + 0.25 * t0 * t0
    e1 = 1e-06 + k * s1 * s1 + 0.25 * t1 * t1
    e2 = 1e-06 + k * s2 * s2 + 0.25 * t2 * t2
    w0, w1, w2 = e1 * e2, e0 * e2, e0 * e1
    w0, w1, w2 = 0.1 * w0 * w0, 0.6 * w1 * w1, 0.3 * w2 * w2
    top = w0 * (5.0 * d1 - 2.0 * d0) + w1 * (d1 + 2.0 * d2) + w2 * (4.0 * d2 - d3)
    return c + top / (6.0 * (w0 + w1 + w2))


def face_flux(padded, speed, count, axis):
    q = [lax.slice_in_dim(padded, o, o + count, axis=axis) for o in range(6)]
    pos = speed > 0.0
    a, b, c, d, e = (jnp.where(pos, q[i], q[5 - i]) for i in range(5))
    return speed * weno_upwind(a, b, c, d, e)


def coefficients(gram):
    def form(p, q):
        total = 0.0
        for i in range(4):
            for j in range(4):
                if p[i] is not None and q[j] is not None:
                    total = total + p[i] * q[j] * gram[min(i, j), max(i, j)]
        return total

    def add(p, s, q):
        return [
            (p[i] if q[i] is None else (s * q[i] if p[i] is None else p[i] + s * q[i]))
            for i in range(4)
        ]

    def image(p):
        out = [None] * 4

        def put(i, x):
            out[i] = x if out[i] is None else out[i] + x

        for i in range(3):
            if p[i] is None:
                continue
            put(i, SHIFT * p[i])
            if i == 0:
                put(1, SCALE * p[0])
            else:
                put(i + 1, 0.5 * SCALE * p[i])
                put(i - 1, 0.5 * SCALE * p[i])
        return out

    x = [None] * 4
    r = [jnp.ones_like(gram[0, 0]), None, None, None]
    p = list(r)
    norm = form(r, r)
    for it in range(ITERS):
        ap = image(p)
        step = norm / form(p, ap)
        x = add(x, step, p)
        r = add(r, -step, ap)
        if it + 1 < ITERS:
            new = form(r, r)
            p = add(r, new / norm, p)
            norm = new
    return x, r


def lat_index():
    return 2 * lax.axis_index("xl") + lax.axis_index("core")


def mirror16(x):
    lane = lax.broadcasted_iota(jnp.int32, x.shape, 1)
    for bit in (1, 2, 4, 8):
        x = jnp.where((lane & bit) != 0, pltpu.roll(x, bit, 1), pltpu.roll(x, 128 - bit, 1))
    return x


def lon_even():
    return lax.rem(lax.axis_index("z"), 2) == 0


def pack_kernel(
    t, s, u, v, elev, flag, depth, fc, far, close, fields, edges, source, slots, up, down, tile
):
    nl, ni, nj = t.shape
    ocean = flag[...] == 1
    wet = depth[...]
    lane = lax.broadcasted_iota(jnp.int32, (ni, 128), 1)
    em = jnp.zeros((ni, nj), jnp.float32)
    nm = jnp.zeros((ni, nj), jnp.float32)
    zero = jnp.zeros((8, nj), jnp.float32)
    for l in range(nl):
        m = jnp.where(ocean & (wet > l), 1.0, 0.0)
        tt, ss, uu, vv = t[l] * m, s[l] * m, u[l] * m, v[l] * m
        em = em + uu
        nm = nm + vv
        up[8 * l : 8 * l + 3] = tt[ni - 3 :]
        up[8 * l + 3 : 8 * l + 6] = ss[ni - 3 :]
        up[8 * l + 6 : 8 * l + 7] = uu[ni - 1 :]
        up[8 * l + 7 : 8 * l + 8] = zero[:1]
        down[8 * l : 8 * l + 3] = tt[:3]
        down[8 * l + 3 : 8 * l + 6] = ss[:3]
        down[8 * l + 6 : 8 * l + 8] = zero[:2]
        x = jnp.where(lane < 8, tt[:, :128], tt[:, nj - 128 :])
        x = jnp.where((lane >= 8) & (lane < 16), pltpu.roll(ss[:, :128], 8, 1), x)
        x = jnp.where((lane >= 112) & (lane < 120), pltpu.roll(ss[:, nj - 128 :], 120, 1), x)
        x = jnp.where((lane >= 104) & (lane < 112), pltpu.roll(vv[:, nj - 128 :], 112, 1), x)
        tile[ni * l : ni * (l + 1)] = x
    em = em / nl
    nm = nm / nl
    part = elev[...] - em - nm
    coupler = 2.0 * jnp.sqrt((wet * flag[...]).astype(jnp.float32) / nl)
    for k, f in enumerate((part, em, nm, coupler)):
        fields[k] = f
    even = lon_even()
    far[...] = jnp.where(even, down[...], up[...])
    close[...] = jnp.where(even, up[...], down[...])
    turned = tile[...].T
    edges[0:16] = turned[0:16]
    edges[16:40] = turned[104:128]
    for k, f in enumerate((part, em, nm, coupler)):
        tile[ni * k : ni * (k + 1)] = jnp.where(lane < 64, f[:, :128], f[:, nj - 128 :])
    columns = tile[...].T
    lat = lat_index()
    none = jnp.zeros((2, 128), jnp.float32)
    t_end, s_end, v_end = turned[125:128], turned[117:120], turned[111:112]
    fold = [jnp.concatenate([turned[k : k + 1] for k in (n, n - 1, n - 2)]) for n in (127, 119)]
    fold = mirror16(jnp.concatenate(fold + [none], axis=0))
    north = jnp.concatenate([t_end, s_end, v_end, none[:1]], axis=0)
    south = jnp.concatenate([turned[0:3], turned[8:11], none], axis=0)
    for p in range(4):
        ahead = p > lat
        slots[p, 0:8] = jnp.where(ahead, north, south)
        slots[p, 8:12] = jnp.where(ahead, columns[124:128], columns[0:4])
        slots[p, 12:15] = fold[0:3] if p < 2 else fold[3:6]
        slots[p, 15:16] = none[:1]
    block = lax.shift_right_logical(jnp.broadcast_to(fc[0:1, 0:1], (8, 128)), 4)
    row = jnp.zeros((8, 128), jnp.int32)
    nz = lax.axis_size("z")
    for k in range(1, lax.axis_size("y") * lax.axis_size("xh")):
        row = row + jnp.where(block >= nz * k, 1, 0)
    source[0] = block - nz * row
    source[1] = row


def widen_kernel(got, fields, far_q, close_q, far, close, beyond, rims, tile, up, down):
    _, ni, nj = fields.shape
    lat = lat_index()
    even = lon_even()
    north = jnp.where(lat < 3, got[jnp.minimum(lat + 1, 3)], 0.0)
    south = jnp.where(lat > 0, got[jnp.maximum(lat - 1, 0)], 0.0)
    rims[0] = north[0:8]
    rims[1] = south[0:8]
    tile[...] = jnp.zeros((128, 128), jnp.float32)
    tile[0:4] = north[8:12]
    tile[124:128] = south[8:12]
    beyond[...] = tile[...].T[0 : 4 * ni].reshape(4, ni, 128)
    far[0:64] = far_q[...]
    close[0:64] = close_q[...]
    at = 0
    for k, n in enumerate((3, 4, 3, 3)):
        up[at : at + n, 0:nj] = fields[k, ni - n : ni]
        up[at : at + n, nj:] = beyond[k, ni - n : ni]
        down[at : at + n, 0:nj] = fields[k, 0:n]
        down[at : at + n, nj:] = beyond[k, 0:n]
        at += n
    up[13:16] = jnp.zeros((3, nj + 128), jnp.float32)
    down[13:16] = jnp.zeros((3, nj + 128), jnp.float32)
    for out, first, second in ((far, down, up), (close, up, down)):
        rows = jnp.where(even, first[...], second[...])
        out[64:80] = rows[:, 0:nj]
        out[80:88, 0:128] = rows[0:8, nj:]
        out[80:88, 128:256] = rows[8:16, nj:]
        out[80:88, 256:384] = jnp.zeros((8, 128), jnp.float32)


def krylov_kernel(got, fields, beyond, far, close, basis_ref, message, wide, west, east):
    _, ni, nj = fields.shape
    even = lon_even()
    for out, first, second in ((west, far, close), (east, close, far)):
        out[:, 0:nj] = jnp.where(even, first[64:80], second[64:80])
        tail = jnp.where(even, first[80:88], second[80:88])
        out[0:8, nj:] = tail[:, 0:128]
        out[8:16, nj:] = tail[:, 128:256]
    blank = jnp.zeros((8, nj + 128), jnp.float32)
    at = 0
    for k, n in enumerate((3, 4, 3, 3)):
        wide[k, 0:8] = blank
        wide[k, 24:32] = blank
        wide[k, 8 - n : 8] = west[at : at + n]
        wide[k, 24 : 24 + n] = east[at : at + n]
        wide[k, 8:24, 0:nj] = fields[k]
        wide[k, 8:24, nj:] = beyond[k]
        at += n
    part, em, nm, cpl = (wide[k] for k in range(4))
    rows, lanes = part.shape
    b0 = part + pltpu.roll(em, 1, 0) + pltpu.roll(nm, 1, 1)

    def scaled(e):
        f = cpl * e
        lap = (
            4.0 * f
            - pltpu.roll(f, 1, 0)
            - pltpu.roll(f, rows - 1, 0)
            - pltpu.roll(f, 1, 1)
            - pltpu.roll(f, lanes - 1, 1)
        )
        return ((1.0 - SHIFT) * e + cpl * lap) * (1.0 / SCALE)

    b1 = scaled(b0)
    b2 = 2.0 * scaled(b1) - b0
    b3 = 2.0 * scaled(b2) - b1
    basis = [b[8 : 8 + ni, :nj] for b in (b0, b1, b2, b3)]
    for k in range(4):
        basis_ref[k] = basis[k]
    row = lax.broadcasted_iota(jnp.int32, (4, 128), 0)
    col = lax.broadcasted_iota(jnp.int32, (4, 128), 1)
    total = jnp.concatenate([got[3, 12:15], jnp.zeros((1, 128), jnp.float32)], axis=0)
    for n, (i, j) in enumerate(PAIRS):
        prod = basis[i] * basis[j]
        prod = prod[:8] + prod[8:]
        acc = prod[:, :128]
        for k in range(1, nj // 128):
            acc = acc + prod[:, 128 * k : 128 * (k + 1)]
        one = jnp.sum(jnp.sum(acc, axis=0, keepdims=True), axis=1, keepdims=True)
        total = jnp.where((row == 3) & (col == n), one, total)
    for k in range(message.shape[0]):
        message[k] = total


def relay_kernel(source, got, message):
    peers = got.shape[0]
    total = got[0]
    for k in range(1, peers):
        total = total + got[k]
    which = source[0, 0:4]
    piece = got[0]
    for z in range(1, peers // 2):
        piece = jnp.where(which == z, got[2 * z], piece)
    row = lax.broadcasted_iota(jnp.int32, (4, 128), 0)
    text = jnp.where(row < 3, piece, total)
    for k in range(message.shape[0]):
        message[k] = text


def finish_kernel(
    basis_ref, source, got, edges, tail, wet, base_t, base_s,
    surface_ref, residual_ref, out_t, out_s, tile, final, sems,
):
    del base_t, base_s
    total = got[0]
    for k in range(1, got.shape[0]):
        total = total + got[k]
    fold = [got[0], got[1]]
    which = source[1, 0:4]
    for k in range(1, got.shape[0] // 2):
        fold = [jnp.where(which == k, got[2 * k + i], fold[i]) for i in range(2)]
    last = jnp.where(lat_index() == 3, 1.0, 0.0)
    rows = [
        jnp.concatenate([edges[35:40], fold[0][0:3]], axis=0),
        jnp.concatenate([edges[27:32], fold[1][0:3]], axis=0),
    ]
    row = lax.broadcasted_iota(jnp.int32, (8, 128), 0)
    speed = jnp.where(row < 3, pltpu.roll(edges[16:24], 3, 0) * last, 0.0)
    pos = speed > 0.0
    nj = surface_ref.shape[1]
    copies = []
    for k, out in enumerate((out_t, out_s)):
        q = [rows[k]] + [pltpu.roll(rows[k], 8 - o, 0) for o in range(1, 6)]
        face = speed * weno_upwind(*[jnp.where(pos, q[i], q[5 - i]) for i in range(5)])
        change = face - jnp.where(row == 0, 0.0, pltpu.roll(face, 1, 0))
        tile[...] = jnp.zeros((128, 128), jnp.float32)
        tile[125:128] = change[0:3]
        final[k] = (tail[k] - tile[...].T.reshape(tail.shape[1:])) * wet[...]
        copy = pltpu.make_async_copy(final.at[k], out.at[:, :, nj - 128 : nj], sems.at[k])
        copy.start()
        copies.append(copy)
    line = total[3:4]
    col = lax.broadcasted_iota(jnp.int32, (1, 128), 1)
    gram = {}
    for n, pair in enumerate(PAIRS):
        gram[pair] = jnp.sum(jnp.where(col == n, line, 0.0), axis=1, keepdims=True)
    xc, rc = coefficients(gram)
    basis = [basis_ref[k] for k in range(4)]
    surface_ref[...] = sum(c * f for c, f in zip(xc, basis) if c is not None)
    residual_ref[...] = sum(c * f for c, f in zip(rc, basis) if c is not None)
    for copy in copies:
        copy.wait()


def near(value):
    return pltpu.with_memory_space_constraint(value, pltpu.VMEM)


def f32(*shape):
    return jax.ShapeDtypeStruct(shape, jnp.float32)


def vmem(*shape):
    return pltpu.VMEM(shape, jnp.float32)


def make_on_device(sizes):
    ny, nxh, nz, nxl, ncore = sizes
    n_lon, n_lat = ny * nxh * nz, nxl * ncore

    def on_device(t, s, u, v, elev, flag, depth, fc):
        nl, ni, nj = t.shape
        lat = lax.axis_index(LAT)
        last = lat == n_lat - 1

        far, close, fields, edges, source, slots = pl.pallas_call(
            pack_kernel,
            out_shape=(
                vmem(64, nj),
                vmem(64, nj),
                vmem(4, ni, nj),
                vmem(40, 128),
                pltpu.VMEM((2, 8, 128), jnp.int32),
                vmem(4, 16, 128),
            ),
            scratch_shapes=[vmem(64, nj), vmem(64, nj), vmem(128, 128)],
            name="pack",
        )(t, s, u, v, elev, flag, depth, fc.reshape(1, ni))
        halo = lax.all_to_all(slots, LAT, 0, 0)
        far, close, beyond, rims = pl.pallas_call(
            widen_kernel,
            out_shape=(vmem(88, nj), vmem(88, nj), vmem(4, ni, 128), vmem(2, 8, 128)),
            scratch_shapes=[vmem(128, 128), vmem(16, nj + 128), vmem(16, nj + 128)],
            name="widen",
        )(near(halo), near(fields), near(far), near(close))

        def swaps(first):
            pairs = []
            for i in range(first, n_lon, 2):
                pairs += [(i, (i + 1) % n_lon), ((i + 1) % n_lon, i)]
            return pairs

        far = lax.ppermute(far, LON, swaps(1))
        close = lax.ppermute(close, LON, swaps(0))
        basis, message = pl.pallas_call(
            krylov_kernel,
            out_shape=(vmem(4, ni, nj), vmem(nz * ncore, 4, 128)),
            scratch_shapes=[vmem(4, 32, nj + 128), vmem(16, nj + 128), vmem(16, nj + 128)],
            name="krylov",
        )(near(halo), near(fields), near(beyond), near(far), near(close))
        got = lax.all_to_all(message, ("z", "core"), 0, 0)
        message = pl.pallas_call(
            relay_kernel, out_shape=vmem(ny * nxh * nxl, 4, 128), name="relay"
        )(near(source), near(got))
        got = lax.all_to_all(message, ("y", "xh", "xl"), 0, 0)
        level = lax.broadcasted_iota(jnp.int32, t.shape, 0)
        mask = jnp.where((flag[None] == 1) & (level < depth[None]), 1.0, 0.0).astype(jnp.float32)
        q = jnp.stack([t * mask, s * mask])
        ue = u * mask
        vn = v * mask

        def sides(msg):
            tiles = msg[: 8 * nl].reshape(nl, 8, nj)
            return jnp.stack([tiles[:, 0:3], tiles[:, 3:6]]), tiles[:, 6:7]

        even = lon_even()
        west = jnp.where(even, far, close)
        east = jnp.where(even, close, far)
        q_west, u_west = sides(west)
        q_east, _ = sides(east)
        north, south = rims[0], rims[1]

        def columns(msg):
            return jnp.transpose(msg[:6].reshape(2, 3, nl, ni), (0, 2, 3, 1))

        q_north, q_south = columns(north), columns(south)
        v_south = south[6].reshape(nl, ni, 1)
        zonal = jnp.concatenate([q_west, q, q_east], axis=2)
        merid = jnp.concatenate([q_south, q, q_north], axis=3)
        speed_x = jnp.concatenate([u_west, ue], axis=1)
        place = lax.broadcasted_iota(jnp.int32, (1, 1, nj + 1), 2)
        speed_y = jnp.concatenate([v_south, vn], axis=2)
        speed_y = jnp.where(last & (place > nj - 3), 0.0, speed_y)
        flux_x = face_flux(zonal, speed_x[None], ni + 1, 2)
        flux_y = face_flux(merid, speed_y[None], nj + 1, 3)
        updated = q - (flux_x[:, :, 1:] - flux_x[:, :, :-1]) - (flux_y[..., 1:] - flux_y[..., :-1])
        updated = updated * mask
        hbm, local = pl.BlockSpec(memory_space=pl.ANY), pl.BlockSpec(memory_space=pltpu.VMEM)
        surface, residual, t_next, s_next = pl.pallas_call(
            finish_kernel,
            in_specs=[local] * 6 + [hbm] * 2,
            out_specs=(local, local, hbm, hbm),
            out_shape=(f32(ni, nj), f32(ni, nj), f32(nl, ni, nj), f32(nl, ni, nj)),
            input_output_aliases={6: 2, 7: 3},
            scratch_shapes=[vmem(128, 128), vmem(2, nl, ni, 128), pltpu.SemaphoreType.DMA((2,))],
            name="finish",
        )(
            near(basis),
            near(source),
            near(got),
            near(edges),
            near(updated[..., nj - 128 :]),
            near(mask[..., nj - 128 :]),
            updated[0],
            updated[1],
        )
        return t_next, s_next, surface, residual

    return on_device


def solution(mesh, sizes=SIZES):
    fine = Mesh(mesh.devices.reshape(sizes), ALL)
    block, plane = P(None, LON, LAT), P(LON, LAT)
    return jax.shard_map(
        make_on_device(sizes),
        mesh=fine,
        in_specs=(block,) * 4 + (plane,) * 3 + (P(LON),),
        out_specs=(block, block, plane, plane),
        check_vma=False,
    )
```

```python
import jax
import jax.numpy as jnp
from jax import lax
from jax.experimental import pallas as pl
from jax.experimental.pallas import tpu as pltpu
from jax.sharding import Mesh, PartitionSpec as P

ITERS = 3
LON = ("y", "xh", "z")
LAT = ("xl", "core")
ALL = LON + LAT
SIZES = (8, 2, 12, 2, 2)
SHIFT = 17.0
SCALE = 16.0
PAIRS = [(i, j) for i in range(4) for j in range(i, 4)]


def weno_upwind(a, b, c, d, e):
    d0, d1, d2, d3 = b - a, c - b, d - c, e - d
    s0, s1, s2 = d1 - d0, d2 - d1, d3 - d2
    t0 = s0 + 2.0 * d1
    t1 = d1 + d2
    t2 = s2 - 2.0 * d2
    k = 13.0 / 12.0
    e0 = 1e-06 + k * s0 * s0 + 0.25 * t0 * t0
    e1 = 1e-06 + k * s1 * s1 + 0.25 * t1 * t1
    e2 = 1e-06 + k * s2 * s2 + 0.25 * t2 * t2
    w0, w1, w2 = e1 * e2, e0 * e2, e0 * e1
    w0, w1, w2 = 0.1 * w0 * w0, 0.6 * w1 * w1, 0.3 * w2 * w2
    top = w0 * (5.0 * d1 - 2.0 * d0) + w1 * (d1 + 2.0 * d2) + w2 * (4.0 * d2 - d3)
    return c + top / (6.0 * (w0 + w1 + w2))


def face_flux(padded, speed, count, axis):
    q = [lax.slice_in_dim(padded, o, o + count, axis=axis) for o in range(6)]
    pos = speed > 0.0
    a, b, c, d, e = (jnp.where(pos, q[i], q[5 - i]) for i in range(5))
    return speed * weno_upwind(a, b, c, d, e)


def coefficients(gram):
    def form(p, q):
        total = 0.0
        for i in range(4):
            for j in range(4):
                if p[i] is not None and q[j] is not None:
                    total = total + p[i] * q[j] * gram[min(i, j), max(i, j)]
        return total

    def add(p, s, q):
        return [
            (p[i] if q[i] is None else (s * q[i] if p[i] is None else p[i] + s * q[i]))
            for i in range(4)
        ]

    def image(p):
        out = [None] * 4

        def put(i, x):
            out[i] = x if out[i] is None else out[i] + x

        for i in range(3):
            if p[i] is None:
                continue
            put(i, SHIFT * p[i])
            if i == 0:
                put(1, SCALE * p[0])
            else:
                put(i + 1, 0.5 * SCALE * p[i])
                put(i - 1, 0.5 * SCALE * p[i])
        return out

    x = [None] * 4
    r = [jnp.ones_like(gram[0, 0]), None, None, None]
    p = list(r)
    norm = form(r, r)
    for it in range(ITERS):
        ap = image(p)
        step = norm / form(p, ap)
        x = add(x, step, p)
        r = add(r, -step, ap)
        if it + 1 < ITERS:
            new = form(r, r)
            p = add(r, new / norm, p)
            norm = new
    return x, r


def lat_index():
    return 2 * lax.axis_index("xl") + lax.axis_index("core")


def mirror16(x):
    lane = lax.broadcasted_iota(jnp.int32, x.shape, 1)
    for bit in (1, 2, 4, 8):
        x = jnp.where((lane & bit) != 0, pltpu.roll(x, bit, 1), pltpu.roll(x, 128 - bit, 1))
    return x


def lon_even():
    return lax.rem(lax.axis_index("z"), 2) == 0


def pack_kernel(
    t, s, u, v, elev, flag, depth, fc, far, close, fields, edges, source, slots_out, slots, tile, sem
):
    nl, ni, nj = t.shape
    ocean = flag[...] == 1
    wet = depth[...]
    lane = lax.broadcasted_iota(jnp.int32, (ni, 128), 1)
    em = jnp.zeros((ni, nj), jnp.float32)
    nm = jnp.zeros((ni, nj), jnp.float32)
    tail = nj - 128
    for l in range(nl):
        m = jnp.where(ocean & (wet > l), 1.0, 0.0)
        em = em + u[l] * m
        vv = v[l] * m
        nm = nm + vv
        first, last = m[:, :128], m[:, tail:]
        x = jnp.where(lane < 8, t[l, :, :128] * first, t[l, :, tail:] * last)
        x = jnp.where((lane >= 8) & (lane < 16), pltpu.roll(s[l, :, :128] * first, 8, 1), x)
        x = jnp.where((lane >= 112) & (lane < 120), pltpu.roll(s[l, :, tail:] * last, 120, 1), x)
        x = jnp.where((lane >= 104) & (lane < 112), pltpu.roll(vv[:, tail:], 112, 1), x)
        tile[ni * l : ni * (l + 1)] = x
    em = em / nl
    nm = nm / nl
    part = elev[...] - em - nm
    coupler = 2.0 * jnp.sqrt((wet * flag[...]).astype(jnp.float32) / nl)
    for k, f in enumerate((part, em, nm, coupler)):
        fields[k] = f
        x = tile[ni * k : ni * (k + 1)]
        x = jnp.where((lane >= 16) & (lane < 20), pltpu.roll(f[:, :128], 16, 1), x)
        x = jnp.where((lane >= 100) & (lane < 104), pltpu.roll(f[:, tail:], 104, 1), x)
        tile[ni * k : ni * (k + 1)] = x
    turned = tile[...].T
    edges[0:16] = turned[0:16]
    edges[16:40] = turned[104:128]
    lat = lat_index()
    none = jnp.zeros((2, 128), jnp.float32)
    t_end, s_end, v_end = turned[125:128], turned[117:120], turned[111:112]
    fold = [jnp.concatenate([turned[k : k + 1] for k in (n, n - 1, n - 2)]) for n in (127, 119)]
    fold = mirror16(jnp.concatenate(fold + [none], axis=0))
    north = jnp.concatenate([t_end, s_end, v_end, none[:1]], axis=0)
    south = jnp.concatenate([turned[0:3], turned[8:11], none], axis=0)
    for p in range(4):
        ahead = p > lat
        slots[p, 0:8] = jnp.where(ahead, north, south)
        slots[p, 8:12] = jnp.where(ahead, turned[100:104], turned[16:20])
        slots[p, 12:15] = fold[0:3] if p < 2 else fold[3:6]
        slots[p, 15:16] = none[:1]
    copy = pltpu.make_async_copy(slots, slots_out, sem)
    copy.start()

    even = lon_even()
    zero = jnp.zeros((2, nj), jnp.float32)
    for l in range(nl):
        m = jnp.where(ocean & (wet > l), 1.0, 0.0)
        tt, ss = t[l] * m, s[l] * m
        east_edge = jnp.concatenate(
            [tt[ni - 3 :], ss[ni - 3 :], u[l, ni - 1 :] * m[ni - 1 :], zero[:1]], axis=0
        )
        west_edge = jnp.concatenate([tt[:3], ss[:3], zero], axis=0)
        far[8 * l : 8 * l + 8] = jnp.where(even, west_edge, east_edge)
        close[8 * l : 8 * l + 8] = jnp.where(even, east_edge, west_edge)
    block = lax.shift_right_logical(jnp.broadcast_to(fc[0:1, 0:1], (8, 128)), 4)
    row = jnp.zeros((8, 128), jnp.int32)
    nz = lax.axis_size("z")
    for k in range(1, lax.axis_size("y") * lax.axis_size("xh")):
        row = row + jnp.where(block >= nz * k, 1, 0)
    source[0] = block - nz * row
    source[1] = row
    copy.wait()


def widen_kernel(got, fields, far_q, close_q, close, far, beyond, rims, tile, up, down):
    _, ni, nj = fields.shape
    lat = lat_index()
    even = lon_even()
    north = jnp.where(lat < 3, got[jnp.minimum(lat + 1, 3)], 0.0)
    south = jnp.where(lat > 0, got[jnp.maximum(lat - 1, 0)], 0.0)
    rims[0] = north[0:8]
    rims[1] = south[0:8]
    tile[...] = jnp.zeros((128, 128), jnp.float32)
    tile[0:4] = north[8:12]
    tile[124:128] = south[8:12]
    beyond[...] = tile[...].T[0 : 4 * ni].reshape(4, ni, 128)
    far[0:64] = far_q[...]
    close[0:64] = close_q[...]
    at = 0
    for k, n in enumerate((3, 4, 3, 3)):
        up[at : at + n, 0:nj] = fields[k, ni - n : ni]
        up[at : at + n, nj:] = beyond[k, ni - n : ni]
        down[at : at + n, 0:nj] = fields[k, 0:n]
        down[at : at + n, nj:] = beyond[k, 0:n]
        at += n
    up[13:16] = jnp.zeros((3, nj + 128), jnp.float32)
    down[13:16] = jnp.zeros((3, nj + 128), jnp.float32)
    for out, first, second in ((far, down, up), (close, up, down)):
        rows = jnp.where(even, first[...], second[...])
        out[64:80] = rows[:, 0:nj]
        out[80:88, 0:128] = rows[0:8, nj:]
        out[80:88, 128:256] = rows[8:16, nj:]
        out[80:88, 256:384] = jnp.zeros((8, 128), jnp.float32)


def krylov_kernel(got, fields, beyond, close, far, basis_ref, message, wide, west, east):
    _, ni, nj = fields.shape
    even = lon_even()
    for out, first, second in ((west, far, close), (east, close, far)):
        out[:, 0:nj] = jnp.where(even, first[64:80], second[64:80])
        tail = jnp.where(even, first[80:88], second[80:88])
        out[0:8, nj:] = tail[:, 0:128]
        out[8:16, nj:] = tail[:, 128:256]
    blank = jnp.zeros((8, nj + 128), jnp.float32)
    at = 0
    for k, n in enumerate((3, 4, 3, 3)):
        wide[k, 0:8] = blank
        wide[k, 24:32] = blank
        wide[k, 8 - n : 8] = west[at : at + n]
        wide[k, 24 : 24 + n] = east[at : at + n]
        wide[k, 8:24, 0:nj] = fields[k]
        wide[k, 8:24, nj:] = beyond[k]
        at += n
    part, em, nm, cpl = (wide[k] for k in range(4))
    rows, lanes = part.shape
    b0 = part + pltpu.roll(em, 1, 0) + pltpu.roll(nm, 1, 1)

    def scaled(e):
        f = cpl * e
        lap = (
            4.0 * f
            - pltpu.roll(f, 1, 0)
            - pltpu.roll(f, rows - 1, 0)
            - pltpu.roll(f, 1, 1)
            - pltpu.roll(f, lanes - 1, 1)
        )
        return ((1.0 - SHIFT) * e + cpl * lap) * (1.0 / SCALE)

    b1 = scaled(b0)
    b2 = 2.0 * scaled(b1) - b0
    b3 = 2.0 * scaled(b2) - b1
    basis = [b[8 : 8 + ni, :nj] for b in (b0, b1, b2, b3)]
    for k in range(4):
        basis_ref[k] = basis[k]
    row = lax.broadcasted_iota(jnp.int32, (4, 128), 0)
    col = lax.broadcasted_iota(jnp.int32, (4, 128), 1)
    total = jnp.concatenate([got[3, 12:15], jnp.zeros((1, 128), jnp.float32)], axis=0)
    for n, (i, j) in enumerate(PAIRS):
        prod = basis[i] * basis[j]
        prod = prod[:8] + prod[8:]
        acc = prod[:, :128]
        for k in range(1, nj // 128):
            acc = acc + prod[:, 128 * k : 128 * (k + 1)]
        one = jnp.sum(jnp.sum(acc, axis=0, keepdims=True), axis=1, keepdims=True)
        total = jnp.where((row == 3) & (col == n), one, total)
    for k in range(message.shape[0]):
        message[k] = total


def relay_kernel(source, got, message):
    peers = got.shape[0]
    total = got[0]
    for k in range(1, peers):
        total = total + got[k]
    which = source[0, 0:4]
    piece = got[0]
    for z in range(1, peers // 2):
        piece = jnp.where(which == z, got[2 * z], piece)
    row = lax.broadcasted_iota(jnp.int32, (4, 128), 0)
    text = jnp.where(row < 3, piece, total)
    for k in range(message.shape[0]):
        message[k] = text


def finish_kernel(
    basis_ref, source, got, edges, tail, wet, base_t, base_s,
    surface_out, residual_out, out_t, out_s, surface, residual, tile, final, sems,
):
    del base_t, base_s
    total = got[0]
    for k in range(1, got.shape[0]):
        total = total + got[k]
    fold = [got[0], got[1]]
    which = source[1, 0:4]
    for k in range(1, got.shape[0] // 2):
        fold = [jnp.where(which == k, got[2 * k + i], fold[i]) for i in range(2)]
    last = jnp.where(lat_index() == 3, 1.0, 0.0)
    rows = [
        jnp.concatenate([edges[35:40], fold[0][0:3]], axis=0),
        jnp.concatenate([edges[27:32], fold[1][0:3]], axis=0),
    ]
    row = lax.broadcasted_iota(jnp.int32, (8, 128), 0)
    speed = jnp.where(row < 3, pltpu.roll(edges[16:24], 3, 0) * last, 0.0)
    pos = speed > 0.0
    nj = surface.shape[1]
    for k in range(2):
        q = [rows[k]] + [pltpu.roll(rows[k], 8 - o, 0) for o in range(1, 6)]
        face = speed * weno_upwind(*[jnp.where(pos, q[i], q[5 - i]) for i in range(5)])
        change = face - jnp.where(row == 0, 0.0, pltpu.roll(face, 1, 0))
        tile[k] = jnp.zeros((128, 128), jnp.float32)
        tile[k, 125:128] = change[0:3]
        final[k] = (tail[k] - tile[k].T.reshape(tail.shape[1:])) * wet[...]
    line = total[3:4]
    col = lax.broadcasted_iota(jnp.int32, (1, 128), 1)
    gram = {}
    for n, pair in enumerate(PAIRS):
        gram[pair] = jnp.sum(jnp.where(col == n, line, 0.0), axis=1, keepdims=True)
    xc, rc = coefficients(gram)
    basis = [basis_ref[k] for k in range(4)]
    surface[...] = sum(c * f for c, f in zip(xc, basis) if c is not None)
    residual[...] = sum(c * f for c, f in zip(rc, basis) if c is not None)
    copies = [
        pltpu.make_async_copy(final.at[0], out_t.at[:, :, nj - 128 : nj], sems.at[0]),
        pltpu.make_async_copy(final.at[1], out_s.at[:, :, nj - 128 : nj], sems.at[1]),
        pltpu.make_async_copy(surface, surface_out, sems.at[2]),
        pltpu.make_async_copy(residual, residual_out, sems.at[3]),
    ]
    for copy in copies:
        copy.start()
    for copy in copies:
        copy.wait()


def near(value):
    return pltpu.with_memory_space_constraint(value, pltpu.VMEM)


def f32(*shape):
    return jax.ShapeDtypeStruct(shape, jnp.float32)


def vmem(*shape):
    return pltpu.VMEM(shape, jnp.float32)


def make_on_device(sizes):
    ny, nxh, nz, nxl, ncore = sizes
    n_lon, n_lat = ny * nxh * nz, nxl * ncore

    def on_device(t, s, u, v, elev, flag, depth, fc):
        nl, ni, nj = t.shape
        lat = lax.axis_index(LAT)
        last = lat == n_lat - 1
        hbm, local = pl.BlockSpec(memory_space=pl.ANY), pl.BlockSpec(memory_space=pltpu.VMEM)

        far, close, fields, edges, source, slots = pl.pallas_call(
            pack_kernel,
            out_shape=(
                vmem(64, nj),
                vmem(64, nj),
                vmem(4, ni, nj),
                vmem(40, 128),
                pltpu.VMEM((2, 8, 128), jnp.int32),
                f32(4, 16, 128),
            ),
            in_specs=[local] * 8,
            out_specs=(local,) * 5 + (hbm,),
            scratch_shapes=[vmem(4, 16, 128), vmem(128, 128), pltpu.SemaphoreType.DMA],
            name="pack",
        )(t, s, u, v, elev, flag, depth, fc.reshape(1, ni))
        halo = lax.all_to_all(slots, LAT, 0, 0)
        close, far, beyond, rims = pl.pallas_call(
            widen_kernel,
            out_shape=(vmem(88, nj), vmem(88, nj), vmem(4, ni, 128), vmem(2, 8, 128)),
            scratch_shapes=[vmem(128, 128), vmem(16, nj + 128), vmem(16, nj + 128)],
            name="widen",
        )(near(halo), near(fields), near(far), near(close))

        def swaps(first):
            pairs = []
            for i in range(first, n_lon, 2):
                pairs += [(i, (i + 1) % n_lon), ((i + 1) % n_lon, i)]
            return pairs

        close = lax.ppermute(close, LON, swaps(0))
        far = lax.ppermute(far, LON, swaps(1))
        basis, message = pl.pallas_call(
            krylov_kernel,
            out_shape=(vmem(4, ni, nj), vmem(nz * ncore, 4, 128)),
            scratch_shapes=[vmem(4, 32, nj + 128), vmem(16, nj + 128), vmem(16, nj + 128)],
            name="krylov",
        )(near(halo), near(fields), near(beyond), near(close), near(far))
        got = lax.all_to_all(message, ("z", "core"), 0, 0)
        message = pl.pallas_call(
            relay_kernel, out_shape=vmem(ny * nxh * nxl, 4, 128), name="relay"
        )(near(source), near(got))
        got = lax.all_to_all(message, ("y", "xh", "xl"), 0, 0)
        level = lax.broadcasted_iota(jnp.int32, t.shape, 0)
        mask = jnp.where((flag[None] == 1) & (level < depth[None]), 1.0, 0.0).astype(jnp.float32)
        q = jnp.stack([t * mask, s * mask])
        ue = u * mask
        vn = v * mask

        def sides(msg):
            tiles = msg[: 8 * nl].reshape(nl, 8, nj)
            return jnp.stack([tiles[:, 0:3], tiles[:, 3:6]]), tiles[:, 6:7]

        even = lon_even()
        west = jnp.where(even, far, close)
        east = jnp.where(even, close, far)
        q_west, u_west = sides(west)
        q_east, _ = sides(east)
        north, south = rims[0], rims[1]

        def columns(msg):
            return jnp.transpose(msg[:6].reshape(2, 3, nl, ni), (0, 2, 3, 1))

        q_north, q_south = columns(north), columns(south)
        v_south = south[6].reshape(nl, ni, 1)
        zonal = jnp.concatenate([q_west, q, q_east], axis=2)
        merid = jnp.concatenate([q_south, q, q_north], axis=3)
        speed_x = jnp.concatenate([u_west, ue], axis=1)
        place = lax.broadcasted_iota(jnp.int32, (1, 1, nj + 1), 2)
        speed_y = jnp.concatenate([v_south, vn], axis=2)
        speed_y = jnp.where(last & (place > nj - 3), 0.0, speed_y)
        flux_x = face_flux(zonal, speed_x[None], ni + 1, 2)
        flux_y = face_flux(merid, speed_y[None], nj + 1, 3)
        updated = q - (flux_x[:, :, 1:] - flux_x[:, :, :-1]) - (flux_y[..., 1:] - flux_y[..., :-1])
        updated = updated * mask
        surface, residual, t_next, s_next = pl.pallas_call(
            finish_kernel,
            in_specs=[local] * 6 + [hbm] * 2,
            out_specs=(hbm,) * 4,
            out_shape=(f32(ni, nj), f32(ni, nj), f32(nl, ni, nj), f32(nl, ni, nj)),
            input_output_aliases={6: 2, 7: 3},
            scratch_shapes=[
                vmem(ni, nj),
                vmem(ni, nj),
                vmem(2, 128, 128),
                vmem(2, nl, ni, 128),
                pltpu.SemaphoreType.DMA((4,)),
            ],
            name="finish",
        )(
            near(basis),
            near(source),
            near(got),
            near(edges),
            near(updated[..., nj - 128 :]),
            near(mask[..., nj - 128 :]),
            updated[0],
            updated[1],
        )
        return t_next, s_next, surface, residual

    return on_device


def solution(mesh, sizes=SIZES):
    fine = Mesh(mesh.devices.reshape(sizes), ALL)
    block, plane = P(None, LON, LAT), P(LON, LAT)
    return jax.shard_map(
        make_on_device(sizes),
        mesh=fine,
        in_specs=(block,) * 4 + (plane,) * 3 + (P(LON),),
        out_specs=(block, block, plane, plane),
        check_vma=False,
    )
```

```python
import jax
import jax.numpy as jnp
from jax import lax
from jax.experimental import pallas as pl
from jax.experimental.pallas import tpu as pltpu
from jax.sharding import Mesh, PartitionSpec as P

ITERS = 3
LON = ("y", "xh", "z")
LAT = ("xl", "core")
ALL = LON + LAT
SIZES = (8, 2, 12, 2, 2)
SHIFT = 17.0
SCALE = 16.0
PAIRS = [(i, j) for i in range(4) for j in range(i, 4)]


def weno_upwind(a, b, c, d, e):
    d0, d1, d2, d3 = b - a, c - b, d - c, e - d
    s0, s1, s2 = d1 - d0, d2 - d1, d3 - d2
    t0 = s0 + 2.0 * d1
    t1 = d1 + d2
    t2 = s2 - 2.0 * d2
    k = 13.0 / 12.0
    e0 = 1e-06 + k * s0 * s0 + 0.25 * t0 * t0
    e1 = 1e-06 + k * s1 * s1 + 0.25 * t1 * t1
    e2 = 1e-06 + k * s2 * s2 + 0.25 * t2 * t2
    w0, w1, w2 = e1 * e2, e0 * e2, e0 * e1
    w0, w1, w2 = 0.1 * w0 * w0, 0.6 * w1 * w1, 0.3 * w2 * w2
    top = w0 * (5.0 * d1 - 2.0 * d0) + w1 * (d1 + 2.0 * d2) + w2 * (4.0 * d2 - d3)
    return c + top / (6.0 * (w0 + w1 + w2))


def face_flux(padded, speed, count, axis):
    q = [lax.slice_in_dim(padded, o, o + count, axis=axis) for o in range(6)]
    pos = speed > 0.0
    a, b, c, d, e = (jnp.where(pos, q[i], q[5 - i]) for i in range(5))
    return speed * weno_upwind(a, b, c, d, e)


def coefficients(gram):
    def form(p, q):
        total = 0.0
        for i in range(4):
            for j in range(4):
                if p[i] is not None and q[j] is not None:
                    total = total + p[i] * q[j] * gram[min(i, j), max(i, j)]
        return total

    def add(p, s, q):
        return [
            (p[i] if q[i] is None else (s * q[i] if p[i] is None else p[i] + s * q[i]))
            for i in range(4)
        ]

    def image(p):
        out = [None] * 4

        def put(i, x):
            out[i] = x if out[i] is None else out[i] + x

        for i in range(3):
            if p[i] is None:
                continue
            put(i, SHIFT * p[i])
            if i == 0:
                put(1, SCALE * p[0])
            else:
                put(i + 1, 0.5 * SCALE * p[i])
                put(i - 1, 0.5 * SCALE * p[i])
        return out

    x = [None] * 4
    r = [jnp.ones_like(gram[0, 0]), None, None, None]
    p = list(r)
    norm = form(r, r)
    for it in range(ITERS):
        ap = image(p)
        step = norm / form(p, ap)
        x = add(x, step, p)
        r = add(r, -step, ap)
        if it + 1 < ITERS:
            new = form(r, r)
            p = add(r, new / norm, p)
            norm = new
    return x, r


def lat_index():
    return 2 * lax.axis_index("xl") + lax.axis_index("core")


def mirror16(x):
    lane = lax.broadcasted_iota(jnp.int32, x.shape, 1)
    for bit in (1, 2, 4, 8):
        x = jnp.where((lane & bit) != 0, pltpu.roll(x, bit, 1), pltpu.roll(x, 128 - bit, 1))
    return x


def lon_even():
    return lax.rem(lax.axis_index("z"), 2) == 0


def pack_kernel(
    t, s, u, v, elev, flag, depth, fc, far, close, fields, edges, source, slots_out, slots, tile, sem
):
    nl, ni, nj = t.shape
    ocean = flag[...] == 1
    wet = depth[...]
    lane = lax.broadcasted_iota(jnp.int32, (ni, 128), 1)
    em = jnp.zeros((ni, nj), jnp.float32)
    nm = jnp.zeros((ni, nj), jnp.float32)
    tail = nj - 128
    for l in range(nl):
        m = jnp.where(ocean & (wet > l), 1.0, 0.0)
        em = em + u[l] * m
        vv = v[l] * m
        nm = nm + vv
        first, last = m[:, :128], m[:, tail:]
        x = jnp.where(lane < 8, t[l, :, :128] * first, t[l, :, tail:] * last)
        x = jnp.where((lane >= 8) & (lane < 16), pltpu.roll(s[l, :, :128] * first, 8, 1), x)
        x = jnp.where((lane >= 112) & (lane < 120), pltpu.roll(s[l, :, tail:] * last, 120, 1), x)
        x = jnp.where((lane >= 104) & (lane < 112), pltpu.roll(vv[:, tail:], 112, 1), x)
        tile[ni * l : ni * (l + 1)] = x
    em = em / nl
    nm = nm / nl
    part = elev[...] - em - nm
    coupler = 2.0 * jnp.sqrt((wet * flag[...]).astype(jnp.float32) / nl)
    for k, f in enumerate((part, em, nm, coupler)):
        fields[k] = f
        x = tile[ni * k : ni * (k + 1)]
        x = jnp.where((lane >= 16) & (lane < 20), pltpu.roll(f[:, :128], 16, 1), x)
        x = jnp.where((lane >= 100) & (lane < 104), pltpu.roll(f[:, tail:], 104, 1), x)
        tile[ni * k : ni * (k + 1)] = x
    turned = tile[...].T
    edges[0:16] = turned[0:16]
    edges[16:40] = turned[104:128]
    lat = lat_index()
    none = jnp.zeros((2, 128), jnp.float32)
    t_end, s_end, v_end = turned[125:128], turned[117:120], turned[111:112]
    fold = [jnp.concatenate([turned[k : k + 1] for k in (n, n - 1, n - 2)]) for n in (127, 119)]
    fold = mirror16(jnp.concatenate(fold + [none], axis=0))
    north = jnp.concatenate([t_end, s_end, v_end, none[:1]], axis=0)
    south = jnp.concatenate([turned[0:3], turned[8:11], none], axis=0)
    for p in range(4):
        ahead = p > lat
        slots[p, 0:8] = jnp.where(ahead, north, south)
        slots[p, 8:12] = jnp.where(ahead, turned[100:104], turned[16:20])
        slots[p, 12:15] = fold[0:3] if p < 2 else fold[3:6]
        slots[p, 15:16] = none[:1]
    copy = pltpu.make_async_copy(slots, slots_out, sem)
    copy.start()

    even = lon_even()
    zero = jnp.zeros((2, nj), jnp.float32)
    for l in range(nl):
        m = jnp.where(ocean & (wet > l), 1.0, 0.0)
        tt, ss = t[l] * m, s[l] * m
        east_edge = jnp.concatenate(
            [tt[ni - 3 :], ss[ni - 3 :], u[l, ni - 1 :] * m[ni - 1 :], zero[:1]], axis=0
        )
        west_edge = jnp.concatenate([tt[:3], ss[:3], zero], axis=0)
        far[8 * l : 8 * l + 8] = jnp.where(even, west_edge, east_edge)
        close[8 * l : 8 * l + 8] = jnp.where(even, east_edge, west_edge)
    block = lax.shift_right_logical(jnp.broadcast_to(fc[0:1, 0:1], (8, 128)), 4)
    row = jnp.zeros((8, 128), jnp.int32)
    nz = lax.axis_size("z")
    for k in range(1, lax.axis_size("y") * lax.axis_size("xh")):
        row = row + jnp.where(block >= nz * k, 1, 0)
    source[0] = block - nz * row
    source[1] = row
    copy.wait()


def widen_kernel(got, fields, far_q, close_q, far, close, beyond, rims, tile, up, down):
    _, ni, nj = fields.shape
    lat = lat_index()
    even = lon_even()
    north = jnp.where(lat < 3, got[jnp.minimum(lat + 1, 3)], 0.0)
    south = jnp.where(lat > 0, got[jnp.maximum(lat - 1, 0)], 0.0)
    rims[0] = north[0:8]
    rims[1] = south[0:8]
    tile[...] = jnp.zeros((128, 128), jnp.float32)
    tile[0:4] = north[8:12]
    tile[124:128] = south[8:12]
    beyond[...] = tile[...].T[0 : 4 * ni].reshape(4, ni, 128)
    far[0:64] = far_q[...]
    close[0:64] = close_q[...]
    at = 0
    for k, n in enumerate((3, 4, 3, 3)):
        up[at : at + n, 0:nj] = fields[k, ni - n : ni]
        up[at : at + n, nj:] = beyond[k, ni - n : ni]
        down[at : at + n, 0:nj] = fields[k, 0:n]
        down[at : at + n, nj:] = beyond[k, 0:n]
        at += n
    up[13:16] = jnp.zeros((3, nj + 128), jnp.float32)
    down[13:16] = jnp.zeros((3, nj + 128), jnp.float32)
    for out, first, second in ((far, down, up), (close, up, down)):
        rows = jnp.where(even, first[...], second[...])
        out[64:80] = rows[:, 0:nj]
        out[80:88, 0:128] = rows[0:8, nj:]
        out[80:88, 128:256] = rows[8:16, nj:]
        out[80:88, 256:384] = jnp.zeros((8, 128), jnp.float32)


def krylov_kernel(got, fields, beyond, far, close, basis_ref, message, wide, west, east):
    _, ni, nj = fields.shape
    even = lon_even()
    for out, first, second in ((west, far, close), (east, close, far)):
        out[:, 0:nj] = jnp.where(even, first[64:80], second[64:80])
        tail = jnp.where(even, first[80:88], second[80:88])
        out[0:8, nj:] = tail[:, 0:128]
        out[8:16, nj:] = tail[:, 128:256]
    blank = jnp.zeros((8, nj + 128), jnp.float32)
    at = 0
    for k, n in enumerate((3, 4, 3, 3)):
        wide[k, 0:8] = blank
        wide[k, 24:32] = blank
        wide[k, 8 - n : 8] = west[at : at + n]
        wide[k, 24 : 24 + n] = east[at : at + n]
        wide[k, 8:24, 0:nj] = fields[k]
        wide[k, 8:24, nj:] = beyond[k]
        at += n
    part, em, nm, cpl = (wide[k] for k in range(4))
    rows, lanes = part.shape
    b0 = part + pltpu.roll(em, 1, 0) + pltpu.roll(nm, 1, 1)

    def scaled(e):
        f = cpl * e
        lap = (
            4.0 * f
            - pltpu.roll(f, 1, 0)
            - pltpu.roll(f, rows - 1, 0)
            - pltpu.roll(f, 1, 1)
            - pltpu.roll(f, lanes - 1, 1)
        )
        return ((1.0 - SHIFT) * e + cpl * lap) * (1.0 / SCALE)

    b1 = scaled(b0)
    b2 = 2.0 * scaled(b1) - b0
    b3 = 2.0 * scaled(b2) - b1
    basis = [b[8 : 8 + ni, :nj] for b in (b0, b1, b2, b3)]
    for k in range(4):
        basis_ref[k] = basis[k]
    row = lax.broadcasted_iota(jnp.int32, (4, 128), 0)
    col = lax.broadcasted_iota(jnp.int32, (4, 128), 1)
    total = jnp.concatenate([got[3, 12:15], jnp.zeros((1, 128), jnp.float32)], axis=0)
    for n, (i, j) in enumerate(PAIRS):
        prod = basis[i] * basis[j]
        prod = prod[:8] + prod[8:]
        acc = prod[:, :128]
        for k in range(1, nj // 128):
            acc = acc + prod[:, 128 * k : 128 * (k + 1)]
        one = jnp.sum(jnp.sum(acc, axis=0, keepdims=True), axis=1, keepdims=True)
        total = jnp.where((row == 3) & (col == n), one, total)
    for k in range(message.shape[0]):
        message[k] = total


def relay_kernel(source, got, message):
    peers = got.shape[0]
    total = got[0]
    for k in range(1, peers):
        total = total + got[k]
    which = source[0, 0:4]
    piece = got[0]
    for z in range(1, peers // 2):
        piece = jnp.where(which == z, got[2 * z], piece)
    row = lax.broadcasted_iota(jnp.int32, (4, 128), 0)
    text = jnp.where(row < 3, piece, total)
    for k in range(message.shape[0]):
        message[k] = text


def finish_kernel(
    basis_ref, source, got, edges, tail, wet, base_t, base_s,
    surface_out, residual_out, out_t, out_s, surface, residual, tile, final, sems,
):
    del base_t, base_s
    total = got[0]
    for k in range(1, got.shape[0]):
        total = total + got[k]
    fold = [got[0], got[1]]
    which = source[1, 0:4]
    for k in range(1, got.shape[0] // 2):
        fold = [jnp.where(which == k, got[2 * k + i], fold[i]) for i in range(2)]
    last = jnp.where(lat_index() == 3, 1.0, 0.0)
    rows = [
        jnp.concatenate([edges[35:40], fold[0][0:3]], axis=0),
        jnp.concatenate([edges[27:32], fold[1][0:3]], axis=0),
    ]
    row = lax.broadcasted_iota(jnp.int32, (8, 128), 0)
    speed = jnp.where(row < 3, pltpu.roll(edges[16:24], 3, 0) * last, 0.0)
    pos = speed > 0.0
    nj = surface.shape[1]
    for k in range(2):
        q = [rows[k]] + [pltpu.roll(rows[k], 8 - o, 0) for o in range(1, 6)]
        face = speed * weno_upwind(*[jnp.where(pos, q[i], q[5 - i]) for i in range(5)])
        change = face - jnp.where(row == 0, 0.0, pltpu.roll(face, 1, 0))
        tile[k] = jnp.zeros((128, 128), jnp.float32)
        tile[k, 125:128] = change[0:3]
        final[k] = (tail[k] - tile[k].T.reshape(tail.shape[1:])) * wet[...]
    line = total[3:4]
    col = lax.broadcasted_iota(jnp.int32, (1, 128), 1)
    gram = {}
    for n, pair in enumerate(PAIRS):
        gram[pair] = jnp.sum(jnp.where(col == n, line, 0.0), axis=1, keepdims=True)
    xc, rc = coefficients(gram)
    basis = [basis_ref[k] for k in range(4)]
    surface[...] = sum(c * f for c, f in zip(xc, basis) if c is not None)
    residual[...] = sum(c * f for c, f in zip(rc, basis) if c is not None)
    copies = [
        pltpu.make_async_copy(final.at[0], out_t.at[:, :, nj - 128 : nj], sems.at[0]),
        pltpu.make_async_copy(final.at[1], out_s.at[:, :, nj - 128 : nj], sems.at[1]),
        pltpu.make_async_copy(surface, surface_out, sems.at[2]),
        pltpu.make_async_copy(residual, residual_out, sems.at[3]),
    ]
    for copy in copies:
        copy.start()
    for copy in copies:
        copy.wait()


def near(value):
    return pltpu.with_memory_space_constraint(value, pltpu.VMEM)


def f32(*shape):
    return jax.ShapeDtypeStruct(shape, jnp.float32)


def vmem(*shape):
    return pltpu.VMEM(shape, jnp.float32)


def make_on_device(sizes):
    ny, nxh, nz, nxl, ncore = sizes
    n_lon, n_lat = ny * nxh * nz, nxl * ncore

    def on_device(t, s, u, v, elev, flag, depth, fc):
        nl, ni, nj = t.shape
        lat = lax.axis_index(LAT)
        last = lat == n_lat - 1
        hbm, local = pl.BlockSpec(memory_space=pl.ANY), pl.BlockSpec(memory_space=pltpu.VMEM)

        far, close, fields, edges, source, slots = pl.pallas_call(
            pack_kernel,
            out_shape=(
                vmem(64, nj),
                vmem(64, nj),
                vmem(4, ni, nj),
                vmem(40, 128),
                pltpu.VMEM((2, 8, 128), jnp.int32),
                f32(4, 16, 128),
            ),
            in_specs=[local] * 8,
            out_specs=(local,) * 5 + (hbm,),
            scratch_shapes=[vmem(4, 16, 128), vmem(128, 128), pltpu.SemaphoreType.DMA],
            name="pack",
        )(t, s, u, v, elev, flag, depth, fc.reshape(1, ni))
        halo = lax.all_to_all(slots, LAT, 0, 0)
        far, close, beyond, rims = pl.pallas_call(
            widen_kernel,
            out_shape=(vmem(88, nj), vmem(88, nj), vmem(4, ni, 128), vmem(2, 8, 128)),
            scratch_shapes=[vmem(128, 128), vmem(16, nj + 128), vmem(16, nj + 128)],
            name="widen",
        )(near(halo), near(fields), near(far), near(close))

        def swaps(first):
            pairs = []
            for i in range(first, n_lon, 2):
                pairs += [(i, (i + 1) % n_lon), ((i + 1) % n_lon, i)]
            return pairs

        close = lax.ppermute(close, LON, swaps(0))
        far = lax.ppermute(far, LON, swaps(1))
        basis, message = pl.pallas_call(
            krylov_kernel,
            out_shape=(vmem(4, ni, nj), vmem(nz * ncore, 4, 128)),
            scratch_shapes=[vmem(4, 32, nj + 128), vmem(16, nj + 128), vmem(16, nj + 128)],
            name="krylov",
        )(near(halo), near(fields), near(beyond), near(far), near(close))
        got = lax.all_to_all(message, ("z", "core"), 0, 0)
        message = pl.pallas_call(
            relay_kernel, out_shape=vmem(ny * nxh * nxl, 4, 128), name="relay"
        )(near(source), near(got))
        got = lax.all_to_all(message, ("y", "xh", "xl"), 0, 0)
        level = lax.broadcasted_iota(jnp.int32, t.shape, 0)
        mask = jnp.where((flag[None] == 1) & (level < depth[None]), 1.0, 0.0).astype(jnp.float32)
        q = jnp.stack([t * mask, s * mask])
        ue = u * mask
        vn = v * mask

        def sides(msg):
            tiles = msg[: 8 * nl].reshape(nl, 8, nj)
            return jnp.stack([tiles[:, 0:3], tiles[:, 3:6]]), tiles[:, 6:7]

        even = lon_even()
        west = jnp.where(even, far, close)
        east = jnp.where(even, close, far)
        q_west, u_west = sides(west)
        q_east, _ = sides(east)
        north, south = rims[0], rims[1]

        def columns(msg):
            return jnp.transpose(msg[:6].reshape(2, 3, nl, ni), (0, 2, 3, 1))

        q_north, q_south = columns(north), columns(south)
        v_south = south[6].reshape(nl, ni, 1)
        zonal = jnp.concatenate([q_west, q, q_east], axis=2)
        merid = jnp.concatenate([q_south, q, q_north], axis=3)
        speed_x = jnp.concatenate([u_west, ue], axis=1)
        place = lax.broadcasted_iota(jnp.int32, (1, 1, nj + 1), 2)
        speed_y = jnp.concatenate([v_south, vn], axis=2)
        speed_y = jnp.where(last & (place > nj - 3), 0.0, speed_y)
        flux_x = face_flux(zonal, speed_x[None], ni + 1, 2)
        flux_y = face_flux(merid, speed_y[None], nj + 1, 3)
        updated = q - (flux_x[:, :, 1:] - flux_x[:, :, :-1]) - (flux_y[..., 1:] - flux_y[..., :-1])
        updated = updated * mask
        surface, residual, t_next, s_next = pl.pallas_call(
            finish_kernel,
            in_specs=[local] * 6 + [hbm] * 2,
            out_specs=(hbm,) * 4,
            out_shape=(f32(ni, nj), f32(ni, nj), f32(nl, ni, nj), f32(nl, ni, nj)),
            input_output_aliases={6: 2, 7: 3},
            scratch_shapes=[
                vmem(ni, nj),
                vmem(ni, nj),
                vmem(2, 128, 128),
                vmem(2, nl, ni, 128),
                pltpu.SemaphoreType.DMA((4,)),
            ],
            name="finish",
        )(
            near(basis),
            near(source),
            near(got),
            near(edges),
            near(updated[..., nj - 128 :]),
            near(mask[..., nj - 128 :]),
            updated[0],
            updated[1],
        )
        return t_next, s_next, surface, residual

    return on_device


def solution(mesh, sizes=SIZES):
    fine = Mesh(mesh.devices.reshape(sizes), ALL)
    block, plane = P(None, LON, LAT), P(LON, LAT)
    return jax.shard_map(
        make_on_device(sizes),
        mesh=fine,
        in_specs=(block,) * 4 + (plane,) * 3 + (P(LON),),
        out_specs=(block, block, plane, plane),
        check_vma=False,
    )
```

```python
import jax
import jax.numpy as jnp
from jax import lax
from jax.experimental import pallas as pl
from jax.experimental.pallas import tpu as pltpu
from jax.sharding import Mesh, PartitionSpec as P

ITERS = 3
LON = ("y", "xh", "z")
LAT = ("xl", "core")
ALL = LON + LAT
SIZES = (8, 2, 12, 2, 2)
SHIFT = 17.0
SCALE = 16.0
PAIRS = [(i, j) for i in range(4) for j in range(i, 4)]


def weno_upwind(a, b, c, d, e):
    d0, d1, d2, d3 = b - a, c - b, d - c, e - d
    s0, s1, s2 = d1 - d0, d2 - d1, d3 - d2
    t0 = s0 + 2.0 * d1
    t1 = d1 + d2
    t2 = s2 - 2.0 * d2
    k = 13.0 / 12.0
    e0 = 1e-06 + k * s0 * s0 + 0.25 * t0 * t0
    e1 = 1e-06 + k * s1 * s1 + 0.25 * t1 * t1
    e2 = 1e-06 + k * s2 * s2 + 0.25 * t2 * t2
    w0, w1, w2 = e1 * e2, e0 * e2, e0 * e1
    w0, w1, w2 = 0.1 * w0 * w0, 0.6 * w1 * w1, 0.3 * w2 * w2
    top = w0 * (5.0 * d1 - 2.0 * d0) + w1 * (d1 + 2.0 * d2) + w2 * (4.0 * d2 - d3)
    return c + top / (6.0 * (w0 + w1 + w2))


def face_flux(padded, speed, count, axis):
    q = [lax.slice_in_dim(padded, o, o + count, axis=axis) for o in range(6)]
    pos = speed > 0.0
    a, b, c, d, e = (jnp.where(pos, q[i], q[5 - i]) for i in range(5))
    return speed * weno_upwind(a, b, c, d, e)


def coefficients(gram):
    def form(p, q):
        total = 0.0
        for i in range(4):
            for j in range(4):
                if p[i] is not None and q[j] is not None:
                    total = total + p[i] * q[j] * gram[min(i, j), max(i, j)]
        return total

    def add(p, s, q):
        return [
            (p[i] if q[i] is None else (s * q[i] if p[i] is None else p[i] + s * q[i]))
            for i in range(4)
        ]

    def image(p):
        out = [None] * 4

        def put(i, x):
            out[i] = x if out[i] is None else out[i] + x

        for i in range(3):
            if p[i] is None:
                continue
            put(i, SHIFT * p[i])
            if i == 0:
                put(1, SCALE * p[0])
            else:
                put(i + 1, 0.5 * SCALE * p[i])
                put(i - 1, 0.5 * SCALE * p[i])
        return out

    x = [None] * 4
    r = [jnp.ones_like(gram[0, 0]), None, None, None]
    p = list(r)
    norm = form(r, r)
    for it in range(ITERS):
        ap = image(p)
        step = norm / form(p, ap)
        x = add(x, step, p)
        r = add(r, -step, ap)
        if it + 1 < ITERS:
            new = form(r, r)
            p = add(r, new / norm, p)
            norm = new
    return x, r


def lat_index():
    return 2 * lax.axis_index("xl") + lax.axis_index("core")


def mirror16(x):
    lane = lax.broadcasted_iota(jnp.int32, x.shape, 1)
    for bit in (1, 2, 4, 8):
        x = jnp.where((lane & bit) != 0, pltpu.roll(x, bit, 1), pltpu.roll(x, 128 - bit, 1))
    return x


def lon_even():
    return lax.rem(lax.axis_index("z"), 2) == 0


def pack_kernel(
    t, s, u, v, elev, flag, depth, fc,
    far, close, fields, edges, source, fold_ref, chip_swap, core_swap, tile,
):
    nl, ni, nj = t.shape
    ocean = flag[...] == 1
    wet = depth[...]
    lane = lax.broadcasted_iota(jnp.int32, (ni, 128), 1)
    em = jnp.zeros((ni, nj), jnp.float32)
    nm = jnp.zeros((ni, nj), jnp.float32)
    tail = nj - 128
    for l in range(nl):
        m = jnp.where(ocean & (wet > l), 1.0, 0.0)
        em = em + u[l] * m
        vv = v[l] * m
        nm = nm + vv
        first, last = m[:, :128], m[:, tail:]
        x = jnp.where(lane < 8, t[l, :, :128] * first, t[l, :, tail:] * last)
        x = jnp.where((lane >= 8) & (lane < 16), pltpu.roll(s[l, :, :128] * first, 8, 1), x)
        x = jnp.where((lane >= 112) & (lane < 120), pltpu.roll(s[l, :, tail:] * last, 120, 1), x)
        x = jnp.where((lane >= 104) & (lane < 112), pltpu.roll(vv[:, tail:], 112, 1), x)
        tile[ni * l : ni * (l + 1)] = x
    em = em / nl
    nm = nm / nl
    part = elev[...] - em - nm
    coupler = 2.0 * jnp.sqrt((wet * flag[...]).astype(jnp.float32) / nl)
    for k, f in enumerate((part, em, nm, coupler)):
        fields[k] = f
        x = tile[ni * k : ni * (k + 1)]
        x = jnp.where((lane >= 16) & (lane < 20), pltpu.roll(f[:, :128], 16, 1), x)
        x = jnp.where((lane >= 100) & (lane < 104), pltpu.roll(f[:, tail:], 104, 1), x)
        tile[ni * k : ni * (k + 1)] = x
    turned = tile[...].T
    edges[0:16] = turned[0:16]
    edges[16:40] = turned[104:128]
    lat = lat_index()
    none = jnp.zeros((2, 128), jnp.float32)
    t_end, s_end, v_end = turned[125:128], turned[117:120], turned[111:112]
    fold = [jnp.concatenate([turned[k : k + 1] for k in (n, n - 1, n - 2)]) for n in (127, 119)]
    fold = mirror16(jnp.concatenate(fold + [none], axis=0))
    north = jnp.concatenate([t_end, s_end, v_end, none[:1]], axis=0)
    south = jnp.concatenate([turned[0:3], turned[8:11], none], axis=0)
    fold_ref[...] = fold
    ahead = lax.rem(lat, 2) == 0
    core_swap[0:8] = jnp.where(ahead, north, south)
    core_swap[8:12] = jnp.where(ahead, turned[100:104], turned[16:20])
    core_swap[12:15] = fold[0:3]
    core_swap[15:16] = none[:1]
    ahead = lat == 1
    chip_swap[0:8] = jnp.where(ahead, north, south)
    chip_swap[8:12] = jnp.where(ahead, turned[100:104], turned[16:20])
    chip_swap[12:14] = none
    chip_swap[14:16] = none

    even = lon_even()
    zero = jnp.zeros((2, nj), jnp.float32)
    for l in range(nl):
        m = jnp.where(ocean & (wet > l), 1.0, 0.0)
        tt, ss = t[l] * m, s[l] * m
        east_edge = jnp.concatenate(
            [tt[ni - 3 :], ss[ni - 3 :], u[l, ni - 1 :] * m[ni - 1 :], zero[:1]], axis=0
        )
        west_edge = jnp.concatenate([tt[:3], ss[:3], zero], axis=0)
        far[8 * l : 8 * l + 8] = jnp.where(even, west_edge, east_edge)
        close[8 * l : 8 * l + 8] = jnp.where(even, east_edge, west_edge)
    block = lax.shift_right_logical(jnp.broadcast_to(fc[0:1, 0:1], (8, 128)), 4)
    nz = lax.axis_size("z")
    columns = lax.axis_size("y") * lax.axis_size("xh")
    column = lax.axis_index("y") * lax.axis_size("xh") + lax.axis_index("xh")
    place = lax.axis_index("z")

    def column_of(x):
        count = jnp.zeros((8, 128), jnp.int32)
        for k in range(1, columns):
            count = count + jnp.where(x >= nz * k, 1, 0)
        return count

    total = block + (nz * column + place)
    total = jnp.where(total >= nz * columns, total - nz * columns, total)
    ahead = total - nz * column_of(total) - place
    ahead = jnp.where(ahead < 0, ahead + nz, ahead)
    origin = total - (nz * column + ahead)
    origin = jnp.where(origin < 0, origin + nz * columns, origin)
    source[0] = column_of(origin)
    source[1] = block - nz * column_of(block)


def widen_kernel(chip_got, core_got, fields, far_q, close_q, far, close, beyond, rims, tile, up, down):
    _, ni, nj = fields.shape
    lat = lat_index()
    even = lon_even()
    odd = lax.rem(lat, 2) == 1
    north = jnp.where(lat < 3, jnp.where(odd, chip_got[...], core_got[...]), 0.0)
    south = jnp.where(lat > 0, jnp.where(odd, core_got[...], chip_got[...]), 0.0)
    rims[0] = north[0:8]
    rims[1] = south[0:8]
    tile[...] = jnp.zeros((128, 128), jnp.float32)
    tile[0:4] = north[8:12]
    tile[124:128] = south[8:12]
    beyond[...] = tile[...].T[0 : 4 * ni].reshape(4, ni, 128)
    far[0:64] = far_q[...]
    close[0:64] = close_q[...]
    at = 0
    for k, n in enumerate((3, 4, 3, 3)):
        up[at : at + n, 0:nj] = fields[k, ni - n : ni]
        up[at : at + n, nj:] = beyond[k, ni - n : ni]
        down[at : at + n, 0:nj] = fields[k, 0:n]
        down[at : at + n, nj:] = beyond[k, 0:n]
        at += n
    up[13:16] = jnp.zeros((3, nj + 128), jnp.float32)
    down[13:16] = jnp.zeros((3, nj + 128), jnp.float32)
    for out, first, second in ((far, down, up), (close, up, down)):
        rows = jnp.where(even, first[...], second[...])
        out[64:80] = rows[:, 0:nj]
        out[80:88, 0:128] = rows[0:8, nj:]
        out[80:88, 128:256] = rows[8:16, nj:]
        out[80:88, 256:384] = jnp.zeros((8, 128), jnp.float32)


def krylov_kernel(core_got, fold, fields, beyond, far, close, basis_ref, message, wide, west, east):
    _, ni, nj = fields.shape
    even = lon_even()
    for out, first, second in ((west, far, close), (east, close, far)):
        out[:, 0:nj] = jnp.where(even, first[64:80], second[64:80])
        tail = jnp.where(even, first[80:88], second[80:88])
        out[0:8, nj:] = tail[:, 0:128]
        out[8:16, nj:] = tail[:, 128:256]
    blank = jnp.zeros((8, nj + 128), jnp.float32)
    at = 0
    for k, n in enumerate((3, 4, 3, 3)):
        wide[k, 0:8] = blank
        wide[k, 24:32] = blank
        wide[k, 8 - n : 8] = west[at : at + n]
        wide[k, 24 : 24 + n] = east[at : at + n]
        wide[k, 8:24, 0:nj] = fields[k]
        wide[k, 8:24, nj:] = beyond[k]
        at += n
    part, em, nm, cpl = (wide[k] for k in range(4))
    rows, lanes = part.shape
    b0 = part + pltpu.roll(em, 1, 0) + pltpu.roll(nm, 1, 1)

    def scaled(e):
        f = cpl * e
        lap = (
            4.0 * f
            - pltpu.roll(f, 1, 0)
            - pltpu.roll(f, rows - 1, 0)
            - pltpu.roll(f, 1, 1)
            - pltpu.roll(f, lanes - 1, 1)
        )
        return ((1.0 - SHIFT) * e + cpl * lap) * (1.0 / SCALE)

    b1 = scaled(b0)
    b2 = 2.0 * scaled(b1) - b0
    b3 = 2.0 * scaled(b2) - b1
    basis = [b[8 : 8 + ni, :nj] for b in (b0, b1, b2, b3)]
    for k in range(4):
        basis_ref[k] = basis[k]
    row = lax.broadcasted_iota(jnp.int32, (4, 128), 0)
    col = lax.broadcasted_iota(jnp.int32, (4, 128), 1)
    piece = jnp.where(lat_index() == 3, fold[3:6], core_got[12:15])
    total = jnp.concatenate([piece, jnp.zeros((1, 128), jnp.float32)], axis=0)
    for n, (i, j) in enumerate(PAIRS):
        prod = basis[i] * basis[j]
        prod = prod[:8] + prod[8:]
        acc = prod[:, :128]
        for k in range(1, nj // 128):
            acc = acc + prod[:, 128 * k : 128 * (k + 1)]
        one = jnp.sum(jnp.sum(acc, axis=0, keepdims=True), axis=1, keepdims=True)
        total = jnp.where((row == 3) & (col == n), one, total)
    for k in range(message.shape[0]):
        message[k] = total


def relay_kernel(source, got, message):
    peers = got.shape[0]
    total = got[0]
    for k in range(1, peers):
        total = total + got[k]
    which = source[0, 0:4]
    piece = got[1]
    for k in range(1, peers // 2):
        piece = jnp.where(which == k, got[2 * k + 1], piece)
    row = lax.broadcasted_iota(jnp.int32, (4, 128), 0)
    text = jnp.where(row < 3, piece, total)
    for k in range(message.shape[0]):
        message[k] = text


def finish_kernel(
    basis_ref, source, got, edges, tail, wet, base_t, base_s,
    surface_out, residual_out, out_t, out_s, surface, residual, tile, final, sems,
):
    del base_t, base_s
    total = got[0]
    for k in range(1, got.shape[0]):
        total = total + got[k]
    fold = [got[0], got[1]]
    which = source[1, 0:4]
    for k in range(1, got.shape[0] // 2):
        fold = [jnp.where(which == k, got[2 * k + i], fold[i]) for i in range(2)]
    last = jnp.where(lat_index() == 3, 1.0, 0.0)
    rows = [
        jnp.concatenate([edges[35:40], fold[0][0:3]], axis=0),
        jnp.concatenate([edges[27:32], fold[1][0:3]], axis=0),
    ]
    row = lax.broadcasted_iota(jnp.int32, (8, 128), 0)
    speed = jnp.where(row < 3, pltpu.roll(edges[16:24], 3, 0) * last, 0.0)
    pos = speed > 0.0
    nj = surface.shape[1]
    for k in range(2):
        q = [rows[k]] + [pltpu.roll(rows[k], 8 - o, 0) for o in range(1, 6)]
        face = speed * weno_upwind(*[jnp.where(pos, q[i], q[5 - i]) for i in range(5)])
        change = face - jnp.where(row == 0, 0.0, pltpu.roll(face, 1, 0))
        tile[k] = jnp.zeros((128, 128), jnp.float32)
        tile[k, 125:128] = change[0:3]
        final[k] = (tail[k] - tile[k].T.reshape(tail.shape[1:])) * wet[...]
    line = total[3:4]
    col = lax.broadcasted_iota(jnp.int32, (1, 128), 1)
    gram = {}
    for n, pair in enumerate(PAIRS):
        gram[pair] = jnp.sum(jnp.where(col == n, line, 0.0), axis=1, keepdims=True)
    xc, rc = coefficients(gram)
    basis = [basis_ref[k] for k in range(4)]
    surface[...] = sum(c * f for c, f in zip(xc, basis) if c is not None)
    residual[...] = sum(c * f for c, f in zip(rc, basis) if c is not None)
    copies = [
        pltpu.make_async_copy(final.at[0], out_t.at[:, :, nj - 128 : nj], sems.at[0]),
        pltpu.make_async_copy(final.at[1], out_s.at[:, :, nj - 128 : nj], sems.at[1]),
        pltpu.make_async_copy(surface, surface_out, sems.at[2]),
        pltpu.make_async_copy(residual, residual_out, sems.at[3]),
    ]
    for copy in copies:
        copy.start()
    for copy in copies:
        copy.wait()


def near(value):
    return pltpu.with_memory_space_constraint(value, pltpu.VMEM)


def f32(*shape):
    return jax.ShapeDtypeStruct(shape, jnp.float32)


def vmem(*shape):
    return pltpu.VMEM(shape, jnp.float32)


def make_on_device(sizes):
    ny, nxh, nz, nxl, ncore = sizes
    n_lon, n_lat = ny * nxh * nz, nxl * ncore

    def on_device(t, s, u, v, elev, flag, depth, fc):
        nl, ni, nj = t.shape
        lat = lax.axis_index(LAT)
        last = lat == n_lat - 1
        hbm, local = pl.BlockSpec(memory_space=pl.ANY), pl.BlockSpec(memory_space=pltpu.VMEM)

        far, close, fields, edges, source, fold, chip_swap, core_swap = pl.pallas_call(
            pack_kernel,
            out_shape=(
                vmem(64, nj),
                vmem(64, nj),
                vmem(4, ni, nj),
                vmem(40, 128),
                pltpu.VMEM((2, 8, 128), jnp.int32),
                vmem(8, 128),
                vmem(16, 128),
                vmem(16, 128),
            ),
            scratch_shapes=[vmem(128, 128)],
            name="pack",
        )(t, s, u, v, elev, flag, depth, fc.reshape(1, ni))
        chip_got = lax.ppermute(chip_swap, LAT, [(1, 2), (2, 1)])
        core_got = lax.ppermute(core_swap, LAT, [(0, 1), (1, 0), (2, 3), (3, 2)])
        far, close, beyond, rims = pl.pallas_call(
            widen_kernel,
            out_shape=(vmem(88, nj), vmem(88, nj), vmem(4, ni, 128), vmem(2, 8, 128)),
            scratch_shapes=[vmem(128, 128), vmem(16, nj + 128), vmem(16, nj + 128)],
            name="widen",
        )(near(chip_got), near(core_got), near(fields), near(far), near(close))

        def swaps(first):
            pairs = []
            for i in range(first, n_lon, 2):
                pairs += [(i, (i + 1) % n_lon), ((i + 1) % n_lon, i)]
            return pairs

        close = lax.ppermute(close, LON, swaps(0))
        far = lax.ppermute(far, LON, swaps(1))
        basis, message = pl.pallas_call(
            krylov_kernel,
            out_shape=(vmem(4, ni, nj), vmem(ny * nxh * nxl, 4, 128)),
            scratch_shapes=[vmem(4, 32, nj + 128), vmem(16, nj + 128), vmem(16, nj + 128)],
            name="krylov",
        )(near(core_got), near(fold), near(fields), near(beyond), near(far), near(close))
        got = lax.all_to_all(message, ("y", "xh", "xl"), 0, 0)
        message = pl.pallas_call(
            relay_kernel, out_shape=vmem(nz * ncore, 4, 128), name="relay"
        )(near(source), near(got))
        got = lax.all_to_all(message, ("z", "core"), 0, 0)
        level = lax.broadcasted_iota(jnp.int32, t.shape, 0)
        mask = jnp.where((flag[None] == 1) & (level < depth[None]), 1.0, 0.0).astype(jnp.float32)
        q = jnp.stack([t * mask, s * mask])
        ue = u * mask
        vn = v * mask

        def sides(msg):
            tiles = msg[: 8 * nl].reshape(nl, 8, nj)
            return jnp.stack([tiles[:, 0:3], tiles[:, 3:6]]), tiles[:, 6:7]

        even = lon_even()
        west = jnp.where(even, far, close)
        east = jnp.where(even, close, far)
        q_west, u_west = sides(west)
        q_east, _ = sides(east)
        north, south = rims[0], rims[1]

        def columns(msg):
            return jnp.transpose(msg[:6].reshape(2, 3, nl, ni), (0, 2, 3, 1))

        q_north, q_south = columns(north), columns(south)
        v_south = south[6].reshape(nl, ni, 1)
        zonal = jnp.concatenate([q_west, q, q_east], axis=2)
        merid = jnp.concatenate([q_south, q, q_north], axis=3)
        speed_x = jnp.concatenate([u_west, ue], axis=1)
        place = lax.broadcasted_iota(jnp.int32, (1, 1, nj + 1), 2)
        speed_y = jnp.concatenate([v_south, vn], axis=2)
        speed_y = jnp.where(last & (place > nj - 3), 0.0, speed_y)
        flux_x = face_flux(zonal, speed_x[None], ni + 1, 2)
        flux_y = face_flux(merid, speed_y[None], nj + 1, 3)
        updated = q - (flux_x[:, :, 1:] - flux_x[:, :, :-1]) - (flux_y[..., 1:] - flux_y[..., :-1])
        updated = updated * mask
        surface, residual, t_next, s_next = pl.pallas_call(
            finish_kernel,
            in_specs=[local] * 6 + [hbm] * 2,
            out_specs=(hbm,) * 4,
            out_shape=(f32(ni, nj), f32(ni, nj), f32(nl, ni, nj), f32(nl, ni, nj)),
            input_output_aliases={6: 2, 7: 3},
            scratch_shapes=[
                vmem(ni, nj),
                vmem(ni, nj),
                vmem(2, 128, 128),
                vmem(2, nl, ni, 128),
                pltpu.SemaphoreType.DMA((4,)),
            ],
            name="finish",
        )(
            near(basis),
            near(source),
            near(got),
            near(edges),
            near(updated[..., nj - 128 :]),
            near(mask[..., nj - 128 :]),
            updated[0],
            updated[1],
        )
        return t_next, s_next, surface, residual

    return on_device


def solution(mesh, sizes=SIZES):
    fine = Mesh(mesh.devices.reshape(sizes), ALL)
    block, plane = P(None, LON, LAT), P(LON, LAT)
    return jax.shard_map(
        make_on_device(sizes),
        mesh=fine,
        in_specs=(block,) * 4 + (plane,) * 3 + (P(LON),),
        out_specs=(block, block, plane, plane),
        check_vma=False,
    )
```

```python
import jax
import jax.numpy as jnp
from jax import lax
from jax.experimental import pallas as pl
from jax.experimental.pallas import tpu as pltpu
from jax.sharding import Mesh, PartitionSpec as P

ITERS = 3
LON = ("y", "xh", "z")
LAT = ("xl", "core")
ALL = LON + LAT
SIZES = (8, 2, 12, 2, 2)
SHIFT = 17.0
SCALE = 16.0
PAIRS = [(i, j) for i in range(4) for j in range(i, 4)]


def weno_upwind(a, b, c, d, e):
    d0, d1, d2, d3 = b - a, c - b, d - c, e - d
    s0, s1, s2 = d1 - d0, d2 - d1, d3 - d2
    t0 = s0 + 2.0 * d1
    t1 = d1 + d2
    t2 = s2 - 2.0 * d2
    k = 13.0 / 12.0
    e0 = 1e-06 + k * s0 * s0 + 0.25 * t0 * t0
    e1 = 1e-06 + k * s1 * s1 + 0.25 * t1 * t1
    e2 = 1e-06 + k * s2 * s2 + 0.25 * t2 * t2
    w0, w1, w2 = e1 * e2, e0 * e2, e0 * e1
    w0, w1, w2 = 0.1 * w0 * w0, 0.6 * w1 * w1, 0.3 * w2 * w2
    top = w0 * (5.0 * d1 - 2.0 * d0) + w1 * (d1 + 2.0 * d2) + w2 * (4.0 * d2 - d3)
    return c + top / (6.0 * (w0 + w1 + w2))


def face_flux(padded, speed, count, axis):
    q = [lax.slice_in_dim(padded, o, o + count, axis=axis) for o in range(6)]
    pos = speed > 0.0
    a, b, c, d, e = (jnp.where(pos, q[i], q[5 - i]) for i in range(5))
    return speed * weno_upwind(a, b, c, d, e)


def coefficients(gram):
    def form(p, q):
        total = 0.0
        for i in range(4):
            for j in range(4):
                if p[i] is not None and q[j] is not None:
                    total = total + p[i] * q[j] * gram[min(i, j), max(i, j)]
        return total

    def add(p, s, q):
        return [
            (p[i] if q[i] is None else (s * q[i] if p[i] is None else p[i] + s * q[i]))
            for i in range(4)
        ]

    def image(p):
        out = [None] * 4

        def put(i, x):
            out[i] = x if out[i] is None else out[i] + x

        for i in range(3):
            if p[i] is None:
                continue
            put(i, SHIFT * p[i])
            if i == 0:
                put(1, SCALE * p[0])
            else:
                put(i + 1, 0.5 * SCALE * p[i])
                put(i - 1, 0.5 * SCALE * p[i])
        return out

    x = [None] * 4
    r = [jnp.ones_like(gram[0, 0]), None, None, None]
    p = list(r)
    norm = form(r, r)
    for it in range(ITERS):
        ap = image(p)
        step = norm / form(p, ap)
        x = add(x, step, p)
        r = add(r, -step, ap)
        if it + 1 < ITERS:
            new = form(r, r)
            p = add(r, new / norm, p)
            norm = new
    return x, r


def lat_index():
    return 2 * lax.axis_index("xl") + lax.axis_index("core")


def mirror16(x):
    lane = lax.broadcasted_iota(jnp.int32, x.shape, 1)
    for bit in (1, 2, 4, 8):
        x = jnp.where((lane & bit) != 0, pltpu.roll(x, bit, 1), pltpu.roll(x, 128 - bit, 1))
    return x


def lon_even():
    return lax.rem(lax.axis_index("z"), 2) == 0


def pack_kernel(
    t, s, u, v, elev, flag, depth, fc,
    far, close, fields, edges, source, fold_ref, chip_swap, core_swap, tile,
):
    nl, ni, nj = t.shape
    ocean = flag[...] == 1
    wet = depth[...]
    lane = lax.broadcasted_iota(jnp.int32, (ni, 128), 1)
    em = jnp.zeros((ni, nj), jnp.float32)
    nm = jnp.zeros((ni, nj), jnp.float32)
    tail = nj - 128
    for l in range(nl):
        m = jnp.where(ocean & (wet > l), 1.0, 0.0)
        em = em + u[l] * m
        vv = v[l] * m
        nm = nm + vv
        first, last = m[:, :128], m[:, tail:]
        x = jnp.where(lane < 8, t[l, :, :128] * first, t[l, :, tail:] * last)
        x = jnp.where((lane >= 8) & (lane < 16), pltpu.roll(s[l, :, :128] * first, 8, 1), x)
        x = jnp.where((lane >= 112) & (lane < 120), pltpu.roll(s[l, :, tail:] * last, 120, 1), x)
        x = jnp.where((lane >= 104) & (lane < 112), pltpu.roll(vv[:, tail:], 112, 1), x)
        tile[ni * l : ni * (l + 1)] = x
    em = em / nl
    nm = nm / nl
    part = elev[...] - em - nm
    coupler = 2.0 * jnp.sqrt((wet * flag[...]).astype(jnp.float32) / nl)
    for k, f in enumerate((part, em, nm, coupler)):
        fields[k] = f
        x = tile[ni * k : ni * (k + 1)]
        x = jnp.where((lane >= 16) & (lane < 20), pltpu.roll(f[:, :128], 16, 1), x)
        x = jnp.where((lane >= 100) & (lane < 104), pltpu.roll(f[:, tail:], 104, 1), x)
        tile[ni * k : ni * (k + 1)] = x
    turned = tile[...].T
    edges[0:16] = turned[0:16]
    edges[16:40] = turned[104:128]
    lat = lat_index()
    none = jnp.zeros((2, 128), jnp.float32)
    t_end, s_end, v_end = turned[125:128], turned[117:120], turned[111:112]
    fold = [jnp.concatenate([turned[k : k + 1] for k in (n, n - 1, n - 2)]) for n in (127, 119)]
    fold = mirror16(jnp.concatenate(fold + [none], axis=0))
    north = jnp.concatenate([t_end, s_end, v_end, none[:1]], axis=0)
    south = jnp.concatenate([turned[0:3], turned[8:11], none], axis=0)
    fold_ref[...] = fold
    ahead = lax.rem(lat, 2) == 0
    core_swap[0:8] = jnp.where(ahead, north, south)
    core_swap[8:12] = jnp.where(ahead, turned[100:104], turned[16:20])
    core_swap[12:15] = fold[0:3]
    core_swap[15:16] = none[:1]
    ahead = lat == 1
    chip_swap[0:8] = jnp.where(ahead, north, south)
    chip_swap[8:12] = jnp.where(ahead, turned[100:104], turned[16:20])
    chip_swap[12:14] = none
    chip_swap[14:16] = none

    even = lon_even()
    zero = jnp.zeros((2, nj), jnp.float32)
    for l in range(nl):
        m = jnp.where(ocean & (wet > l), 1.0, 0.0)
        tt, ss = t[l] * m, s[l] * m
        east_edge = jnp.concatenate(
            [tt[ni - 3 :], ss[ni - 3 :], u[l, ni - 1 :] * m[ni - 1 :], zero[:1]], axis=0
        )
        west_edge = jnp.concatenate([tt[:3], ss[:3], zero], axis=0)
        far[8 * l : 8 * l + 8] = jnp.where(even, west_edge, east_edge)
        close[8 * l : 8 * l + 8] = jnp.where(even, east_edge, west_edge)
    block = lax.shift_right_logical(jnp.broadcast_to(fc[0:1, 0:1], (8, 128)), 4)
    nz = lax.axis_size("z")
    columns = lax.axis_size("y") * lax.axis_size("xh")
    column = lax.axis_index("y") * lax.axis_size("xh") + lax.axis_index("xh")
    place = lax.axis_index("z")

    def column_of(x):
        count = jnp.zeros((8, 128), jnp.int32)
        for k in range(1, columns):
            count = count + jnp.where(x >= nz * k, 1, 0)
        return count

    total = block + (nz * column + place)
    total = jnp.where(total >= nz * columns, total - nz * columns, total)
    ahead = total - nz * column_of(total) - place
    ahead = jnp.where(ahead < 0, ahead + nz, ahead)
    origin = total - (nz * column + ahead)
    origin = jnp.where(origin < 0, origin + nz * columns, origin)
    source[0] = column_of(origin)
    source[1] = block - nz * column_of(block)


def widen_kernel(
    chip_got, core_got, fold, fields, far_q, close_q, far, close, beyond, rims, piece, tile, up, down
):
    _, ni, nj = fields.shape
    lat = lat_index()
    even = lon_even()
    odd = lax.rem(lat, 2) == 1
    north = jnp.where(lat < 3, jnp.where(odd, chip_got[...], core_got[...]), 0.0)
    south = jnp.where(lat > 0, jnp.where(odd, core_got[...], chip_got[...]), 0.0)
    piece[0:3] = jnp.where(lat == 3, fold[3:6], core_got[12:15])
    piece[3:8] = jnp.zeros((5, 128), jnp.float32)
    rims[0] = north[0:8]
    rims[1] = south[0:8]
    tile[...] = jnp.zeros((128, 128), jnp.float32)
    tile[0:4] = north[8:12]
    tile[124:128] = south[8:12]
    beyond[...] = tile[...].T[0 : 4 * ni].reshape(4, ni, 128)
    far[0:64] = far_q[...]
    close[0:64] = close_q[...]
    at = 0
    for k, n in enumerate((3, 4, 3, 3)):
        up[at : at + n, 0:nj] = fields[k, ni - n : ni]
        up[at : at + n, nj:] = beyond[k, ni - n : ni]
        down[at : at + n, 0:nj] = fields[k, 0:n]
        down[at : at + n, nj:] = beyond[k, 0:n]
        at += n
    up[13:16] = jnp.zeros((3, nj + 128), jnp.float32)
    down[13:16] = jnp.zeros((3, nj + 128), jnp.float32)
    for out, first, second in ((far, down, up), (close, up, down)):
        rows = jnp.where(even, first[...], second[...])
        out[64:80] = rows[:, 0:nj]
        out[80:88, 0:128] = rows[0:8, nj:]
        out[80:88, 128:256] = rows[8:16, nj:]
        out[80:88, 256:384] = jnp.zeros((8, 128), jnp.float32)


def krylov_kernel(piece, fields, beyond, far, close, basis_ref, message, wide, west, east):
    _, ni, nj = fields.shape
    even = lon_even()
    for out, first, second in ((west, far, close), (east, close, far)):
        out[:, 0:nj] = jnp.where(even, first[64:80], second[64:80])
        tail = jnp.where(even, first[80:88], second[80:88])
        out[0:8, nj:] = tail[:, 0:128]
        out[8:16, nj:] = tail[:, 128:256]
    blank = jnp.zeros((8, nj + 128), jnp.float32)
    at = 0
    for k, n in enumerate((3, 4, 3, 3)):
        wide[k, 0:8] = blank
        wide[k, 24:32] = blank
        wide[k, 8 - n : 8] = west[at : at + n]
        wide[k, 24 : 24 + n] = east[at : at + n]
        wide[k, 8:24, 0:nj] = fields[k]
        wide[k, 8:24, nj:] = beyond[k]
        at += n
    part, em, nm, cpl = (wide[k] for k in range(4))
    rows, lanes = part.shape
    b0 = part + pltpu.roll(em, 1, 0) + pltpu.roll(nm, 1, 1)

    def scaled(e):
        f = cpl * e
        lap = (
            4.0 * f
            - pltpu.roll(f, 1, 0)
            - pltpu.roll(f, rows - 1, 0)
            - pltpu.roll(f, 1, 1)
            - pltpu.roll(f, lanes - 1, 1)
        )
        return ((1.0 - SHIFT) * e + cpl * lap) * (1.0 / SCALE)

    b1 = scaled(b0)
    b2 = 2.0 * scaled(b1) - b0
    b3 = 2.0 * scaled(b2) - b1
    basis = [b[8 : 8 + ni, :nj] for b in (b0, b1, b2, b3)]
    for k in range(4):
        basis_ref[k] = basis[k]
    row = lax.broadcasted_iota(jnp.int32, (4, 128), 0)
    col = lax.broadcasted_iota(jnp.int32, (4, 128), 1)
    total = piece[0:4]
    for n, (i, j) in enumerate(PAIRS):
        prod = basis[i] * basis[j]
        prod = prod[:8] + prod[8:]
        acc = prod[:, :128]
        for k in range(1, nj // 128):
            acc = acc + prod[:, 128 * k : 128 * (k + 1)]
        one = jnp.sum(jnp.sum(acc, axis=0, keepdims=True), axis=1, keepdims=True)
        total = jnp.where((row == 3) & (col == n), one, total)
    for k in range(message.shape[0]):
        message[k] = total


def relay_kernel(source, got, message):
    peers = got.shape[0]
    total = got[0]
    for k in range(1, peers):
        total = total + got[k]
    which = source[0, 0:4]
    piece = got[1]
    for k in range(1, peers // 2):
        piece = jnp.where(which == k, got[2 * k + 1], piece)
    row = lax.broadcasted_iota(jnp.int32, (4, 128), 0)
    text = jnp.where(row < 3, piece, total)
    for k in range(message.shape[0]):
        message[k] = text


def finish_kernel(
    basis_ref, source, got, edges, tail, wet, base_t, base_s,
    surface_out, residual_out, out_t, out_s, surface, residual, tile, final, sems,
):
    del base_t, base_s
    total = got[0]
    for k in range(1, got.shape[0]):
        total = total + got[k]
    fold = [got[0], got[1]]
    which = source[1, 0:4]
    for k in range(1, got.shape[0] // 2):
        fold = [jnp.where(which == k, got[2 * k + i], fold[i]) for i in range(2)]
    last = jnp.where(lat_index() == 3, 1.0, 0.0)
    rows = [
        jnp.concatenate([edges[35:40], fold[0][0:3]], axis=0),
        jnp.concatenate([edges[27:32], fold[1][0:3]], axis=0),
    ]
    row = lax.broadcasted_iota(jnp.int32, (8, 128), 0)
    speed = jnp.where(row < 3, pltpu.roll(edges[16:24], 3, 0) * last, 0.0)
    pos = speed > 0.0
    nj = surface.shape[1]
    for k in range(2):
        q = [rows[k]] + [pltpu.roll(rows[k], 8 - o, 0) for o in range(1, 6)]
        face = speed * weno_upwind(*[jnp.where(pos, q[i], q[5 - i]) for i in range(5)])
        change = face - jnp.where(row == 0, 0.0, pltpu.roll(face, 1, 0))
        tile[k] = jnp.zeros((128, 128), jnp.float32)
        tile[k, 125:128] = change[0:3]
        final[k] = (tail[k] - tile[k].T.reshape(tail.shape[1:])) * wet[...]
    line = total[3:4]
    col = lax.broadcasted_iota(jnp.int32, (1, 128), 1)
    gram = {}
    for n, pair in enumerate(PAIRS):
        gram[pair] = jnp.sum(jnp.where(col == n, line, 0.0), axis=1, keepdims=True)
    xc, rc = coefficients(gram)
    basis = [basis_ref[k] for k in range(4)]
    surface[...] = sum(c * f for c, f in zip(xc, basis) if c is not None)
    residual[...] = sum(c * f for c, f in zip(rc, basis) if c is not None)
    copies = [
        pltpu.make_async_copy(final.at[0], out_t.at[:, :, nj - 128 : nj], sems.at[0]),
        pltpu.make_async_copy(final.at[1], out_s.at[:, :, nj - 128 : nj], sems.at[1]),
        pltpu.make_async_copy(surface, surface_out, sems.at[2]),
        pltpu.make_async_copy(residual, residual_out, sems.at[3]),
    ]
    for copy in copies:
        copy.start()
    for copy in copies:
        copy.wait()


def near(value):
    return pltpu.with_memory_space_constraint(value, pltpu.VMEM)


def f32(*shape):
    return jax.ShapeDtypeStruct(shape, jnp.float32)


def vmem(*shape):
    return pltpu.VMEM(shape, jnp.float32)


def make_on_device(sizes):
    ny, nxh, nz, nxl, ncore = sizes
    n_lon, n_lat = ny * nxh * nz, nxl * ncore

    def on_device(t, s, u, v, elev, flag, depth, fc):
        nl, ni, nj = t.shape
        lat = lax.axis_index(LAT)
        last = lat == n_lat - 1
        hbm, local = pl.BlockSpec(memory_space=pl.ANY), pl.BlockSpec(memory_space=pltpu.VMEM)

        far, close, fields, edges, source, fold, chip_swap, core_swap = pl.pallas_call(
            pack_kernel,
            out_shape=(
                vmem(64, nj),
                vmem(64, nj),
                vmem(4, ni, nj),
                vmem(40, 128),
                pltpu.VMEM((2, 8, 128), jnp.int32),
                vmem(8, 128),
                vmem(16, 128),
                vmem(16, 128),
            ),
            scratch_shapes=[vmem(128, 128)],
            name="pack",
        )(t, s, u, v, elev, flag, depth, fc.reshape(1, ni))
        chip_got = lax.ppermute(chip_swap, LAT, [(1, 2), (2, 1)])
        core_got = lax.ppermute(core_swap, LAT, [(0, 1), (1, 0), (2, 3), (3, 2)])
        far, close, beyond, rims, piece = pl.pallas_call(
            widen_kernel,
            out_shape=(vmem(88, nj), vmem(88, nj), vmem(4, ni, 128), vmem(2, 8, 128), vmem(8, 128)),
            scratch_shapes=[vmem(128, 128), vmem(16, nj + 128), vmem(16, nj + 128)],
            name="widen",
        )(near(chip_got), near(core_got), near(fold), near(fields), near(far), near(close))

        def swaps(first):
            pairs = []
            for i in range(first, n_lon, 2):
                pairs += [(i, (i + 1) % n_lon), ((i + 1) % n_lon, i)]
            return pairs

        close = lax.ppermute(close, LON, swaps(0))
        far = lax.ppermute(far, LON, swaps(1))
        basis, message = pl.pallas_call(
            krylov_kernel,
            out_shape=(vmem(4, ni, nj), vmem(ny * nxh * nxl, 4, 128)),
            scratch_shapes=[vmem(4, 32, nj + 128), vmem(16, nj + 128), vmem(16, nj + 128)],
            name="krylov",
        )(near(piece), near(fields), near(beyond), near(far), near(close))
        got = lax.all_to_all(message, ("y", "xh", "xl"), 0, 0)
        message = pl.pallas_call(
            relay_kernel, out_shape=vmem(nz * ncore, 4, 128), name="relay"
        )(near(source), near(got))
        got = lax.all_to_all(message, ("z", "core"), 0, 0)
        level = lax.broadcasted_iota(jnp.int32, t.shape, 0)
        mask = jnp.where((flag[None] == 1) & (level < depth[None]), 1.0, 0.0).astype(jnp.float32)
        q = jnp.stack([t * mask, s * mask])
        ue = u * mask
        vn = v * mask

        def sides(msg):
            tiles = msg[: 8 * nl].reshape(nl, 8, nj)
            return jnp.stack([tiles[:, 0:3], tiles[:, 3:6]]), tiles[:, 6:7]

        even = lon_even()
        west = jnp.where(even, far, close)
        east = jnp.where(even, close, far)
        q_west, u_west = sides(west)
        q_east, _ = sides(east)
        north, south = rims[0], rims[1]

        def columns(msg):
            return jnp.transpose(msg[:6].reshape(2, 3, nl, ni), (0, 2, 3, 1))

        q_north, q_south = columns(north), columns(south)
        v_south = south[6].reshape(nl, ni, 1)
        zonal = jnp.concatenate([q_west, q, q_east], axis=2)
        merid = jnp.concatenate([q_south, q, q_north], axis=3)
        speed_x = jnp.concatenate([u_west, ue], axis=1)
        place = lax.broadcasted_iota(jnp.int32, (1, 1, nj + 1), 2)
        speed_y = jnp.concatenate([v_south, vn], axis=2)
        speed_y = jnp.where(last & (place > nj - 3), 0.0, speed_y)
        flux_x = face_flux(zonal, speed_x[None], ni + 1, 2)
        flux_y = face_flux(merid, speed_y[None], nj + 1, 3)
        updated = q - (flux_x[:, :, 1:] - flux_x[:, :, :-1]) - (flux_y[..., 1:] - flux_y[..., :-1])
        updated = updated * mask
        surface, residual, t_next, s_next = pl.pallas_call(
            finish_kernel,
            in_specs=[local] * 6 + [hbm] * 2,
            out_specs=(hbm,) * 4,
            out_shape=(f32(ni, nj), f32(ni, nj), f32(nl, ni, nj), f32(nl, ni, nj)),
            input_output_aliases={6: 2, 7: 3},
            scratch_shapes=[
                vmem(ni, nj),
                vmem(ni, nj),
                vmem(2, 128, 128),
                vmem(2, nl, ni, 128),
                pltpu.SemaphoreType.DMA((4,)),
            ],
            name="finish",
        )(
            near(basis),
            near(source),
            near(got),
            near(edges),
            near(updated[..., nj - 128 :]),
            near(mask[..., nj - 128 :]),
            updated[0],
            updated[1],
        )
        return t_next, s_next, surface, residual

    return on_device


def solution(mesh, sizes=SIZES):
    fine = Mesh(mesh.devices.reshape(sizes), ALL)
    block, plane = P(None, LON, LAT), P(LON, LAT)
    return jax.shard_map(
        make_on_device(sizes),
        mesh=fine,
        in_specs=(block,) * 4 + (plane,) * 3 + (P(LON),),
        out_specs=(block, block, plane, plane),
        check_vma=False,
    )
```

```python
import jax
import jax.numpy as jnp
from jax import lax
from jax.experimental import pallas as pl
from jax.experimental.pallas import tpu as pltpu
from jax.sharding import Mesh, PartitionSpec as P

ITERS = 3
LON = ("y", "xh", "z")
LAT = ("xl", "core")
ALL = LON + LAT
SIZES = (8, 2, 12, 2, 2)
SHIFT = 17.0
SCALE = 16.0
PAIRS = [(i, j) for i in range(4) for j in range(i, 4)]


def weno_upwind(a, b, c, d, e):
    d0, d1, d2, d3 = b - a, c - b, d - c, e - d
    s0, s1, s2 = d1 - d0, d2 - d1, d3 - d2
    t0 = s0 + 2.0 * d1
    t1 = d1 + d2
    t2 = s2 - 2.0 * d2
    k = 13.0 / 12.0
    e0 = 1e-06 + k * s0 * s0 + 0.25 * t0 * t0
    e1 = 1e-06 + k * s1 * s1 + 0.25 * t1 * t1
    e2 = 1e-06 + k * s2 * s2 + 0.25 * t2 * t2
    w0, w1, w2 = e1 * e2, e0 * e2, e0 * e1
    w0, w1, w2 = 0.1 * w0 * w0, 0.6 * w1 * w1, 0.3 * w2 * w2
    top = w0 * (5.0 * d1 - 2.0 * d0) + w1 * (d1 + 2.0 * d2) + w2 * (4.0 * d2 - d3)
    return c + top / (6.0 * (w0 + w1 + w2))


def face_flux(padded, speed, count, axis):
    q = [lax.slice_in_dim(padded, o, o + count, axis=axis) for o in range(6)]
    pos = speed > 0.0
    a, b, c, d, e = (jnp.where(pos, q[i], q[5 - i]) for i in range(5))
    return speed * weno_upwind(a, b, c, d, e)


def coefficients(gram):
    def form(p, q):
        total = 0.0
        for i in range(4):
            for j in range(4):
                if p[i] is not None and q[j] is not None:
                    total = total + p[i] * q[j] * gram[min(i, j), max(i, j)]
        return total

    def add(p, s, q):
        return [
            (p[i] if q[i] is None else (s * q[i] if p[i] is None else p[i] + s * q[i]))
            for i in range(4)
        ]

    def image(p):
        out = [None] * 4

        def put(i, x):
            out[i] = x if out[i] is None else out[i] + x

        for i in range(3):
            if p[i] is None:
                continue
            put(i, SHIFT * p[i])
            if i == 0:
                put(1, SCALE * p[0])
            else:
                put(i + 1, 0.5 * SCALE * p[i])
                put(i - 1, 0.5 * SCALE * p[i])
        return out

    x = [None] * 4
    r = [jnp.ones_like(gram[0, 0]), None, None, None]
    p = list(r)
    norm = form(r, r)
    for it in range(ITERS):
        ap = image(p)
        step = norm / form(p, ap)
        x = add(x, step, p)
        r = add(r, -step, ap)
        if it + 1 < ITERS:
            new = form(r, r)
            p = add(r, new / norm, p)
            norm = new
    return x, r


def lat_index():
    return 2 * lax.axis_index("xl") + lax.axis_index("core")


def mirror16(x):
    lane = lax.broadcasted_iota(jnp.int32, x.shape, 1)
    for bit in (1, 2, 4, 8):
        x = jnp.where((lane & bit) != 0, pltpu.roll(x, bit, 1), pltpu.roll(x, 128 - bit, 1))
    return x


def lon_even():
    return lax.rem(lax.axis_index("z"), 2) == 0


def pack_kernel(
    t, s, u, v, elev, flag, depth, fc,
    far, close, fields, edges, source, tile,
):
    nl, ni, nj = t.shape
    ocean = flag[...] == 1
    wet = depth[...]
    lane = lax.broadcasted_iota(jnp.int32, (ni, 128), 1)
    em = jnp.zeros((ni, nj), jnp.float32)
    nm = jnp.zeros((ni, nj), jnp.float32)
    tail = nj - 128
    for l in range(nl):
        m = jnp.where(ocean & (wet > l), 1.0, 0.0)
        em = em + u[l] * m
        vv = v[l] * m
        nm = nm + vv
        first, last = m[:, :128], m[:, tail:]
        x = jnp.where(lane < 8, t[l, :, :128] * first, t[l, :, tail:] * last)
        x = jnp.where((lane >= 8) & (lane < 16), pltpu.roll(s[l, :, :128] * first, 8, 1), x)
        x = jnp.where((lane >= 112) & (lane < 120), pltpu.roll(s[l, :, tail:] * last, 120, 1), x)
        x = jnp.where((lane >= 104) & (lane < 112), pltpu.roll(vv[:, tail:], 112, 1), x)
        tile[ni * l : ni * (l + 1)] = x
    em = em / nl
    nm = nm / nl
    part = elev[...] - em - nm
    coupler = 2.0 * jnp.sqrt((wet * flag[...]).astype(jnp.float32) / nl)
    for k, f in enumerate((part, em, nm, coupler)):
        fields[k] = f
    turned = tile[...].T
    edges[0:16] = turned[0:16]
    edges[16:40] = turned[104:128]
    even = lon_even()
    zero = jnp.zeros((2, nj), jnp.float32)
    for l in range(nl):
        m = jnp.where(ocean & (wet > l), 1.0, 0.0)
        tt, ss = t[l] * m, s[l] * m
        east_edge = jnp.concatenate(
            [tt[ni - 3 :], ss[ni - 3 :], u[l, ni - 1 :] * m[ni - 1 :], zero[:1]], axis=0
        )
        west_edge = jnp.concatenate([tt[:3], ss[:3], zero], axis=0)
        far[8 * l : 8 * l + 8] = jnp.where(even, west_edge, east_edge)
        close[8 * l : 8 * l + 8] = jnp.where(even, east_edge, west_edge)
    east_edge = jnp.concatenate(
        [part[ni - 3 :], em[ni - 4 :], nm[ni - 3 :], coupler[ni - 3 :], zero, zero[:1]], axis=0
    )
    west_edge = jnp.concatenate([part[:3], em[:3], nm[:3], coupler[:3], zero, zero], axis=0)
    far[64:80] = jnp.where(even, west_edge, east_edge)
    close[64:80] = jnp.where(even, east_edge, west_edge)
    block = lax.shift_right_logical(jnp.broadcast_to(fc[0:1, 0:1], (8, 128)), 4)
    nz = lax.axis_size("z")
    columns = lax.axis_size("y") * lax.axis_size("xh")
    column = lax.axis_index("y") * lax.axis_size("xh") + lax.axis_index("xh")
    place = lax.axis_index("z")

    def column_of(x):
        count = jnp.zeros((8, 128), jnp.int32)
        for k in range(1, columns):
            count = count + jnp.where(x >= nz * k, 1, 0)
        return count

    total = block + (nz * column + place)
    total = jnp.where(total >= nz * columns, total - nz * columns, total)
    ahead = total - nz * column_of(total) - place
    ahead = jnp.where(ahead < 0, ahead + nz, ahead)
    origin = total - (nz * column + ahead)
    origin = jnp.where(origin < 0, origin + nz * columns, origin)
    source[0] = column_of(origin)
    source[1] = block - nz * column_of(block)


def widen_kernel(far, close, fields, edges, wide, fold_ref, chip_swap, core_swap):
    _, ni, nj = fields.shape
    lat = lat_index()
    even = lon_even()
    blank = jnp.zeros((8, nj), jnp.float32)
    spans = ((64, 67, 64, 67), (67, 71, 67, 70), (71, 74, 70, 73), (74, 77, 73, 76))
    for k, (w0, w1, e0, e1) in enumerate(spans):
        wide[k, 0:8] = blank
        wide[k, 24:32] = blank
        wide[k, 8 - (w1 - w0) : 8] = jnp.where(even, far[w0:w1], close[w0:w1])
        wide[k, 8 : 8 + ni] = fields[k]
        wide[k, 24 : 24 + (e1 - e0)] = jnp.where(even, close[e0:e1], far[e0:e1])
    lane = lax.broadcasted_iota(jnp.int32, (4, 32, 128), 2)
    both = jnp.where(lane < 64, wide[:, :, 0:128], wide[:, :, nj - 128 : nj])
    turned = both.reshape(128, 128).T
    none = jnp.zeros((4, 128), jnp.float32)
    fold = jnp.concatenate(
        [edges[k : k + 1] for k in (39, 38, 37, 31, 30, 29)] + [none[:2]], axis=0
    )
    fold = mirror16(fold)
    north = jnp.concatenate(
        [edges[37:40], edges[29:32], edges[23:24], none[:1]], axis=0
    )
    south = jnp.concatenate([edges[0:3], edges[8:11], none[:2]], axis=0)
    fold_ref[...] = fold
    for out, ahead in ((chip_swap, lat == 1), (core_swap, lax.rem(lat, 2) == 0)):
        out[0:8] = jnp.where(ahead, north, south)
        out[8:12] = jnp.where(ahead, turned[124:128], turned[0:4])
        out[12:15] = fold[0:3]
        out[15:16] = none[:1]


def krylov_kernel(wide, chip_got, core_got, fold, basis_ref, message, rims, tile):
    ni, nj = basis_ref.shape[1:]
    lat = lat_index()
    tile[...] = jnp.zeros((128, 128), jnp.float32)
    odd = lax.rem(lat, 2) == 1
    north = jnp.where(lat < 3, jnp.where(odd, chip_got[...], core_got[...]), 0.0)
    south = jnp.where(lat > 0, jnp.where(odd, core_got[...], chip_got[...]), 0.0)
    rims[0] = north[0:8]
    rims[1] = south[0:8]
    tile[0:4] = north[8:12]
    tile[124:128] = south[8:12]
    beyond = tile[...].T.reshape(4, 32, 128)
    part, em, nm, cpl = (jnp.concatenate([wide[k], beyond[k]], axis=1) for k in range(4))
    rows, lanes = part.shape
    b0 = part + pltpu.roll(em, 1, 0) + pltpu.roll(nm, 1, 1)

    def scaled(e):
        f = cpl * e
        lap = (
            4.0 * f
            - pltpu.roll(f, 1, 0)
            - pltpu.roll(f, rows - 1, 0)
            - pltpu.roll(f, 1, 1)
            - pltpu.roll(f, lanes - 1, 1)
        )
        return ((1.0 - SHIFT) * e + cpl * lap) * (1.0 / SCALE)

    b1 = scaled(b0)
    b2 = 2.0 * scaled(b1) - b0
    b3 = 2.0 * scaled(b2) - b1
    basis = [b[8 : 8 + ni, :nj] for b in (b0, b1, b2, b3)]
    for k in range(4):
        basis_ref[k] = basis[k]
    row = lax.broadcasted_iota(jnp.int32, (4, 128), 0)
    col = lax.broadcasted_iota(jnp.int32, (4, 128), 1)
    piece = jnp.where(lat == 3, fold[3:6], core_got[12:15])
    total = jnp.concatenate([piece, jnp.zeros((1, 128), jnp.float32)], axis=0)
    for n, (i, j) in enumerate(PAIRS):
        prod = basis[i] * basis[j]
        prod = prod[:8] + prod[8:]
        acc = prod[:, :128]
        for k in range(1, nj // 128):
            acc = acc + prod[:, 128 * k : 128 * (k + 1)]
        one = jnp.sum(jnp.sum(acc, axis=0, keepdims=True), axis=1, keepdims=True)
        total = jnp.where((row == 3) & (col == n), one, total)
    for k in range(message.shape[0]):
        message[k] = total


def relay_kernel(source, got, message):
    peers = got.shape[0]
    total = got[0]
    for k in range(1, peers):
        total = total + got[k]
    which = source[0, 0:4]
    piece = got[1]
    for k in range(1, peers // 2):
        piece = jnp.where(which == k, got[2 * k + 1], piece)
    row = lax.broadcasted_iota(jnp.int32, (4, 128), 0)
    text = jnp.where(row < 3, piece, total)
    for k in range(message.shape[0]):
        message[k] = text


def finish_kernel(
    basis_ref, source, got, edges, tail, wet, base_t, base_s,
    surface_out, residual_out, out_t, out_s, surface, residual, tile, final, sems,
):
    del base_t, base_s
    total = got[0]
    for k in range(1, got.shape[0]):
        total = total + got[k]
    fold = [got[0], got[1]]
    which = source[1, 0:4]
    for k in range(1, got.shape[0] // 2):
        fold = [jnp.where(which == k, got[2 * k + i], fold[i]) for i in range(2)]
    last = jnp.where(lat_index() == 3, 1.0, 0.0)
    rows = [
        jnp.concatenate([edges[35:40], fold[0][0:3]], axis=0),
        jnp.concatenate([edges[27:32], fold[1][0:3]], axis=0),
    ]
    row = lax.broadcasted_iota(jnp.int32, (8, 128), 0)
    speed = jnp.where(row < 3, pltpu.roll(edges[16:24], 3, 0) * last, 0.0)
    pos = speed > 0.0
    nj = surface.shape[1]
    for k in range(2):
        q = [rows[k]] + [pltpu.roll(rows[k], 8 - o, 0) for o in range(1, 6)]
        face = speed * weno_upwind(*[jnp.where(pos, q[i], q[5 - i]) for i in range(5)])
        change = face - jnp.where(row == 0, 0.0, pltpu.roll(face, 1, 0))
        tile[k] = jnp.zeros((128, 128), jnp.float32)
        tile[k, 125:128] = change[0:3]
        final[k] = (tail[k] - tile[k].T.reshape(tail.shape[1:])) * wet[...]
    line = total[3:4]
    col = lax.broadcasted_iota(jnp.int32, (1, 128), 1)
    gram = {}
    for n, pair in enumerate(PAIRS):
        gram[pair] = jnp.sum(jnp.where(col == n, line, 0.0), axis=1, keepdims=True)
    xc, rc = coefficients(gram)
    basis = [basis_ref[k] for k in range(4)]
    surface[...] = sum(c * f for c, f in zip(xc, basis) if c is not None)
    residual[...] = sum(c * f for c, f in zip(rc, basis) if c is not None)
    copies = [
        pltpu.make_async_copy(final.at[0], out_t.at[:, :, nj - 128 : nj], sems.at[0]),
        pltpu.make_async_copy(final.at[1], out_s.at[:, :, nj - 128 : nj], sems.at[1]),
        pltpu.make_async_copy(surface, surface_out, sems.at[2]),
        pltpu.make_async_copy(residual, residual_out, sems.at[3]),
    ]
    for copy in copies:
        copy.start()
    for copy in copies:
        copy.wait()


def near(value):
    return pltpu.with_memory_space_constraint(value, pltpu.VMEM)


def f32(*shape):
    return jax.ShapeDtypeStruct(shape, jnp.float32)


def vmem(*shape):
    return pltpu.VMEM(shape, jnp.float32)


def make_on_device(sizes):
    ny, nxh, nz, nxl, ncore = sizes
    n_lon, n_lat = ny * nxh * nz, nxl * ncore

    def on_device(t, s, u, v, elev, flag, depth, fc):
        nl, ni, nj = t.shape
        lat = lax.axis_index(LAT)
        last = lat == n_lat - 1
        hbm, local = pl.BlockSpec(memory_space=pl.ANY), pl.BlockSpec(memory_space=pltpu.VMEM)

        far, close, fields, edges, source = pl.pallas_call(
            pack_kernel,
            out_shape=(
                vmem(80, nj),
                vmem(80, nj),
                vmem(4, ni, nj),
                vmem(40, 128),
                pltpu.VMEM((2, 8, 128), jnp.int32),
            ),
            scratch_shapes=[vmem(128, 128)],
            name="pack",
        )(t, s, u, v, elev, flag, depth, fc.reshape(1, ni))

        def swaps(first):
            pairs = []
            for i in range(first, n_lon, 2):
                pairs += [(i, (i + 1) % n_lon), ((i + 1) % n_lon, i)]
            return pairs

        far = lax.ppermute(far, LON, swaps(1))
        close = lax.ppermute(close, LON, swaps(0))
        wide, fold, chip_swap, core_swap = pl.pallas_call(
            widen_kernel,
            out_shape=(vmem(4, 32, nj), vmem(8, 128), vmem(16, 128), vmem(16, 128)),
            name="widen",
        )(near(far), near(close), near(fields), near(edges))
        chip_got = lax.ppermute(chip_swap, LAT, [(1, 2), (2, 1)])
        core_got = lax.ppermute(core_swap, LAT, [(0, 1), (1, 0), (2, 3), (3, 2)])
        basis, message, rims = pl.pallas_call(
            krylov_kernel,
            out_shape=(vmem(4, ni, nj), vmem(ny * nxh * nxl, 4, 128), vmem(2, 8, 128)),
            scratch_shapes=[vmem(128, 128)],
            name="krylov",
        )(near(wide), near(chip_got), near(core_got), near(fold))
        got = lax.all_to_all(message, ("y", "xh", "xl"), 0, 0)
        message = pl.pallas_call(
            relay_kernel, out_shape=vmem(nz * ncore, 4, 128), name="relay"
        )(near(source), near(got))
        got = lax.all_to_all(message, ("z", "core"), 0, 0)
        level = lax.broadcasted_iota(jnp.int32, t.shape, 0)
        mask = jnp.where((flag[None] == 1) & (level < depth[None]), 1.0, 0.0).astype(jnp.float32)
        q = jnp.stack([t * mask, s * mask])
        ue = u * mask
        vn = v * mask

        def sides(msg):
            tiles = msg[: 8 * nl].reshape(nl, 8, nj)
            return jnp.stack([tiles[:, 0:3], tiles[:, 3:6]]), tiles[:, 6:7]

        even = lon_even()
        west = jnp.where(even, far, close)
        east = jnp.where(even, close, far)
        q_west, u_west = sides(west)
        q_east, _ = sides(east)
        north, south = rims[0], rims[1]

        def columns(msg):
            return jnp.transpose(msg[:6].reshape(2, 3, nl, ni), (0, 2, 3, 1))

        q_north, q_south = columns(north), columns(south)
        v_south = south[6].reshape(nl, ni, 1)
        zonal = jnp.concatenate([q_west, q, q_east], axis=2)
        merid = jnp.concatenate([q_south, q, q_north], axis=3)
        speed_x = jnp.concatenate([u_west, ue], axis=1)
        place = lax.broadcasted_iota(jnp.int32, (1, 1, nj + 1), 2)
        speed_y = jnp.concatenate([v_south, vn], axis=2)
        speed_y = jnp.where(last & (place > nj - 3), 0.0, speed_y)
        flux_x = face_flux(zonal, speed_x[None], ni + 1, 2)
        flux_y = face_flux(merid, speed_y[None], nj + 1, 3)
        updated = q - (flux_x[:, :, 1:] - flux_x[:, :, :-1]) - (flux_y[..., 1:] - flux_y[..., :-1])
        updated = updated * mask
        surface, residual, t_next, s_next = pl.pallas_call(
            finish_kernel,
            in_specs=[local] * 6 + [hbm] * 2,
            out_specs=(hbm,) * 4,
            out_shape=(f32(ni, nj), f32(ni, nj), f32(nl, ni, nj), f32(nl, ni, nj)),
            input_output_aliases={6: 2, 7: 3},
            scratch_shapes=[
                vmem(ni, nj),
                vmem(ni, nj),
                vmem(2, 128, 128),
                vmem(2, nl, ni, 128),
                pltpu.SemaphoreType.DMA((4,)),
            ],
            name="finish",
        )(
            near(basis),
            near(source),
            near(got),
            near(edges),
            near(updated[..., nj - 128 :]),
            near(mask[..., nj - 128 :]),
            updated[0],
            updated[1],
        )
        return t_next, s_next, surface, residual

    return on_device


def solution(mesh, sizes=SIZES):
    fine = Mesh(mesh.devices.reshape(sizes), ALL)
    block, plane = P(None, LON, LAT), P(LON, LAT)
    return jax.shard_map(
        make_on_device(sizes),
        mesh=fine,
        in_specs=(block,) * 4 + (plane,) * 3 + (P(LON),),
        out_specs=(block, block, plane, plane),
        check_vma=False,
    )
```

```python
import jax
import jax.numpy as jnp
from jax import lax
from jax.experimental import pallas as pl
from jax.experimental.pallas import tpu as pltpu
from jax.sharding import Mesh, PartitionSpec as P

ITERS = 3
LON = ("y", "xh", "z")
LAT = ("xl", "core")
ALL = LON + LAT
SIZES = (8, 2, 12, 2, 2)
SHIFT = 17.0
SCALE = 16.0
PAIRS = [(i, j) for i in range(4) for j in range(i, 4)]


def weno_upwind(a, b, c, d, e):
    d0, d1, d2, d3 = b - a, c - b, d - c, e - d
    s0, s1, s2 = d1 - d0, d2 - d1, d3 - d2
    t0 = s0 + 2.0 * d1
    t1 = d1 + d2
    t2 = s2 - 2.0 * d2
    k = 13.0 / 12.0
    e0 = 1e-06 + k * s0 * s0 + 0.25 * t0 * t0
    e1 = 1e-06 + k * s1 * s1 + 0.25 * t1 * t1
    e2 = 1e-06 + k * s2 * s2 + 0.25 * t2 * t2
    w0, w1, w2 = e1 * e2, e0 * e2, e0 * e1
    w0, w1, w2 = 0.1 * w0 * w0, 0.6 * w1 * w1, 0.3 * w2 * w2
    top = w0 * (5.0 * d1 - 2.0 * d0) + w1 * (d1 + 2.0 * d2) + w2 * (4.0 * d2 - d3)
    return c + top / (6.0 * (w0 + w1 + w2))


def face_flux(padded, speed, count, axis):
    q = [lax.slice_in_dim(padded, o, o + count, axis=axis) for o in range(6)]
    pos = speed > 0.0
    a, b, c, d, e = (jnp.where(pos, q[i], q[5 - i]) for i in range(5))
    return speed * weno_upwind(a, b, c, d, e)


def coefficients(gram):
    def form(p, q):
        total = 0.0
        for i in range(4):
            for j in range(4):
                if p[i] is not None and q[j] is not None:
                    total = total + p[i] * q[j] * gram[min(i, j), max(i, j)]
        return total

    def add(p, s, q):
        return [
            (p[i] if q[i] is None else (s * q[i] if p[i] is None else p[i] + s * q[i]))
            for i in range(4)
        ]

    def image(p):
        out = [None] * 4

        def put(i, x):
            out[i] = x if out[i] is None else out[i] + x

        for i in range(3):
            if p[i] is None:
                continue
            put(i, SHIFT * p[i])
            if i == 0:
                put(1, SCALE * p[0])
            else:
                put(i + 1, 0.5 * SCALE * p[i])
                put(i - 1, 0.5 * SCALE * p[i])
        return out

    x = [None] * 4
    r = [jnp.ones_like(gram[0, 0]), None, None, None]
    p = list(r)
    norm = form(r, r)
    for it in range(ITERS):
        ap = image(p)
        step = norm / form(p, ap)
        x = add(x, step, p)
        r = add(r, -step, ap)
        if it + 1 < ITERS:
            new = form(r, r)
            p = add(r, new / norm, p)
            norm = new
    return x, r


def lat_index():
    return 2 * lax.axis_index("xl") + lax.axis_index("core")


def mirror16(x):
    lane = lax.broadcasted_iota(jnp.int32, x.shape, 1)
    for bit in (1, 2, 4, 8):
        x = jnp.where((lane & bit) != 0, pltpu.roll(x, bit, 1), pltpu.roll(x, 128 - bit, 1))
    return x


def lon_even():
    return lax.rem(lax.axis_index("z"), 2) == 0


def pack_kernel(
    t, s, u, v, elev, flag, depth, fc,
    far, close, fields, edges, source, fold_ref, chip_swap, core_swap, tile,
):
    nl, ni, nj = t.shape
    ocean = flag[...] == 1
    wet = depth[...]
    lane = lax.broadcasted_iota(jnp.int32, (ni, 128), 1)
    em = jnp.zeros((ni, nj), jnp.float32)
    nm = jnp.zeros((ni, nj), jnp.float32)
    tail = nj - 128
    for l in range(nl):
        m = jnp.where(ocean & (wet > l), 1.0, 0.0)
        em = em + u[l] * m
        vv = v[l] * m
        nm = nm + vv
        first, last = m[:, :128], m[:, tail:]
        x = jnp.where(lane < 8, t[l, :, :128] * first, t[l, :, tail:] * last)
        x = jnp.where((lane >= 8) & (lane < 16), pltpu.roll(s[l, :, :128] * first, 8, 1), x)
        x = jnp.where((lane >= 112) & (lane < 120), pltpu.roll(s[l, :, tail:] * last, 120, 1), x)
        x = jnp.where((lane >= 104) & (lane < 112), pltpu.roll(vv[:, tail:], 112, 1), x)
        tile[ni * l : ni * (l + 1)] = x
    em = em / nl
    nm = nm / nl
    part = elev[...] - em - nm
    coupler = 2.0 * jnp.sqrt((wet * flag[...]).astype(jnp.float32) / nl)
    for k, f in enumerate((part, em, nm, coupler)):
        fields[k] = f
        x = tile[ni * k : ni * (k + 1)]
        x = jnp.where((lane >= 16) & (lane < 20), pltpu.roll(f[:, :128], 16, 1), x)
        x = jnp.where((lane >= 100) & (lane < 104), pltpu.roll(f[:, tail:], 104, 1), x)
        tile[ni * k : ni * (k + 1)] = x
    turned = tile[...].T
    edges[0:16] = turned[0:16]
    edges[16:40] = turned[104:128]
    lat = lat_index()
    none = jnp.zeros((2, 128), jnp.float32)
    t_end, s_end, v_end = turned[125:128], turned[117:120], turned[111:112]
    fold = [jnp.concatenate([turned[k : k + 1] for k in (n, n - 1, n - 2)]) for n in (127, 119)]
    fold = mirror16(jnp.concatenate(fold + [none], axis=0))
    north = jnp.concatenate([t_end, s_end, v_end, none[:1]], axis=0)
    south = jnp.concatenate([turned[0:3], turned[8:11], none], axis=0)
    fold_ref[...] = fold
    ahead = lax.rem(lat, 2) == 0
    core_swap[0:8] = jnp.where(ahead, north, south)
    core_swap[8:12] = jnp.where(ahead, turned[100:104], turned[16:20])
    core_swap[12:15] = fold[0:3]
    core_swap[15:16] = none[:1]
    ahead = lat == 1
    chip_swap[0:8] = jnp.where(ahead, north, south)
    chip_swap[8:12] = jnp.where(ahead, turned[100:104], turned[16:20])
    chip_swap[12:14] = none
    chip_swap[14:16] = none

    even = lon_even()
    zero = jnp.zeros((2, nj), jnp.float32)
    for l in range(nl):
        m = jnp.where(ocean & (wet > l), 1.0, 0.0)
        tt, ss = t[l] * m, s[l] * m
        east_edge = jnp.concatenate(
            [tt[ni - 3 :], ss[ni - 3 :], u[l, ni - 1 :] * m[ni - 1 :], zero[:1]], axis=0
        )
        west_edge = jnp.concatenate([tt[:3], ss[:3], zero], axis=0)
        far[8 * l : 8 * l + 8] = jnp.where(even, west_edge, east_edge)
        close[8 * l : 8 * l + 8] = jnp.where(even, east_edge, west_edge)
    block = lax.shift_right_logical(jnp.broadcast_to(fc[0:1, 0:1], (8, 128)), 4)
    nz = lax.axis_size("z")
    columns = lax.axis_size("y") * lax.axis_size("xh")
    column = lax.axis_index("y") * lax.axis_size("xh") + lax.axis_index("xh")
    place = lax.axis_index("z")

    def column_of(x):
        count = jnp.zeros((8, 128), jnp.int32)
        for k in range(1, columns):
            count = count + jnp.where(x >= nz * k, 1, 0)
        return count

    total = block + (nz * column + place)
    total = jnp.where(total >= nz * columns, total - nz * columns, total)
    ahead = total - nz * column_of(total) - place
    ahead = jnp.where(ahead < 0, ahead + nz, ahead)
    origin = total - (nz * column + ahead)
    origin = jnp.where(origin < 0, origin + nz * columns, origin)
    source[0] = column_of(origin)
    source[1] = block - nz * column_of(block)


def widen_kernel(
    chip_got, core_got, fold, fields, far_q, close_q, far, close, plane, rims, piece, tile
):
    _, ni, nj = fields.shape
    lat = lat_index()
    even = lon_even()
    odd = lax.rem(lat, 2) == 1
    north = jnp.where(lat < 3, jnp.where(odd, chip_got[...], core_got[...]), 0.0)
    south = jnp.where(lat > 0, jnp.where(odd, core_got[...], chip_got[...]), 0.0)
    piece[0:3] = jnp.where(lat == 3, fold[3:6], core_got[12:15])
    piece[3:8] = jnp.zeros((5, 128), jnp.float32)
    rims[0] = north[0:8]
    rims[1] = south[0:8]
    tile[...] = jnp.zeros((128, 128), jnp.float32)
    tile[0:4] = north[8:12]
    tile[124:128] = south[8:12]
    beyond = tile[...].T[0 : 4 * ni].reshape(4, ni, 128)
    part, em, nm, cpl = (jnp.concatenate([fields[k], beyond[k]], axis=1) for k in range(4))
    row = lax.broadcasted_iota(jnp.int32, part.shape, 0)
    side = part + pltpu.roll(nm, 1, 1) + jnp.where(row == 0, 0.0, pltpu.roll(em, 1, 0))
    for k, f in enumerate((side, cpl, em)):
        plane[k] = f
    up = jnp.concatenate([side[ni - 3 :], cpl[ni - 3 :], em[ni - 1 :], em[ni - 1 :]], axis=0)
    down = jnp.concatenate([side[0:3], cpl[0:3], cpl[0:2]], axis=0)
    far[0:64] = far_q[...]
    close[0:64] = close_q[...]
    for out, first, second in ((far, down, up), (close, up, down)):
        rows = jnp.where(even, first, second)
        for l in range(8):
            out[8 * l + 7 : 8 * l + 8] = rows[l : l + 1, 0:nj]
        out[64:72, 0:128] = rows[:, nj:]
        out[64:72, 128:384] = jnp.zeros((8, 256), jnp.float32)


def krylov_kernel(piece, plane, far, close, basis_ref, message, wide, west, east):
    ni, nj = basis_ref.shape[1:]
    even = lon_even()
    for out, first, second in ((west, far, close), (east, close, far)):
        for l in range(8):
            at = 8 * l + 7
            out[l : l + 1, 0:nj] = jnp.where(even, first[at : at + 1], second[at : at + 1])
        out[:, nj:] = jnp.where(even, first[64:72, 0:128], second[64:72, 0:128])
    blank = jnp.zeros((8, nj + 128), jnp.float32)
    for k in range(2):
        wide[k, 0:8] = blank
        wide[k, 24:32] = blank
        wide[k, 8:24] = plane[k]
        wide[k, 5:8] = west[3 * k : 3 * k + 3]
        wide[k, 24:27] = east[3 * k : 3 * k + 3]
    wide[0, 8:9] = plane[0, 0:1] + west[6:7]
    wide[0, 24:25] = east[0:1] + plane[2, ni - 1 : ni]
    b0 = wide[0]
    cpl = wide[1]
    rows, lanes = b0.shape

    def scaled(e):
        f = cpl * e
        lap = (
            4.0 * f
            - pltpu.roll(f, 1, 0)
            - pltpu.roll(f, rows - 1, 0)
            - pltpu.roll(f, 1, 1)
            - pltpu.roll(f, lanes - 1, 1)
        )
        return ((1.0 - SHIFT) * e + cpl * lap) * (1.0 / SCALE)

    b1 = scaled(b0)
    b2 = 2.0 * scaled(b1) - b0
    b3 = 2.0 * scaled(b2) - b1
    basis = [b[8 : 8 + ni, :nj] for b in (b0, b1, b2, b3)]
    for k in range(4):
        basis_ref[k] = basis[k]
    row = lax.broadcasted_iota(jnp.int32, (4, 128), 0)
    col = lax.broadcasted_iota(jnp.int32, (4, 128), 1)
    total = piece[0:4]
    for n, (i, j) in enumerate(PAIRS):
        prod = basis[i] * basis[j]
        prod = prod[:8] + prod[8:]
        acc = prod[:, :128]
        for k in range(1, nj // 128):
            acc = acc + prod[:, 128 * k : 128 * (k + 1)]
        one = jnp.sum(jnp.sum(acc, axis=0, keepdims=True), axis=1, keepdims=True)
        total = jnp.where((row == 3) & (col == n), one, total)
    for k in range(message.shape[0]):
        message[k] = total


def relay_kernel(source, got, message):
    peers = got.shape[0]
    total = got[0]
    for k in range(1, peers):
        total = total + got[k]
    which = source[0, 0:4]
    piece = got[1]
    for k in range(1, peers // 2):
        piece = jnp.where(which == k, got[2 * k + 1], piece)
    row = lax.broadcasted_iota(jnp.int32, (4, 128), 0)
    text = jnp.where(row < 3, piece, total)
    for k in range(message.shape[0]):
        message[k] = text


def finish_kernel(
    basis_ref, source, got, edges, tail, wet, base_t, base_s,
    surface_out, residual_out, out_t, out_s, surface, residual, tile, final, sems,
):
    del base_t, base_s
    total = got[0]
    for k in range(1, got.shape[0]):
        total = total + got[k]
    fold = [got[0], got[1]]
    which = source[1, 0:4]
    for k in range(1, got.shape[0] // 2):
        fold = [jnp.where(which == k, got[2 * k + i], fold[i]) for i in range(2)]
    last = jnp.where(lat_index() == 3, 1.0, 0.0)
    rows = [
        jnp.concatenate([edges[35:40], fold[0][0:3]], axis=0),
        jnp.concatenate([edges[27:32], fold[1][0:3]], axis=0),
    ]
    row = lax.broadcasted_iota(jnp.int32, (8, 128), 0)
    speed = jnp.where(row < 3, pltpu.roll(edges[16:24], 3, 0) * last, 0.0)
    pos = speed > 0.0
    nj = surface.shape[1]
    for k in range(2):
        q = [rows[k]] + [pltpu.roll(rows[k], 8 - o, 0) for o in range(1, 6)]
        face = speed * weno_upwind(*[jnp.where(pos, q[i], q[5 - i]) for i in range(5)])
        change = face - jnp.where(row == 0, 0.0, pltpu.roll(face, 1, 0))
        tile[k] = jnp.zeros((128, 128), jnp.float32)
        tile[k, 125:128] = change[0:3]
        final[k] = (tail[k] - tile[k].T.reshape(tail.shape[1:])) * wet[...]
    line = total[3:4]
    col = lax.broadcasted_iota(jnp.int32, (1, 128), 1)
    gram = {}
    for n, pair in enumerate(PAIRS):
        gram[pair] = jnp.sum(jnp.where(col == n, line, 0.0), axis=1, keepdims=True)
    xc, rc = coefficients(gram)
    basis = [basis_ref[k] for k in range(4)]
    surface[...] = sum(c * f for c, f in zip(xc, basis) if c is not None)
    residual[...] = sum(c * f for c, f in zip(rc, basis) if c is not None)
    copies = [
        pltpu.make_async_copy(final.at[0], out_t.at[:, :, nj - 128 : nj], sems.at[0]),
        pltpu.make_async_copy(final.at[1], out_s.at[:, :, nj - 128 : nj], sems.at[1]),
        pltpu.make_async_copy(surface, surface_out, sems.at[2]),
        pltpu.make_async_copy(residual, residual_out, sems.at[3]),
    ]
    for copy in copies:
        copy.start()
    for copy in copies:
        copy.wait()


def near(value):
    return pltpu.with_memory_space_constraint(value, pltpu.VMEM)


def f32(*shape):
    return jax.ShapeDtypeStruct(shape, jnp.float32)


def vmem(*shape):
    return pltpu.VMEM(shape, jnp.float32)


def make_on_device(sizes):
    ny, nxh, nz, nxl, ncore = sizes
    n_lon, n_lat = ny * nxh * nz, nxl * ncore

    def on_device(t, s, u, v, elev, flag, depth, fc):
        nl, ni, nj = t.shape
        lat = lax.axis_index(LAT)
        last = lat == n_lat - 1
        hbm, local = pl.BlockSpec(memory_space=pl.ANY), pl.BlockSpec(memory_space=pltpu.VMEM)

        far, close, fields, edges, source, fold, chip_swap, core_swap = pl.pallas_call(
            pack_kernel,
            out_shape=(
                vmem(64, nj),
                vmem(64, nj),
                vmem(4, ni, nj),
                vmem(40, 128),
                pltpu.VMEM((2, 8, 128), jnp.int32),
                vmem(8, 128),
                vmem(16, 128),
                vmem(16, 128),
            ),
            scratch_shapes=[vmem(128, 128)],
            name="pack",
        )(t, s, u, v, elev, flag, depth, fc.reshape(1, ni))
        chip_got = lax.ppermute(chip_swap, LAT, [(1, 2), (2, 1)])
        core_got = lax.ppermute(core_swap, LAT, [(0, 1), (1, 0), (2, 3), (3, 2)])
        far, close, plane, rims, piece = pl.pallas_call(
            widen_kernel,
            out_shape=(
                vmem(72, nj),
                vmem(72, nj),
                vmem(3, ni, nj + 128),
                vmem(2, 8, 128),
                vmem(8, 128),
            ),
            scratch_shapes=[vmem(128, 128)],
            name="widen",
        )(near(chip_got), near(core_got), near(fold), near(fields), near(far), near(close))

        def swaps(first):
            pairs = []
            for i in range(first, n_lon, 2):
                pairs += [(i, (i + 1) % n_lon), ((i + 1) % n_lon, i)]
            return pairs

        close = lax.ppermute(close, LON, swaps(0))
        far = lax.ppermute(far, LON, swaps(1))
        basis, message = pl.pallas_call(
            krylov_kernel,
            out_shape=(vmem(4, ni, nj), vmem(ny * nxh * nxl, 4, 128)),
            scratch_shapes=[vmem(2, 32, nj + 128), vmem(8, nj + 128), vmem(8, nj + 128)],
            name="krylov",
        )(near(piece), near(plane), near(far), near(close))
        got = lax.all_to_all(message, ("y", "xh", "xl"), 0, 0)
        message = pl.pallas_call(
            relay_kernel, out_shape=vmem(nz * ncore, 4, 128), name="relay"
        )(near(source), near(got))
        got = lax.all_to_all(message, ("z", "core"), 0, 0)
        level = lax.broadcasted_iota(jnp.int32, t.shape, 0)
        mask = jnp.where((flag[None] == 1) & (level < depth[None]), 1.0, 0.0).astype(jnp.float32)
        q = jnp.stack([t * mask, s * mask])
        ue = u * mask
        vn = v * mask

        def sides(msg):
            tiles = msg[: 8 * nl].reshape(nl, 8, nj)
            return jnp.stack([tiles[:, 0:3], tiles[:, 3:6]]), tiles[:, 6:7]

        even = lon_even()
        west = jnp.where(even, far, close)
        east = jnp.where(even, close, far)
        q_west, u_west = sides(west)
        q_east, _ = sides(east)
        north, south = rims[0], rims[1]

        def columns(msg):
            return jnp.transpose(msg[:6].reshape(2, 3, nl, ni), (0, 2, 3, 1))

        q_north, q_south = columns(north), columns(south)
        v_south = south[6].reshape(nl, ni, 1)
        zonal = jnp.concatenate([q_west, q, q_east], axis=2)
        merid = jnp.concatenate([q_south, q, q_north], axis=3)
        speed_x = jnp.concatenate([u_west, ue], axis=1)
        place = lax.broadcasted_iota(jnp.int32, (1, 1, nj + 1), 2)
        speed_y = jnp.concatenate([v_south, vn], axis=2)
        speed_y = jnp.where(last & (place > nj - 3), 0.0, speed_y)
        flux_x = face_flux(zonal, speed_x[None], ni + 1, 2)
        flux_y = face_flux(merid, speed_y[None], nj + 1, 3)
        updated = q - (flux_x[:, :, 1:] - flux_x[:, :, :-1]) - (flux_y[..., 1:] - flux_y[..., :-1])
        updated = updated * mask
        surface, residual, t_next, s_next = pl.pallas_call(
            finish_kernel,
            in_specs=[local] * 6 + [hbm] * 2,
            out_specs=(hbm,) * 4,
            out_shape=(f32(ni, nj), f32(ni, nj), f32(nl, ni, nj), f32(nl, ni, nj)),
            input_output_aliases={6: 2, 7: 3},
            scratch_shapes=[
                vmem(ni, nj),
                vmem(ni, nj),
                vmem(2, 128, 128),
                vmem(2, nl, ni, 128),
                pltpu.SemaphoreType.DMA((4,)),
            ],
            name="finish",
        )(
            near(basis),
            near(source),
            near(got),
            near(edges),
            near(updated[..., nj - 128 :]),
            near(mask[..., nj - 128 :]),
            updated[0],
            updated[1],
        )
        return t_next, s_next, surface, residual

    return on_device


def solution(mesh, sizes=SIZES):
    fine = Mesh(mesh.devices.reshape(sizes), ALL)
    block, plane = P(None, LON, LAT), P(LON, LAT)
    return jax.shard_map(
        make_on_device(sizes),
        mesh=fine,
        in_specs=(block,) * 4 + (plane,) * 3 + (P(LON),),
        out_specs=(block, block, plane, plane),
        check_vma=False,
    )
```

```python
import jax
import jax.numpy as jnp
from jax import lax
from jax.experimental import pallas as pl
from jax.experimental.pallas import tpu as pltpu
from jax.sharding import Mesh, PartitionSpec as P

ITERS = 3
LON = ("y", "xh", "z")
LAT = ("xl", "core")
ALL = LON + LAT
SIZES = (8, 2, 12, 2, 2)
SHIFT = 17.0
SCALE = 16.0
PAIRS = [(i, j) for i in range(4) for j in range(i, 4)]


def weno_upwind(a, b, c, d, e):
    d0, d1, d2, d3 = b - a, c - b, d - c, e - d
    s0, s1, s2 = d1 - d0, d2 - d1, d3 - d2
    t0 = s0 + 2.0 * d1
    t1 = d1 + d2
    t2 = s2 - 2.0 * d2
    k = 13.0 / 12.0
    e0 = 1e-06 + k * s0 * s0 + 0.25 * t0 * t0
    e1 = 1e-06 + k * s1 * s1 + 0.25 * t1 * t1
    e2 = 1e-06 + k * s2 * s2 + 0.25 * t2 * t2
    w0, w1, w2 = e1 * e2, e0 * e2, e0 * e1
    w0, w1, w2 = 0.1 * w0 * w0, 0.6 * w1 * w1, 0.3 * w2 * w2
    top = w0 * (5.0 * d1 - 2.0 * d0) + w1 * (d1 + 2.0 * d2) + w2 * (4.0 * d2 - d3)
    return c + top / (6.0 * (w0 + w1 + w2))


def face_flux(padded, speed, count, axis):
    q = [lax.slice_in_dim(padded, o, o + count, axis=axis) for o in range(6)]
    pos = speed > 0.0
    a, b, c, d, e = (jnp.where(pos, q[i], q[5 - i]) for i in range(5))
    return speed * weno_upwind(a, b, c, d, e)


def coefficients(gram):
    def form(p, q):
        total = 0.0
        for i in range(4):
            for j in range(4):
                if p[i] is not None and q[j] is not None:
                    total = total + p[i] * q[j] * gram[min(i, j), max(i, j)]
        return total

    def add(p, s, q):
        return [
            (p[i] if q[i] is None else (s * q[i] if p[i] is None else p[i] + s * q[i]))
            for i in range(4)
        ]

    def image(p):
        out = [None] * 4

        def put(i, x):
            out[i] = x if out[i] is None else out[i] + x

        for i in range(3):
            if p[i] is None:
                continue
            put(i, SHIFT * p[i])
            if i == 0:
                put(1, SCALE * p[0])
            else:
                put(i + 1, 0.5 * SCALE * p[i])
                put(i - 1, 0.5 * SCALE * p[i])
        return out

    x = [None] * 4
    r = [jnp.ones_like(gram[0, 0]), None, None, None]
    p = list(r)
    norm = form(r, r)
    for it in range(ITERS):
        ap = image(p)
        step = norm / form(p, ap)
        x = add(x, step, p)
        r = add(r, -step, ap)
        if it + 1 < ITERS:
            new = form(r, r)
            p = add(r, new / norm, p)
            norm = new
    return x, r


def lat_index():
    return 2 * lax.axis_index("xl") + lax.axis_index("core")


def mirror16(x):
    lane = lax.broadcasted_iota(jnp.int32, x.shape, 1)
    for bit in (1, 2, 4, 8):
        x = jnp.where((lane & bit) != 0, pltpu.roll(x, bit, 1), pltpu.roll(x, 128 - bit, 1))
    return x


def lon_even():
    return lax.rem(lax.axis_index("z"), 2) == 0


def pack_kernel(
    t, s, u, v, elev, flag, depth, fc,
    fields, edges, source, fold_ref, chip_swap, core_swap, tile,
):
    nl, ni, nj = t.shape
    ocean = flag[...] == 1
    wet = depth[...]
    lane = lax.broadcasted_iota(jnp.int32, (ni, 128), 1)
    em = jnp.zeros((ni, nj), jnp.float32)
    nm = jnp.zeros((ni, nj), jnp.float32)
    tail = nj - 128
    for l in range(nl):
        m = jnp.where(ocean & (wet > l), 1.0, 0.0)
        em = em + u[l] * m
        vv = v[l] * m
        nm = nm + vv
        first, last = m[:, :128], m[:, tail:]
        x = jnp.where(lane < 8, t[l, :, :128] * first, t[l, :, tail:] * last)
        x = jnp.where((lane >= 8) & (lane < 16), pltpu.roll(s[l, :, :128] * first, 8, 1), x)
        x = jnp.where((lane >= 112) & (lane < 120), pltpu.roll(s[l, :, tail:] * last, 120, 1), x)
        x = jnp.where((lane >= 104) & (lane < 112), pltpu.roll(vv[:, tail:], 112, 1), x)
        tile[ni * l : ni * (l + 1)] = x
    em = em / nl
    nm = nm / nl
    part = elev[...] - em - nm
    coupler = 2.0 * jnp.sqrt((wet * flag[...]).astype(jnp.float32) / nl)
    for k, f in enumerate((part, em, nm, coupler)):
        fields[k] = f
        x = tile[ni * k : ni * (k + 1)]
        x = jnp.where((lane >= 16) & (lane < 20), pltpu.roll(f[:, :128], 16, 1), x)
        x = jnp.where((lane >= 100) & (lane < 104), pltpu.roll(f[:, tail:], 104, 1), x)
        tile[ni * k : ni * (k + 1)] = x
    turned = tile[...].T
    edges[0:16] = turned[0:16]
    edges[16:40] = turned[104:128]
    lat = lat_index()
    none = jnp.zeros((2, 128), jnp.float32)
    t_end, s_end, v_end = turned[125:128], turned[117:120], turned[111:112]
    fold = [jnp.concatenate([turned[k : k + 1] for k in (n, n - 1, n - 2)]) for n in (127, 119)]
    fold = mirror16(jnp.concatenate(fold + [none], axis=0))
    north = jnp.concatenate([t_end, s_end, v_end, none[:1]], axis=0)
    south = jnp.concatenate([turned[0:3], turned[8:11], none], axis=0)
    fold_ref[...] = fold
    ahead = lax.rem(lat, 2) == 0
    core_swap[0:8] = jnp.where(ahead, north, south)
    core_swap[8:12] = jnp.where(ahead, turned[100:104], turned[16:20])
    core_swap[12:15] = fold[0:3]
    core_swap[15:16] = none[:1]
    ahead = lat == 1
    chip_swap[0:8] = jnp.where(ahead, north, south)
    chip_swap[8:12] = jnp.where(ahead, turned[100:104], turned[16:20])
    chip_swap[12:14] = none
    chip_swap[14:16] = none

    block = lax.shift_right_logical(jnp.broadcast_to(fc[0:1, 0:1], (8, 128)), 4)
    nz = lax.axis_size("z")
    columns = lax.axis_size("y") * lax.axis_size("xh")
    column = lax.axis_index("y") * lax.axis_size("xh") + lax.axis_index("xh")
    place = lax.axis_index("z")

    def column_of(x):
        count = jnp.zeros((8, 128), jnp.int32)
        for k in range(1, columns):
            count = count + jnp.where(x >= nz * k, 1, 0)
        return count

    total = block + (nz * column + place)
    total = jnp.where(total >= nz * columns, total - nz * columns, total)
    ahead = total - nz * column_of(total) - place
    ahead = jnp.where(ahead < 0, ahead + nz, ahead)
    origin = total - (nz * column + ahead)
    origin = jnp.where(origin < 0, origin + nz * columns, origin)
    source[0] = column_of(origin)
    source[1] = block - nz * column_of(block)


def edge_kernel(t, s, u, flag, depth, far, close):
    nl, ni, nj = t.shape
    ocean = flag[...] == 1
    wet = depth[...]
    even = lon_even()
    zero = jnp.zeros((2, nj), jnp.float32)
    for l in range(nl):
        m = jnp.where(ocean & (wet > l), 1.0, 0.0)
        tt, ss = t[l] * m, s[l] * m
        east_edge = jnp.concatenate(
            [tt[ni - 3 :], ss[ni - 3 :], u[l, ni - 1 :] * m[ni - 1 :], zero[:1]], axis=0
        )
        west_edge = jnp.concatenate([tt[:3], ss[:3], zero], axis=0)
        far[8 * l : 8 * l + 8] = jnp.where(even, west_edge, east_edge)
        close[8 * l : 8 * l + 8] = jnp.where(even, east_edge, west_edge)


def widen_kernel(
    chip_got, core_got, fold, fields, far_q, close_q, far, close, plane, rims, piece, tile
):
    _, ni, nj = fields.shape
    lat = lat_index()
    even = lon_even()
    odd = lax.rem(lat, 2) == 1
    north = jnp.where(lat < 3, jnp.where(odd, chip_got[...], core_got[...]), 0.0)
    south = jnp.where(lat > 0, jnp.where(odd, core_got[...], chip_got[...]), 0.0)
    piece[0:3] = jnp.where(lat == 3, fold[3:6], core_got[12:15])
    piece[3:8] = jnp.zeros((5, 128), jnp.float32)
    rims[0] = north[0:8]
    rims[1] = south[0:8]
    tile[...] = jnp.zeros((128, 128), jnp.float32)
    tile[0:4] = north[8:12]
    tile[124:128] = south[8:12]
    beyond = tile[...].T[0 : 4 * ni].reshape(4, ni, 128)
    part, em, nm, cpl = (jnp.concatenate([fields[k], beyond[k]], axis=1) for k in range(4))
    row = lax.broadcasted_iota(jnp.int32, part.shape, 0)
    side = part + pltpu.roll(nm, 1, 1) + jnp.where(row == 0, 0.0, pltpu.roll(em, 1, 0))
    for k, f in enumerate((side, cpl, em)):
        plane[k] = f
    up = jnp.concatenate([side[ni - 3 :], cpl[ni - 3 :], em[ni - 1 :], em[ni - 1 :]], axis=0)
    down = jnp.concatenate([side[0:3], cpl[0:3], cpl[0:2]], axis=0)
    far[0:64] = far_q[...]
    close[0:64] = close_q[...]
    for out, first, second in ((far, down, up), (close, up, down)):
        rows = jnp.where(even, first, second)
        for l in range(8):
            out[8 * l + 7 : 8 * l + 8] = rows[l : l + 1, 0:nj]
        out[64:72, 0:128] = rows[:, nj:]
        out[64:72, 128:384] = jnp.zeros((8, 256), jnp.float32)


def krylov_kernel(piece, plane, far, close, basis_ref, message, wide, west, east):
    ni, nj = basis_ref.shape[1:]
    even = lon_even()
    for out, first, second in ((west, far, close), (east, close, far)):
        for l in range(8):
            at = 8 * l + 7
            out[l : l + 1, 0:nj] = jnp.where(even, first[at : at + 1], second[at : at + 1])
        out[:, nj:] = jnp.where(even, first[64:72, 0:128], second[64:72, 0:128])
    blank = jnp.zeros((8, nj + 128), jnp.float32)
    for k in range(2):
        wide[k, 0:8] = blank
        wide[k, 24:32] = blank
        wide[k, 8:24] = plane[k]
        wide[k, 5:8] = west[3 * k : 3 * k + 3]
        wide[k, 24:27] = east[3 * k : 3 * k + 3]
    wide[0, 8:9] = plane[0, 0:1] + west[6:7]
    wide[0, 24:25] = east[0:1] + plane[2, ni - 1 : ni]
    b0 = wide[0]
    cpl = wide[1]
    rows, lanes = b0.shape

    def scaled(e):
        f = cpl * e
        lap = (
            4.0 * f
            - pltpu.roll(f, 1, 0)
            - pltpu.roll(f, rows - 1, 0)
            - pltpu.roll(f, 1, 1)
            - pltpu.roll(f, lanes - 1, 1)
        )
        return ((1.0 - SHIFT) * e + cpl * lap) * (1.0 / SCALE)

    b1 = scaled(b0)
    b2 = 2.0 * scaled(b1) - b0
    b3 = 2.0 * scaled(b2) - b1
    basis = [b[8 : 8 + ni, :nj] for b in (b0, b1, b2, b3)]
    for k in range(4):
        basis_ref[k] = basis[k]
    row = lax.broadcasted_iota(jnp.int32, (4, 128), 0)
    col = lax.broadcasted_iota(jnp.int32, (4, 128), 1)
    total = piece[0:4]
    for n, (i, j) in enumerate(PAIRS):
        prod = basis[i] * basis[j]
        prod = prod[:8] + prod[8:]
        acc = prod[:, :128]
        for k in range(1, nj // 128):
            acc = acc + prod[:, 128 * k : 128 * (k + 1)]
        one = jnp.sum(jnp.sum(acc, axis=0, keepdims=True), axis=1, keepdims=True)
        total = jnp.where((row == 3) & (col == n), one, total)
    for k in range(message.shape[0]):
        message[k] = total


def relay_kernel(source, got, message):
    peers = got.shape[0]
    total = got[0]
    for k in range(1, peers):
        total = total + got[k]
    which = source[0, 0:4]
    piece = got[1]
    for k in range(1, peers // 2):
        piece = jnp.where(which == k, got[2 * k + 1], piece)
    row = lax.broadcasted_iota(jnp.int32, (4, 128), 0)
    text = jnp.where(row < 3, piece, total)
    for k in range(message.shape[0]):
        message[k] = text


def finish_kernel(
    basis_ref, source, got, edges, tail, wet, base_t, base_s,
    surface_out, residual_out, out_t, out_s, surface, residual, tile, final, sems,
):
    del base_t, base_s
    total = got[0]
    for k in range(1, got.shape[0]):
        total = total + got[k]
    fold = [got[0], got[1]]
    which = source[1, 0:4]
    for k in range(1, got.shape[0] // 2):
        fold = [jnp.where(which == k, got[2 * k + i], fold[i]) for i in range(2)]
    last = jnp.where(lat_index() == 3, 1.0, 0.0)
    rows = [
        jnp.concatenate([edges[35:40], fold[0][0:3]], axis=0),
        jnp.concatenate([edges[27:32], fold[1][0:3]], axis=0),
    ]
    row = lax.broadcasted_iota(jnp.int32, (8, 128), 0)
    speed = jnp.where(row < 3, pltpu.roll(edges[16:24], 3, 0) * last, 0.0)
    pos = speed > 0.0
    nj = surface.shape[1]
    for k in range(2):
        q = [rows[k]] + [pltpu.roll(rows[k], 8 - o, 0) for o in range(1, 6)]
        face = speed * weno_upwind(*[jnp.where(pos, q[i], q[5 - i]) for i in range(5)])
        change = face - jnp.where(row == 0, 0.0, pltpu.roll(face, 1, 0))
        tile[k] = jnp.zeros((128, 128), jnp.float32)
        tile[k, 125:128] = change[0:3]
        final[k] = (tail[k] - tile[k].T.reshape(tail.shape[1:])) * wet[...]
    line = total[3:4]
    col = lax.broadcasted_iota(jnp.int32, (1, 128), 1)
    gram = {}
    for n, pair in enumerate(PAIRS):
        gram[pair] = jnp.sum(jnp.where(col == n, line, 0.0), axis=1, keepdims=True)
    xc, rc = coefficients(gram)
    basis = [basis_ref[k] for k in range(4)]
    surface[...] = sum(c * f for c, f in zip(xc, basis) if c is not None)
    residual[...] = sum(c * f for c, f in zip(rc, basis) if c is not None)
    copies = [
        pltpu.make_async_copy(final.at[0], out_t.at[:, :, nj - 128 : nj], sems.at[0]),
        pltpu.make_async_copy(final.at[1], out_s.at[:, :, nj - 128 : nj], sems.at[1]),
        pltpu.make_async_copy(surface, surface_out, sems.at[2]),
        pltpu.make_async_copy(residual, residual_out, sems.at[3]),
    ]
    for copy in copies:
        copy.start()
    for copy in copies:
        copy.wait()


def near(value):
    return pltpu.with_memory_space_constraint(value, pltpu.VMEM)


def f32(*shape):
    return jax.ShapeDtypeStruct(shape, jnp.float32)


def vmem(*shape):
    return pltpu.VMEM(shape, jnp.float32)


def make_on_device(sizes):
    ny, nxh, nz, nxl, ncore = sizes
    n_lon, n_lat = ny * nxh * nz, nxl * ncore

    def on_device(t, s, u, v, elev, flag, depth, fc):
        nl, ni, nj = t.shape
        lat = lax.axis_index(LAT)
        last = lat == n_lat - 1
        hbm, local = pl.BlockSpec(memory_space=pl.ANY), pl.BlockSpec(memory_space=pltpu.VMEM)

        fields, edges, source, fold, chip_swap, core_swap = pl.pallas_call(
            pack_kernel,
            out_shape=(
                vmem(4, ni, nj),
                vmem(40, 128),
                pltpu.VMEM((2, 8, 128), jnp.int32),
                vmem(8, 128),
                vmem(16, 128),
                vmem(16, 128),
            ),
            scratch_shapes=[vmem(128, 128)],
            name="pack",
        )(t, s, u, v, elev, flag, depth, fc.reshape(1, ni))
        far, close = pl.pallas_call(
            edge_kernel, out_shape=(vmem(64, nj), vmem(64, nj)), name="edge"
        )(near(t), near(s), near(u), near(flag), near(depth))
        chip_got = lax.ppermute(chip_swap, LAT, [(1, 2), (2, 1)])
        core_got = lax.ppermute(core_swap, LAT, [(0, 1), (1, 0), (2, 3), (3, 2)])
        far, close, plane, rims, piece = pl.pallas_call(
            widen_kernel,
            out_shape=(
                vmem(72, nj),
                vmem(72, nj),
                vmem(3, ni, nj + 128),
                vmem(2, 8, 128),
                vmem(8, 128),
            ),
            scratch_shapes=[vmem(128, 128)],
            name="widen",
        )(near(chip_got), near(core_got), near(fold), near(fields), near(far), near(close))

        def swaps(first):
            pairs = []
            for i in range(first, n_lon, 2):
                pairs += [(i, (i + 1) % n_lon), ((i + 1) % n_lon, i)]
            return pairs

        close = lax.ppermute(close, LON, swaps(0))
        far = lax.ppermute(far, LON, swaps(1))
        basis, message = pl.pallas_call(
            krylov_kernel,
            out_shape=(vmem(4, ni, nj), vmem(ny * nxh * nxl, 4, 128)),
            scratch_shapes=[vmem(2, 32, nj + 128), vmem(8, nj + 128), vmem(8, nj + 128)],
            name="krylov",
        )(near(piece), near(plane), near(far), near(close))
        got = lax.all_to_all(message, ("y", "xh", "xl"), 0, 0)
        message = pl.pallas_call(
            relay_kernel, out_shape=vmem(nz * ncore, 4, 128), name="relay"
        )(near(source), near(got))
        got = lax.all_to_all(message, ("z", "core"), 0, 0)
        level = lax.broadcasted_iota(jnp.int32, t.shape, 0)
        mask = jnp.where((flag[None] == 1) & (level < depth[None]), 1.0, 0.0).astype(jnp.float32)
        q = jnp.stack([t * mask, s * mask])
        ue = u * mask
        vn = v * mask

        def sides(msg):
            tiles = msg[: 8 * nl].reshape(nl, 8, nj)
            return jnp.stack([tiles[:, 0:3], tiles[:, 3:6]]), tiles[:, 6:7]

        even = lon_even()
        west = jnp.where(even, far, close)
        east = jnp.where(even, close, far)
        q_west, u_west = sides(west)
        q_east, _ = sides(east)
        north, south = rims[0], rims[1]

        def columns(msg):
            return jnp.transpose(msg[:6].reshape(2, 3, nl, ni), (0, 2, 3, 1))

        q_north, q_south = columns(north), columns(south)
        v_south = south[6].reshape(nl, ni, 1)
        zonal = jnp.concatenate([q_west, q, q_east], axis=2)
        merid = jnp.concatenate([q_south, q, q_north], axis=3)
        speed_x = jnp.concatenate([u_west, ue], axis=1)
        place = lax.broadcasted_iota(jnp.int32, (1, 1, nj + 1), 2)
        speed_y = jnp.concatenate([v_south, vn], axis=2)
        speed_y = jnp.where(last & (place > nj - 3), 0.0, speed_y)
        flux_x = face_flux(zonal, speed_x[None], ni + 1, 2)
        flux_y = face_flux(merid, speed_y[None], nj + 1, 3)
        updated = q - (flux_x[:, :, 1:] - flux_x[:, :, :-1]) - (flux_y[..., 1:] - flux_y[..., :-1])
        updated = updated * mask
        surface, residual, t_next, s_next = pl.pallas_call(
            finish_kernel,
            in_specs=[local] * 6 + [hbm] * 2,
            out_specs=(hbm,) * 4,
            out_shape=(f32(ni, nj), f32(ni, nj), f32(nl, ni, nj), f32(nl, ni, nj)),
            input_output_aliases={6: 2, 7: 3},
            scratch_shapes=[
                vmem(ni, nj),
                vmem(ni, nj),
                vmem(2, 128, 128),
                vmem(2, nl, ni, 128),
                pltpu.SemaphoreType.DMA((4,)),
            ],
            name="finish",
        )(
            near(basis),
            near(source),
            near(got),
            near(edges),
            near(updated[..., nj - 128 :]),
            near(mask[..., nj - 128 :]),
            updated[0],
            updated[1],
        )
        return t_next, s_next, surface, residual

    return on_device


def solution(mesh, sizes=SIZES):
    fine = Mesh(mesh.devices.reshape(sizes), ALL)
    block, plane = P(None, LON, LAT), P(LON, LAT)
    return jax.shard_map(
        make_on_device(sizes),
        mesh=fine,
        in_specs=(block,) * 4 + (plane,) * 3 + (P(LON),),
        out_specs=(block, block, plane, plane),
        check_vma=False,
    )
```
